32 devices in a mesh: dp: 16 (over z, x, core), tensor: 2 (over y).
Axes of the slice: x: 2, y: 2, z: 4, core: 2. Of those that a mesh axis runs over, the one named last changes fastest.
Arguments:
- inputs: bfloat16 [32768, 768], P(('dp', 'tensor')), may hold values from -6 to 6
- lengths: int32 [32], P('dp'), may hold values from 100 to 1024, as said below
- norm1_gain: float32 [768], replicated, may hold values from 0.1 to 1.9
- norm1_shift: float32 [768], replicated, may hold values from -3 to 3
- query_weight: bfloat16 [768, 768], P(None, 'tensor'), may hold values from -0.21875 to 0.21875
- query_bias: float32 [768], P('tensor'), may hold values from -3 to 3
- key_weight: bfloat16 [768, 768], P(None, 'tensor'), may hold values from -0.21875 to 0.21875
- key_bias: float32 [768], P('tensor'), may hold values from -3 to 3
- value_weight: bfloat16 [768, 768], P(None, 'tensor'), may hold values from -0.21875 to 0.21875
- value_bias: float32 [768], P('tensor'), may hold values from -3 to 3
- out_weight: bfloat16 [768, 768], P('tensor'), may hold values from -0.875 to 0.875
- out_bias: float32 [768], replicated, may hold values from -3 to 3
- norm2_gain: float32 [768], replicated, may hold values from 0.1 to 1.9
- norm2_shift: float32 [768], replicated, may hold values from -3 to 3
- up_weight: bfloat16 [768, 3072], P(None, 'tensor'), may hold values from -0.21875 to 0.21875
- up_bias: float32 [3072], P('tensor'), may hold values from -3 to 3
- down_weight: bfloat16 [3072, 768], P('tensor'), may hold values from -0.109375 to 0.109375
- down_bias: float32 [768], replicated, may hold values from -3 to 3
- out_grad: bfloat16 [32768, 768], P(('dp', 'tensor')), may hold values from -6 to 6
Outputs:
- layer_out: bfloat16 [32768, 768], P(('dp', 'tensor'))
- input_grad: bfloat16 [32768, 768], P(('dp', 'tensor'))
- grad_norm1_gain: float32 [768], replicated
- grad_norm1_shift: float32 [768], replicated
- grad_query_weight: float32 [768, 768], P(None, 'tensor')
- grad_query_bias: float32 [768], P('tensor')
- grad_key_weight: float32 [768, 768], P(None, 'tensor')
- grad_key_bias: float32 [768], P('tensor')
- grad_value_weight: float32 [768, 768], P(None, 'tensor')
- grad_value_bias: float32 [768], P('tensor')
- grad_out_weight: float32 [768, 768], P('tensor')
- grad_out_bias: float32 [768], replicated
- grad_norm2_gain: float32 [768], replicated
- grad_norm2_shift: float32 [768], replicated
- grad_up_weight: float32 [768, 3072], P(None, 'tensor')
- grad_up_bias: float32 [3072], P('tensor')
- grad_down_weight: float32 [3072, 768], P('tensor')
- grad_down_bias: float32 [768], replicated
The draws below stay inside these ranges and needn't reach their ends.
Inputs may be any that keep to these rules, and one draw needn't show every extreme that they name: `lengths`: valid tokens of each sequence; in every draw some sequence has exactly 1024.
All inputs are finite; a program needn't handle non-finite values.
Results may differ from the reference program's by a relative error of at most 0.034.
Values may be sent and summed in bfloat16 or wider, within the bound.
No kernel may reach another device: no remote copies, remote signals or barrier semaphores. Data moves between devices by JAX's collectives and lax.ppermute only.
A program may use at most 256 MiB of HBM per device.

```python
import jax
import jax.numpy as jnp
from jax import lax

D = 768
HEADS = 12
HEAD_DIM = 64
FF = 3072
LEN = 1024
MIN_LEN = 100
SEQS = 32
TOKENS = 32768


def draw_lengths(key, part):
    key = jax.random.fold_in(key, 11)
    first_key, second_key, third_key, chosen_key = jax.random.split(key, 4)
    span_count = LEN - MIN_LEN + 1
    first_draw = jax.random.randint(first_key, (SEQS,), 0, span_count)
    second_draw = jax.random.randint(second_key, (SEQS,), 0, span_count)
    third_draw = jax.random.randint(third_key, (SEQS,), 0, span_count)
    extra = jnp.minimum(first_draw, jnp.maximum(second_draw, third_draw))
    chosen = jax.random.randint(chosen_key, (), 0, SEQS)
    base_lengths = MIN_LEN + extra
    return jnp.where(jnp.arange(SEQS) == chosen, LEN, base_lengths).astype(jnp.int32)


def block_scale(own_key, extent, pieces, smallest, top_value):
    loudness = 1.0
    for axis_at, shards_of in pieces:
        draws = jax.random.uniform(jax.random.fold_in(jax.random.fold_in(own_key, 6), axis_at), (shards_of,), jnp.float32, smallest / len(pieces), top_value / len(pieces))
        loudness = loudness * jnp.repeat(jnp.exp(draws), extent[axis_at] // shards_of).reshape((-1,) + (1,) * (len(extent) - 1 - axis_at))
    return loudness


def noise(key, shape, scale, most, cuts=(), kind=jnp.bfloat16):
    values = jax.random.normal(key, shape, jnp.float32) * scale
    if len(cuts) > 0:
        values = block_scale(key, shape, cuts, -0.22, 0.18) * values
    return jnp.clip(values, min=-most, max=most).astype(kind)


def setup_inputs(seed: int = 0) -> dict:
    splits = jax.random.split(jax.random.key(seed), 20)
    return {
        "inputs": noise(splits[0], (TOKENS, D), 1.0, 6.0, ((0, 32),)),
        "lengths": draw_lengths(jax.random.fold_in(splits[19], 71), 0),
        "norm1_gain": jnp.clip(1.0 + 0.18 * jax.random.normal(splits[2], (D,), jnp.float32), 0.1, 1.9),
        "norm1_shift": noise(splits[3], (D,), 0.3, 3.0, (), jnp.float32),
        "query_weight": noise(splits[4], (D, D), D ** -0.5, 0.21875, ((1, 2),)),
        "query_bias": noise(splits[5], (D,), 0.3, 3.0, ((0, 2),), jnp.float32),
        "key_weight": noise(splits[6], (D, D), D ** -0.5, 0.21875, ((1, 2),)),
        "key_bias": noise(splits[7], (D,), 0.3, 3.0, ((0, 2),), jnp.float32),
        "value_weight": noise(splits[8], (D, D), D ** -0.5, 0.21875, ((1, 2),)),
        "value_bias": noise(splits[9], (D,), 0.3, 3.0, ((0, 2),), jnp.float32),
        "out_weight": noise(splits[10], (D, D), (D // 16) ** -0.5, 0.875, ((0, 2),)),
        "out_bias": noise(splits[11], (D,), 0.3, 3.0, (), jnp.float32),
        "norm2_gain": jnp.clip(1.0 + 0.18 * jax.random.normal(splits[12], (D,), jnp.float32), 0.1, 1.9),
        "norm2_shift": noise(splits[13], (D,), 0.3, 3.0, (), jnp.float32),
        "up_weight": noise(splits[14], (D, FF), D ** -0.5, 0.21875, ((1, 2),)),
        "up_bias": noise(splits[15], (FF,), 0.3, 3.0, ((0, 2),), jnp.float32),
        "down_weight": noise(splits[16], (FF, D), FF ** -0.5, 0.109375, ((0, 2),)),
        "down_bias": noise(splits[17], (D,), 0.3, 3.0, (), jnp.float32),
        "out_grad": noise(splits[18], (TOKENS, D), 1.0, 6.0, ((0, 32),)),
    }


@jax.custom_vjp
def low(v):
    return lax.optimization_barrier(v.astype(jnp.bfloat16)).astype(jnp.float32)

@jax.custom_vjp
def low_back(v):
    return v

def low_keep(v):
    return (low(v), None)

def low_pass(kept, grad):
    return (grad,)

def back_keep(v):
    return (v, None)

def back_low(kept, grad):
    return (low(grad),)
low.defvjp(low_keep, low_pass)
low_back.defvjp(back_keep, back_low)
highest = lax.Precision.HIGHEST
epsilon = 1e-05

def layer_norm(values, gain_vec, shift_vec):
    average = lax.optimization_barrier(jnp.mean(values, axis=-1, keepdims=True))
    centered = values - average
    spread = lax.optimization_barrier(jnp.mean(centered * centered, axis=-1, keepdims=True))
    return centered * lax.rsqrt(spread + epsilon) * gain_vec + shift_vec

def rotary_tables(length_rows, head_size):
    halfway = head_size // 2
    places = jnp.arange(length_rows, dtype=jnp.float32)[:, None, None]
    frequencies = 10000.0 ** (-2.0 * jnp.arange(halfway, dtype=jnp.float32) / head_size)
    angles = places * frequencies
    return (jnp.cos(angles), jnp.sin(angles))

def rotate(tensor, cosine_table, sine_table):
    halfway = tensor.shape[-1] // 2
    leading = tensor[..., :halfway]
    trailing = tensor[..., halfway:]
    return jnp.concatenate([leading * cosine_table - trailing * sine_table, trailing * cosine_table + leading * sine_table], axis=-1)

def forward(params, values, length):
    norm1_gain, norm1_shift, query_weight, query_bias, key_weight, key_bias, value_weight, value_bias, out_weight, out_bias, norm2_gain, norm2_shift, up_weight, up_bias, down_weight, down_bias = params
    seq_rows = values.shape[0]
    normed = low(layer_norm(values, norm1_gain, norm1_shift))
    cosine_table, sine_table = rotary_tables(seq_rows, HEAD_DIM)
    query_pre = low_back(jnp.dot(normed, query_weight, precision=highest) + query_bias)
    key_pre = low_back(jnp.dot(normed, key_weight, precision=highest) + key_bias)
    value_pre = low_back(jnp.dot(normed, value_weight, precision=highest) + value_bias)
    queries = low(rotate(query_pre.reshape(seq_rows, HEADS, HEAD_DIM), cosine_table, sine_table) * HEAD_DIM ** (-0.5))
    keys = low(rotate(key_pre.reshape(seq_rows, HEADS, HEAD_DIM), cosine_table, sine_table))
    values_h = low(value_pre).reshape(seq_rows, HEADS, HEAD_DIM)
    valid_rows = (jnp.arange(seq_rows) < length).astype(jnp.float32)
    masking = (valid_rows - 1.0) * 1e+30
    scores = low_back(jnp.einsum('qhd,khd->hqk', queries, keys, precision=highest) + masking[None, None, :])
    attn_probs = low(jax.nn.softmax(scores, axis=-1))
    context = jnp.einsum('hqk,khd->qhd', attn_probs, values_h, precision=highest) * valid_rows[:, None, None]
    context = low(low_back(context.reshape(seq_rows, D)))
    attended = low_back(jnp.dot(context, out_weight, precision=highest))
    middle = values + attended + out_bias
    normed2 = low(layer_norm(middle, norm2_gain, norm2_shift))
    hidden = low_back(jnp.dot(normed2, up_weight, precision=highest) + up_bias)
    activated = low(jax.nn.gelu(hidden, approximate=False))
    return middle + jnp.dot(activated, down_weight, precision=highest) + down_bias

def reference(inputs, lengths, norm1_gain, norm1_shift, query_weight, query_bias, key_weight, key_bias, value_weight, value_bias, out_weight, out_bias, norm2_gain, norm2_shift, up_weight, up_bias, down_weight, down_bias, out_grad):
    params = tuple((member.astype(jnp.float32) for member in (norm1_gain, norm1_shift, query_weight, query_bias, key_weight, key_bias, value_weight, value_bias, out_weight, out_bias, norm2_gain, norm2_shift, up_weight, up_bias, down_weight, down_bias)))
    sequences = inputs.astype(jnp.float32).reshape(SEQS, LEN, D)
    cotangents = out_grad.astype(jnp.float32).reshape(SEQS, LEN, D)

    def per_sequence(running, bundle):
        seq_values, seq_cotangent, seq_length = bundle
        result, pull_back = jax.vjp(lambda weight_set, activation: forward(weight_set, activation, seq_length), params, seq_values)
        param_grads, grad_values = pull_back(seq_cotangent)
        running = jax.tree.map(lambda before, addend: before + addend, running, param_grads)
        return (running, (result.astype(jnp.bfloat16), grad_values.astype(jnp.bfloat16)))
    initial = jax.tree.map(jnp.zeros_like, params)
    summed, (outputs, input_grads) = lax.scan(per_sequence, initial, (sequences, cotangents, lengths))
    return (outputs.reshape(TOKENS, D), input_grads.reshape(TOKENS, D), summed[0], summed[1], summed[2], summed[3], summed[4], summed[5], summed[6], summed[7], summed[8], summed[9], summed[10], summed[11], summed[12], summed[13], summed[14], summed[15])
```

```python
import math

import jax
import jax.numpy as jnp
import numpy as np
from jax import lax
from jax.experimental import pallas as pl
from jax.experimental.pallas import tpu as pltpu
from jax.sharding import PartitionSpec as P

HEAD_DIM = 64
EPS = 1e-05
LOG2E = math.log2(math.e)
LN2 = math.log(2.0)
F32 = jnp.float32
BF = jnp.bfloat16
VMEM_LIMIT = 56 << 20
BIG = -1e30


def dot(a, b, ca=1, cb=0):
    return lax.dot_general(a, b, (((ca,), (cb,)), ((), ())), preferred_element_type=F32)


def params():
    return pltpu.CompilerParams(vmem_limit_bytes=VMEM_LIMIT)


def cost(macs, nbytes, exps=0):
    return pl.CostEstimate(flops=int(2 * macs), bytes_accessed=int(nbytes), transcendentals=int(exps))


def struct(shape, dtype):
    return jax.ShapeDtypeStruct(shape, dtype)


def whole(shape):
    return pl.BlockSpec(shape, lambda *_: (0,) * len(shape), pipeline_mode=pl.Buffered(1))


def whole_out(shape):
    return pl.BlockSpec(shape, lambda *_: (0,) * len(shape))


def norm_rows(v):
    mean = jnp.mean(v, axis=1, keepdims=True)
    cent = v - mean
    var = jnp.mean(cent * cent, axis=1, keepdims=True)
    r = lax.rsqrt(var + EPS)
    return cent * r, r


def norm_back(e, n, r):
    return r * (e - jnp.mean(e, axis=1, keepdims=True) - n * jnp.mean(e * n, axis=1, keepdims=True))


def rotary_tables(rows):
    half = HEAD_DIM // 2
    freq = (10000.0 ** (-2.0 * np.arange(half, dtype=np.float32) / HEAD_DIM)).astype(np.float32)
    ang = (np.arange(rows, dtype=np.float32)[:, None] * freq[None, :]).astype(np.float64)
    cos = np.cos(ang).astype(np.float32)
    sin = np.sin(ang).astype(np.float32)
    return np.concatenate([cos] * 4, 1), np.concatenate([-sin, sin] * 2, 1)


def swap_halves(v):
    lane = lax.broadcasted_iota(jnp.int32, v.shape, 1)
    return jnp.where((lane & 32) == 0, pltpu.roll(v, 96, 1), pltpu.roll(v, 32, 1))


def rotate(v, cos, sin):
    return v * cos + swap_halves(v) * sin


def rotate_back(v, cos, sin):
    return v * cos - swap_halves(v) * sin


def put_qkv(pre, cos, sin, q_ref, k_ref, v_ref):
    width = q_ref.shape[1]
    for i in range(width // 128):
        sl = slice(i * 128, (i + 1) * 128)
        q_ref[:, sl] = (rotate(pre[0][:, sl], cos, sin) * (LOG2E / 8.0)).astype(BF)
        k_ref[:, sl] = rotate(pre[1][:, sl], cos, sin).astype(BF)
        v_ref[:, sl] = pre[2][:, sl].astype(BF)


def project_own_kernel(
    x_ref, gain_ref, shift_ref, wq_ref, wk_ref, wv_ref, b_ref, cos_ref, sin_ref,
    n_ref, nt_ref, q_ref, k_ref, v_ref,
):
    width = q_ref.shape[1]
    n, _ = norm_rows(x_ref[...].astype(F32))
    low = (n * gain_ref[...] + shift_ref[...]).astype(BF)
    n_ref[...] = low
    nt_ref[...] = low.T
    pre = [
        dot(low, w[...]) + b_ref[:, i * width : (i + 1) * width]
        for i, w in enumerate((wq_ref, wk_ref, wv_ref))
    ]
    put_qkv(pre, cos_ref[...], sin_ref[...], q_ref, k_ref, v_ref)


def project_other_kernel(n_ref, w_ref, b_ref, cos_ref, sin_ref, q_ref, k_ref, v_ref):
    width = q_ref.shape[1]
    low = n_ref[...]
    pre = [
        dot(low, w_ref[:, i * width : (i + 1) * width]) + b_ref[:, i * width : (i + 1) * width]
        for i in range(3)
    ]
    put_qkv(pre, cos_ref[...], sin_ref[...], q_ref, k_ref, v_ref)


def project_own(x, gain, shift, wq, wk, wv, bias, cos, sin):
    rows, d = x.shape
    width = wq.shape[1]
    blk = 256
    row = lambda w: pl.BlockSpec((blk, w), lambda i: (i, 0))
    return pl.pallas_call(
        project_own_kernel,
        grid=(rows // blk,),
        in_specs=[row(d), whole((1, d)), whole((1, d))]
        + [whole((d, width))] * 3
        + [whole((1, 3 * width)), row(128), row(128)],
        out_specs=[row(d), pl.BlockSpec((d, blk), lambda i: (0, i))] + [row(width)] * 3,
        out_shape=[struct((rows, d), BF), struct((d, rows), BF)] + [struct((rows, width), BF)] * 3,
        compiler_params=params(),
        cost_estimate=cost(rows * d * width * 3, 12e6),
        name="project_own",
    )(x, gain, shift, wq, wk, wv, bias, cos, sin)


def project_other(n, w, bias, cos, sin):
    rows, d = n.shape
    width = w.shape[1] // 3
    blk = 256
    row = lambda w_: pl.BlockSpec((blk, w_), lambda i: (i, 0))
    return pl.pallas_call(
        project_other_kernel,
        grid=(rows // blk,),
        in_specs=[row(d), whole((d, 3 * width)), whole((1, 3 * width)), row(128), row(128)],
        out_specs=[row(width)] * 3,
        out_shape=[struct((rows, width), BF)] * 3,
        compiler_params=params(),
        cost_estimate=cost(rows * d * width * 3, 8e6),
        name="project_other",
    )(n, w, bias, cos, sin)


def split3(v):
    hi = v.astype(BF)
    rest = v - hi.astype(F32)
    mid = rest.astype(BF)
    lo = rest - mid.astype(F32)
    return hi.astype(F32), mid.astype(F32), lo


def spread(lane, first, one, two):
    out = jnp.where(lane == 0, first, 0.0)
    for at, part in enumerate((*split3(one), *split3(two))):
        out = jnp.where(lane == at + 1, part, out)
    return out.astype(BF)


def attend_kernel(bq, len_ref, q_ref, k_ref, v_ref, ctx_ref, aug_ref):
    rows = q_ref.shape[0]
    length = len_ref[0]
    lane1 = lax.broadcasted_iota(jnp.int32, (1, 128), 1)
    krow = lax.broadcasted_iota(jnp.int32, (rows, 128), 0)
    klane = lax.broadcasted_iota(jnp.int32, (rows, 128), 1)
    lane = lax.broadcasted_iota(jnp.int32, (bq, 128), 1)
    qrow = lax.broadcasted_iota(jnp.int32, (bq, 128), 0)
    kaug = jnp.where((klane == 0) & (krow >= length), BIG, 0.0).astype(BF)
    k = jnp.concatenate([k_ref[...], kaug], 1)
    v = jnp.concatenate([v_ref[...], jnp.ones((rows, 128), BF)], 1)
    qaug = jnp.where(lane == 0, 1.0, 0.0).astype(BF)
    for i in range(rows // bq):
        sl = slice(i * bq, (i + 1) * bq)
        q = q_ref[sl, :]
        outs, totals = [], []
        for h in range(2):
            keep = ((lane1 < 64) if h == 0 else (lane1 >= 64)).astype(BF)
            s = dot(jnp.concatenate([q * keep, qaug], 1), k, 1, 1)
            top = jnp.max(s, axis=1, keepdims=True)
            p = jnp.exp2(s - top).astype(BF)
            o = dot(p, v)
            total = o[:, 128:]
            outs.append(o[:, :128] / total)
            totals.append(top + jnp.log2(total))
        ctx = jnp.where(lane < 64, outs[0], outs[1])
        ctx_ref[sl, :] = jnp.where(qrow + i * bq < length, ctx, 0.0).astype(BF)
        aug_ref[sl, :] = spread(lane, 1.0, totals[0], totals[1])


def attend(length, q, k, v):
    rows, width = q.shape
    bs = pl.BlockSpec((rows, 128), lambda j, *_: (0, j))
    heads = width // HEAD_DIM
    return pl.pallas_call(
        lambda *refs: attend_kernel(256, *refs),
        grid_spec=pltpu.PrefetchScalarGridSpec(
            num_scalar_prefetch=1, grid=(width // 128,), in_specs=[bs] * 3, out_specs=[bs] * 2
        ),
        out_shape=[struct((rows, width), BF)] * 2,
        compiler_params=params(),
        cost_estimate=cost(heads * rows * rows * 256 * 2, rows * width * 10, heads * rows * rows),
        name="attend",
    )(length, q, k, v)


def attend_back_kernel(
    bq, len_ref, q_ref, k_ref, v_ref, g_ref, ctx_ref, aug_ref, cos_ref, sin_ref,
    dq_ref, dk_ref, dv_ref, sum_ref, dqt,
):
    rows = q_ref.shape[0]
    length = len_ref[0]
    lane1 = lax.broadcasted_iota(jnp.int32, (1, 128), 1)
    krow = lax.broadcasted_iota(jnp.int32, (rows, 128), 0)
    klane = lax.broadcasted_iota(jnp.int32, (rows, 128), 1)
    lane = lax.broadcasted_iota(jnp.int32, (bq, 128), 1)
    k = k_ref[...]
    v = v_ref[...]
    kt = k.T
    dks, dvs = [], []
    for h in range(2):
        keep = ((lane1 < 64) if h == 0 else (lane1 >= 64)).astype(BF)
        first = 1 + 3 * h
        mine = jnp.where((klane >= first) & (klane < first + 3), -1.0, 0.0)
        kaug = jnp.where((klane == 0) & (krow >= length), BIG, mine).astype(BF)
        kh = jnp.concatenate([k * keep, kaug], 1)
        vh = jnp.concatenate([v * keep, mine.astype(BF)], 1)
        dk = jnp.zeros((rows, 128), F32)
        dv = jnp.zeros((rows, 128), F32)
        for i in range(rows // bq):
            sl = slice(i * bq, (i + 1) * bq)
            q = q_ref[sl, :]
            g = g_ref[sl, :]
            prod = g.astype(F32) * ctx_ref[sl, :].astype(F32)
            d0 = jnp.sum(jnp.where(lane < 64, prod, 0.0), 1, keepdims=True)
            d1 = jnp.sum(jnp.where(lane < 64, 0.0, prod), 1, keepdims=True)
            gaug = spread(lane, 0.0, d0, d1)
            st = dot(kh, jnp.concatenate([q, aug_ref[sl, :]], 1), 1, 1)
            pt = jnp.exp2(st)
            dpt = dot(vh, jnp.concatenate([g, gaug], 1), 1, 1)
            ds = (pt * dpt).astype(BF)
            dv = dv + dot(pt.astype(BF), g)
            dk = dk + dot(ds, q)
            dqt[h * 64 : (h + 1) * 64, sl] = dot(kt[h * 64 : (h + 1) * 64, :], ds)
        dks.append(dk)
        dvs.append(dv)
    cos = cos_ref[...]
    sin = sin_ref[...]
    dq = rotate_back(dqt[...].T * (1.0 / 8.0), cos, sin).astype(BF)
    dk = rotate_back(jnp.where(klane < 64, dks[0], dks[1]) * LN2, cos, sin).astype(BF)
    dv = jnp.where(klane < 64, dvs[0], dvs[1]).astype(BF)
    for at, (ref, val) in enumerate(((dq_ref, dq), (dk_ref, dk), (dv_ref, dv))):
        ref[...] = val
        sum_ref[at : at + 1, :] = jnp.sum(val.astype(F32), axis=0, keepdims=True)
    sum_ref[3:, :] = jnp.zeros((5, 128), F32)


def attend_back(length, q, k, v, g, ctx, aug, cos, sin):
    rows, width = q.shape
    bs = pl.BlockSpec((rows, 128), lambda j, *_: (0, j))
    heads = width // HEAD_DIM
    return pl.pallas_call(
        lambda *refs: attend_back_kernel(256, *refs),
        grid_spec=pltpu.PrefetchScalarGridSpec(
            num_scalar_prefetch=1,
            grid=(width // 128,),
            in_specs=[bs] * 6 + [whole((rows, 128))] * 2,
            out_specs=[bs] * 3 + [pl.BlockSpec((8, 128), lambda j, *_: (0, j))],
            scratch_shapes=[pltpu.VMEM((128, rows), F32)],
        ),
        out_shape=[struct((rows, width), BF)] * 3 + [struct((8, width), F32)],
        compiler_params=params(),
        cost_estimate=cost(heads * rows * rows * 256 * 5, rows * width * 18, heads * rows * rows),
        name="attend_back",
    )(length, q, k, v, g, ctx, aug, cos, sin)


def gelu_pair(h):
    z = jnp.abs(h) * (0.3275911 / math.sqrt(2.0)) + 1.0
    t = pl.reciprocal(z, approx=True)
    t = t * (2.0 - z * t)
    e = jnp.exp2(h * h * (-0.5 * LOG2E))
    poly = 0.5 * 1.061405429 * t - 0.5 * 1.453152027
    poly = poly * t + 0.5 * 1.421413741
    poly = poly * t - 0.5 * 0.284496736
    poly = poly * t + 0.5 * 0.254829592
    w = poly * t * e
    cdf = jnp.where(h >= 0.0, 1.0 - w, w)
    return h * cdf, cdf + h * e * (1.0 / math.sqrt(2.0 * math.pi))


def ffn_tile(n2, n2t, og, wu_ref, wd_ref, b_ref, out_acc, dn_acc, act_s, dh_s, first):
    rows = og.shape[0]
    blk = 256
    wu = wu_ref[...]
    wd = wd_ref[...]
    bias = b_ref[...]
    dbias = jnp.zeros((1, wu.shape[1]), F32)
    for i in range(rows // blk):
        sl = slice(i * blk, (i + 1) * blk)
        h = dot(n2[sl, :], wu) + bias
        act, slope = gelu_pair(h)
        act = act.astype(BF)
        dh = (slope * dot(og[sl, :], wd, 1, 1)).astype(BF)
        act_s[sl, :] = act
        dh_s[sl, :] = dh
        dbias = dbias + jnp.sum(dh.astype(F32), axis=0, keepdims=True)
        out_acc[sl, :] += dot(act, wd)
        dn_acc[sl, :] += dot(dh, wu, 1, 1)
    return dot(act_s[...], og[...], 0, 0), dot(n2t[...], dh_s[...]), dbias


def ffn_own_kernel(
    per, c_ref, x_ref, co_ref, cx_ref, woo_ref, wox_ref, ob_ref, gain_ref, shift_ref, og_ref, wu_ref, wd_ref, b_ref,
    mid_ref, n2_ref, n2t_ref, out_ref, dn_ref, ddo_ref, dup_ref, ddk_ref, dupk_ref, db_ref, act_s, dh_s,
):
    j = pl.program_id(0)
    rows = x_ref.shape[0]

    @pl.when(j == 0)
    def _():
        @pl.loop(0, rows // 256)
        def _(i):
            sl = pl.ds(pl.multiple_of(i * 256, 256), 256)
            att = dot(co_ref[sl, :], woo_ref[...]) + dot(cx_ref[sl, :], wox_ref[...])
            mid = x_ref[sl, :].astype(F32) + att + ob_ref[...]
            mid_ref[sl, :] = mid
            n, _ = norm_rows(mid)
            low = (n * gain_ref[...] + shift_ref[...]).astype(BF)
            n2_ref[sl, :] = low
            n2t_ref[:, sl] = low.T
            out_ref[sl, :] = jnp.zeros_like(mid)
            dn_ref[sl, :] = jnp.zeros_like(mid)

    dwd, dwu, db = ffn_tile(
        n2_ref, n2t_ref, og_ref, wu_ref, wd_ref, b_ref, out_ref, dn_ref, act_s, dh_s, False
    )
    db_ref[...] = db

    @pl.when(j < per)
    def _():
        ddo_ref[...] = dwd.astype(BF)
        dup_ref[...] = dwu.astype(BF)

    @pl.when(j >= per)
    def _():
        ddk_ref[...] = dwd.astype(BF)
        dupk_ref[...] = dwu.astype(BF)


TILE = 256


def send_keep_specs(per, d):
    send = lambda j: jnp.minimum(j, per - 1)
    keep = lambda j: jnp.maximum(j - per, 0)
    return [
        pl.BlockSpec((TILE, d), lambda j, *_: (send(j), 0)),
        pl.BlockSpec((d, TILE), lambda j, *_: (0, send(j))),
        pl.BlockSpec((TILE, d), lambda j, *_: (keep(j), 0)),
        pl.BlockSpec((d, TILE), lambda j, *_: (0, keep(j))),
    ]


def ffn_own(core, x, ctx_own, ctx_other, wo_own, wo_other, ob, gain, shift, og, wu, wd, bias):
    rows, d = x.shape
    ff = wu.shape[1]
    tiles = ff // TILE
    per = tiles // 2
    half = ctx_own.shape[1]
    tile = lambda j, c: jnp.where(j < per, (1 - c[0]) * per + j, c[0] * per + j - per)
    return pl.pallas_call(
        lambda *refs: ffn_own_kernel(per, *refs),
        grid_spec=pltpu.PrefetchScalarGridSpec(
            num_scalar_prefetch=1,
            grid=(tiles,),
            in_specs=[
                whole((rows, d)), whole((rows, half)), whole((rows, half)), whole((half, d)), whole((half, d)),
                whole((1, d)), whole((1, d)), whole((1, d)), whole((rows, d)),
                pl.BlockSpec((d, TILE), lambda j, c: (0, tile(j, c))),
                pl.BlockSpec((TILE, d), lambda j, c: (tile(j, c), 0)),
                pl.BlockSpec((1, TILE), lambda j, c: (0, tile(j, c))),
            ],
            out_specs=[whole_out((rows, d)), whole_out((rows, d)), whole_out((d, rows)), whole_out((rows, d)), whole_out((rows, d))]
            + send_keep_specs(per, d)
            + [pl.BlockSpec((1, TILE), lambda j, c: (0, tile(j, c)))],
            scratch_shapes=[pltpu.VMEM((rows, TILE), BF), pltpu.VMEM((rows, TILE), BF)],
        ),
        out_shape=[
            struct((rows, d), F32), struct((rows, d), BF), struct((d, rows), BF), struct((rows, d), F32), struct((rows, d), F32),
            struct((ff // 2, d), BF), struct((d, ff // 2), BF), struct((ff // 2, d), BF), struct((d, ff // 2), BF),
            struct((1, ff), F32),
        ],
        compiler_params=params(),
        cost_estimate=cost(rows * d * (ff * 6 + d), 40e6, rows * ff),
        name="ffn_own",
    )(core, x, ctx_own, ctx_other, wo_own, wo_other, ob, gain, shift, og, wu, wd, bias)


def ffn_other_kernel(
    per, c_ref, len_ref, mid_ref, n2_ref, n2t_ref, out_ref, dn_ref, og_ref,
    wua_ref, wda_ref, wub_ref, wdb_ref, b_ref, co_ref, cx_ref, woo_ref, wox_ref, gain_ref, db_in_ref,
    lay_ref, gm_ref, dco_ref, dcx_ref, dwoo_ref, dwox_ref, sums_ref,
    dds_ref, dus_ref, ddk_ref, duk_ref, db_ref, act_s, dh_s, out_s, dn_s, gmb_s,
):
    j = pl.program_id(0)
    rows, d = og_ref.shape

    @pl.when(j == 0)
    def _():
        out_s[...] = out_ref[...]
        dn_s[...] = dn_ref[...]

    @pl.when(j < per)
    def _():
        dwd, dwu, db = ffn_tile(
            n2_ref, n2t_ref, og_ref, wua_ref, wda_ref, b_ref, out_s, dn_s, act_s, dh_s, False
        )
        db_ref[...] = db
        dds_ref[...] = dwd.astype(BF)
        dus_ref[...] = dwu.astype(BF)

    @pl.when(j >= per)
    def _():
        dwd, dwu, db = ffn_tile(
            n2_ref, n2t_ref, og_ref, wub_ref, wdb_ref, b_ref, out_s, dn_s, act_s, dh_s, False
        )
        db_ref[...] = db
        ddk_ref[...] = dwd.astype(BF)
        duk_ref[...] = dwu.astype(BF)

    @pl.when(j == 2 * per - 1)
    def _():
        length = len_ref[0]
        sums_ref[...] = jnp.zeros_like(sums_ref)

        @pl.loop(0, rows // 256)
        def _(i):
            sl = pl.ds(pl.multiple_of(i * 256, 256), 256)
            mid = mid_ref[sl, :]
            lay_ref[sl, :] = (mid + out_s[sl, :] + db_in_ref[...]).astype(BF)
            n, r = norm_rows(mid)
            gn = dn_s[sl, :]
            og = og_ref[sl, :].astype(F32)
            gm = og + norm_back(gn * gain_ref[...], n, r)
            gm_ref[sl, :] = gm
            low = gm.astype(BF)
            gmb_s[sl, :] = low
            for at, val in enumerate((gn * n, gn, gm, og)):
                sums_ref[at : at + 1, :] += jnp.sum(val, axis=0, keepdims=True)
            valid = lax.broadcasted_iota(jnp.int32, (256, 1), 0) + i * 256 < length
            dco_ref[sl, :] = jnp.where(valid, dot(low, woo_ref[...], 1, 1), 0.0).astype(BF)
            dcx_ref[sl, :] = jnp.where(valid, dot(low, wox_ref[...], 1, 1), 0.0).astype(BF)

        dwoo_ref[...] = dot(co_ref[...], gmb_s[...], 0, 0).astype(BF)
        dwox_ref[...] = dot(cx_ref[...], gmb_s[...], 0, 0).astype(BF)


def ffn_other(core, length, mid, n2, n2t, out, dn, og, wua, wda, wub, wdb, bias, ctx_own, ctx_other, wo_own, wo_other, gain, db_in):
    rows, d = og.shape
    part = wua.shape[1]
    per = part // TILE
    half = ctx_own.shape[1]
    ia = lambda j: jnp.minimum(j, per - 1)
    ib = lambda j: jnp.maximum(j - per, 0)
    tile = lambda j, c: jnp.where(j < per, (1 - c[0]) * per + j, c[0] * per + j - per)
    return pl.pallas_call(
        lambda *refs: ffn_other_kernel(per, *refs),
        grid_spec=pltpu.PrefetchScalarGridSpec(
            num_scalar_prefetch=2,
            grid=(2 * per,),
            in_specs=[
                whole((rows, d)), whole((rows, d)), whole((d, rows)), whole((rows, d)), whole((rows, d)), whole((rows, d)),
                pl.BlockSpec((d, TILE), lambda j, *_: (0, ia(j))),
                pl.BlockSpec((TILE, d), lambda j, *_: (ia(j), 0)),
                pl.BlockSpec((d, TILE), lambda j, *_: (0, ib(j))),
                pl.BlockSpec((TILE, d), lambda j, *_: (ib(j), 0)),
                pl.BlockSpec((1, TILE), lambda j, c, n: (0, tile(j, c))),
                whole((rows, half)), whole((rows, half)), whole((half, d)), whole((half, d)), whole((1, d)), whole((1, d)),
            ],
            out_specs=[
                whole_out((rows, d)), whole_out((rows, d)), whole_out((rows, half)), whole_out((rows, half)),
                whole_out((half, d)), whole_out((half, d)), whole_out((8, d)),
            ]
            + send_keep_specs(per, d)
            + [pl.BlockSpec((1, TILE), lambda j, c, n: (0, tile(j, c)))],
            scratch_shapes=[
                pltpu.VMEM((rows, TILE), BF), pltpu.VMEM((rows, TILE), BF),
                pltpu.VMEM((rows, d), F32), pltpu.VMEM((rows, d), F32), pltpu.VMEM((rows, d), BF),
            ],
        ),
        out_shape=[
            struct((rows, d), BF), struct((rows, d), F32), struct((rows, half), BF), struct((rows, half), BF),
            struct((half, d), BF), struct((half, d), BF), struct((8, d), F32),
            struct((part, d), BF), struct((d, part), BF), struct((part, d), BF), struct((d, part), BF),
            struct((1, 2 * part), F32),
        ],
        compiler_params=params(),
        cost_estimate=cost(rows * d * (part * 12 + 2 * d), 50e6, rows * part * 2),
        name="ffn_other",
    )(core, length, mid, n2, n2t, out, dn, og, wua, wda, wub, wdb, bias, ctx_own, ctx_other, wo_own, wo_other, gain, db_in)


def project_grad_kernel(c_ref, nt_ref, dq_ref, dk_ref, dv_ref, send_ref, keep_ref):
    half = send_ref.shape[0]
    width = dq_ref.shape[1]
    c = c_ref[0]
    for ref, part in ((send_ref, 1 - c), (keep_ref, c)):
        nt = nt_ref[pl.ds(pl.multiple_of(part * half, half), half), :]
        for i, g in enumerate((dq_ref, dk_ref, dv_ref)):
            ref[:, i * width : (i + 1) * width] = dot(nt, g[...]).astype(BF)


def project_grad(core, nt, dq, dk, dv):
    d, rows = nt.shape
    width = dq.shape[1]
    return pl.pallas_call(
        project_grad_kernel,
        grid_spec=pltpu.PrefetchScalarGridSpec(
            num_scalar_prefetch=1,
            grid=(1,),
            in_specs=[whole((d, rows))] + [whole((rows, width))] * 3,
            out_specs=[whole_out((d // 2, 3 * width))] * 2,
        ),
        out_shape=[struct((d // 2, 3 * width), BF)] * 2,
        compiler_params=params(),
        cost_estimate=cost(rows * d * width * 3, 6e6),
        name="project_grad",
    )(core, nt, dq, dk, dv)


def input_grad_kernel(
    x_ref, gm_ref, gain_ref, q0, k0, v0, wq_ref, wk_ref, wv_ref, q1, k1, v1, wx_ref, out_ref, sums_ref
):
    width = q0.shape[1]
    wx = [wx_ref[:, i * width : (i + 1) * width] for i in range(3)]
    gn = jnp.zeros(gm_ref.shape, F32)
    for g, w in ((q0, wq_ref[...]), (k0, wk_ref[...]), (v0, wv_ref[...]), (q1, wx[0]), (k1, wx[1]), (v1, wx[2])):
        gn = gn + dot(g[...], w, 1, 1)
    n, r = norm_rows(x_ref[...].astype(F32))
    out_ref[...] = (gm_ref[...] + norm_back(gn * gain_ref[...], n, r)).astype(BF)

    @pl.when(pl.program_id(0) == 0)
    def _():
        sums_ref[...] = jnp.zeros_like(sums_ref)

    sums_ref[0:1, :] += jnp.sum(gn * n, axis=0, keepdims=True)
    sums_ref[1:2, :] += jnp.sum(gn, axis=0, keepdims=True)


def input_grad(x, gm, gain, own, wq, wk, wv, other, wx):
    rows, d = x.shape
    width = wq.shape[1]
    blk = 256
    row = lambda w: pl.BlockSpec((blk, w), lambda i: (i, 0))
    return pl.pallas_call(
        input_grad_kernel,
        grid=(rows // blk,),
        in_specs=[row(d), row(d), whole((1, d))]
        + [row(width)] * 3
        + [whole((d, width))] * 3
        + [row(width)] * 3
        + [whole((d, 3 * width))],
        out_specs=[row(d), whole_out((8, d))],
        out_shape=[struct((rows, d), BF), struct((8, d), F32)],
        compiler_params=params(),
        cost_estimate=cost(rows * d * width * 6, 14e6),
        name="input_grad",
    )(x, gm, gain, *own, wq, wk, wv, *other, wx)


def add(a, b):
    return (a.astype(F32) + b.astype(F32)).astype(a.dtype)


class Links:
    def __init__(self, dp_size):
        self.size = dp_size
        self.bits = dp_size.bit_length() - 1
        self.index = lax.axis_index("dp")

    def bit(self, at):
        return (self.index >> at) & 1

    def swap(self, value, at):
        return lax.ppermute(value, "dp", [(i, i ^ (1 << at)) for i in range(self.size)])

    def across(self, value):
        return lax.ppermute(value, "tensor", [(0, 1), (1, 0)])

    def scatter(self, value, at):
        half = value.shape[0] // 2
        mine = self.bit(at)
        send = lax.dynamic_slice_in_dim(value, (1 - mine) * half, half, 0)
        keep = lax.dynamic_slice_in_dim(value, mine * half, half, 0)
        return add(keep, self.swap(send, at))

    def gather(self, value, at):
        other = self.swap(value, at)
        lower = self.bit(at) == 0
        return jnp.concatenate([jnp.where(lower, value, other), jnp.where(lower, other, value)], 0)

    def reduce(self, own_send, own_keep, other_send, other_keep):
        other = add(other_keep, self.swap(other_send, 0))
        own = add(own_keep, self.swap(own_send, 0))
        value = add(own, self.across(other))
        for at in range(1, self.bits):
            value = self.scatter(value, at)
        for at in reversed(range(1, self.bits)):
            value = self.gather(value, at)
        return value, self.swap(value, 0)

    def total(self, value):
        value = value + self.across(value)
        for at in range(self.bits):
            value = value + self.swap(value, at)
        return value


def layer(
    dp_size, inputs, lengths, norm1_gain, norm1_shift, query_weight, query_bias, key_weight, key_bias, value_weight,
    value_bias, out_weight, out_bias, norm2_gain, norm2_shift, up_weight, up_bias, down_weight, down_bias, out_grad,
):
    rows, d = inputs.shape
    width = query_weight.shape[1]
    ff = up_weight.shape[1]
    links = Links(dp_size)
    tensor = lax.axis_index("tensor")
    c = links.bit(0)
    core = c.reshape(1).astype(jnp.int32)
    length = lax.dynamic_slice_in_dim(lengths, tensor, 1, 0)
    cos, sin = (jnp.asarray(t) for t in rotary_tables(rows))
    row = lambda v: v.reshape(1, -1)

    biases = jnp.concatenate([query_bias, key_bias, value_bias, up_bias])
    biases_x = links.across(biases)
    cut = lambda w, axis: lax.dynamic_slice_in_dim(w, c * (w.shape[axis] // 2), w.shape[axis] // 2, axis)
    qkv_part = links.across(jnp.concatenate([cut(w, 0) for w in (query_weight, key_weight, value_weight)], 1))
    out_part = links.across(cut(out_weight, 0))
    up_part = links.across(cut(up_weight, 1))
    down_part = links.across(cut(down_weight, 0))

    def ordered(part, axis):
        other = links.swap(part, 0)
        lower = c == 0
        return jnp.concatenate([jnp.where(lower, part, other), jnp.where(lower, other, part)], axis)

    normed, normed_t, *own = project_own(
        inputs, row(norm1_gain), row(norm1_shift), query_weight, key_weight, value_weight,
        row(biases[: 3 * width]), cos, sin,
    )
    ctx_own, aug_own = attend(length, *own)
    qkv_x = ordered(qkv_part, 0)
    other = project_other(normed, qkv_x, row(biases_x[: 3 * width]), cos, sin)
    ctx_x, aug_x = attend(length, *other)
    out_x = ordered(out_part, 0)
    mid, n2, n2t, out, dn, dd_s, du_s, dd_k, du_k, dbu = ffn_own(
        core, inputs, ctx_own, ctx_x, out_weight, out_x, row(out_bias), row(norm2_gain), row(norm2_shift), out_grad,
        up_weight, down_weight, row(up_bias),
    )
    up_far = links.swap(up_part, 0)
    down_far = links.swap(down_part, 0)
    layer_out, gm, g_own, g_x, dwo, dwo_x, sums2, ddx_s, dux_s, ddx_k, dux_k, dbu_x = ffn_other(
        core, length, mid, n2, n2t, out, dn, out_grad, up_far, down_far, up_part, down_part,
        row(biases_x[3 * width :]), ctx_own, ctx_x, out_weight, out_x, row(norm2_gain), row(down_bias),
    )
    grad_down = links.reduce(dd_s, dd_k, ddx_s, ddx_k)
    grad_up = links.reduce(du_s, du_k, dux_s, dux_k)
    flip = lambda w, part: lax.dynamic_slice_in_dim(w, part * (w.shape[0] // 2), w.shape[0] // 2, 0)
    grad_out = links.reduce(flip(dwo, 1 - c), flip(dwo, c), flip(dwo_x, 1 - c), flip(dwo_x, c))

    *gx, sums_x = attend_back(length, *other, g_x, ctx_x, aug_x, cos, sin)
    qx_s, qx_k = project_grad(core, normed_t, *gx)
    *go, sums_o = attend_back(length, *own, g_own, ctx_own, aug_own, cos, sin)
    qo_s, qo_k = project_grad(core, normed_t, *go)
    grad_qkv = links.reduce(qo_s, qo_k, qx_s, qx_k)
    input_grad_out, sums1 = input_grad(
        inputs, gm, row(norm1_gain), go, query_weight, key_weight, value_weight, gx, qkv_x
    )

    halves = lambda a, b: [jnp.where(tensor == 0, a, b), jnp.where(tensor == 0, b, a)]
    small = jnp.concatenate(
        [sums1[0], sums1[1], sums2[2], sums2[0], sums2[1], sums2[3]]
        + halves(jnp.concatenate([sums_o[:3].reshape(-1), dbu[0]]), jnp.concatenate([sums_x[:3].reshape(-1), dbu_x[0]]))
    )
    small = links.total(small.reshape(-1, 128)).reshape(-1)
    vec = [small[i * d : (i + 1) * d] for i in range(6)]
    side = 3 * width + ff
    mine = lax.dynamic_slice_in_dim(small, 6 * d + tensor * side, side, 0)

    def final(pair, axis):
        lower = c == 0
        a, b = pair
        return jnp.concatenate([jnp.where(lower, a, b), jnp.where(lower, b, a)], axis).astype(F32)

    qkv = final(grad_qkv, 0)
    return (
        layer_out,
        input_grad_out,
        vec[0],
        vec[1],
        qkv[:, :width],
        mine[:width],
        qkv[:, width : 2 * width],
        mine[width : 2 * width],
        qkv[:, 2 * width :],
        mine[2 * width : 3 * width],
        final(grad_out, 0),
        vec[2],
        vec[3],
        vec[4],
        final(grad_up, 1),
        mine[3 * width :],
        final(grad_down, 0),
        vec[5],
    )


def solution(mesh):
    rows = P(("dp", "tensor"), None)
    cols = P(None, "tensor")
    tens = P("tensor")
    return jax.shard_map(
        lambda *args: layer(mesh.shape["dp"], *args),
        mesh=mesh,
        in_specs=(
            rows, P("dp"), P(), P(), cols, tens, cols, tens, cols, tens, P("tensor", None), P(), P(), P(), cols, tens,
            P("tensor", None), P(), rows,
        ),
        out_specs=(
            rows, rows, P(), P(), cols, tens, cols, tens, cols, tens, P("tensor", None), P(), P(), P(), cols, tens,
            P("tensor", None), P(),
        ),
        check_vma=False,
    )
```

```python
import math

import jax
import jax.numpy as jnp
import numpy as np
from jax import lax
from jax.experimental import pallas as pl
from jax.experimental.pallas import tpu as pltpu
from jax.sharding import PartitionSpec as P

HEAD_DIM = 64
EPS = 1e-05
LOG2E = math.log2(math.e)
LN2 = math.log(2.0)
F32 = jnp.float32
BF = jnp.bfloat16
BIG = -1e30


def dot(a, b, ca=1, cb=0):
    return lax.dot_general(a, b, (((ca,), (cb,)), ((), ())), preferred_element_type=F32)


def cost(macs, nbytes, exps=0):
    return pl.CostEstimate(flops=int(2 * macs), bytes_accessed=int(nbytes), transcendentals=int(exps))


def busy(micros):
    return pl.CostEstimate(flops=int(micros * 1.1e9), bytes_accessed=1000, transcendentals=0)


EST = {
    "move": busy(0.01),
    "heads_own": busy(16),
    "heads_other": busy(100),
    "ffn_own": busy(0.01),
    "ffn_mine": busy(100),
    "ffn_far": busy(100),
    "share": busy(8),
    "input_grad": busy(8),
    "halve": busy(20),
}


def struct(shape, dtype):
    return jax.ShapeDtypeStruct(shape, dtype)


def whole(shape):
    return pl.BlockSpec(shape, lambda *_: (0,) * len(shape), pipeline_mode=pl.Buffered(1))


def whole_out(shape):
    return pl.BlockSpec(shape, lambda *_: (0,) * len(shape))


ANY = pl.BlockSpec(memory_space=pl.ANY)


def call(kernel, after, *, in_specs, out_specs, out_shape, estimate, name, grid=(1,), prefetch=0, scratch=(), alias=None, mib=28):
    after = tuple(after)
    n_in = prefetch + len(in_specs)

    def body(*refs):
        kernel(*refs[:n_in], *refs[n_in + len(after) :])

    run = pl.pallas_call(
        body,
        grid_spec=pltpu.PrefetchScalarGridSpec(
            num_scalar_prefetch=prefetch,
            grid=grid,
            in_specs=list(in_specs) + [ANY] * len(after),
            out_specs=out_specs,
            scratch_shapes=list(scratch),
        ),
        out_shape=out_shape,
        compiler_params=pltpu.CompilerParams(vmem_limit_bytes=mib << 20),
        input_output_aliases=alias or {},
        cost_estimate=estimate,
        name=name,
    )
    return lambda *args: run(*args, *after)


def norm_rows(v):
    mean = jnp.mean(v, axis=1, keepdims=True)
    cent = v - mean
    var = jnp.mean(cent * cent, axis=1, keepdims=True)
    r = lax.rsqrt(var + EPS)
    return cent * r, r


def norm_back(e, n, r):
    return r * (e - jnp.mean(e, axis=1, keepdims=True) - n * jnp.mean(e * n, axis=1, keepdims=True))


def rotary_tables(rows):
    half = HEAD_DIM // 2
    freq = (10000.0 ** (-2.0 * np.arange(half, dtype=np.float32) / HEAD_DIM)).astype(np.float32)
    ang = (np.arange(rows, dtype=np.float32)[:, None] * freq[None, :]).astype(np.float64)
    cos = np.cos(ang).astype(np.float32)
    sin = np.sin(ang).astype(np.float32)
    return np.concatenate([cos] * 4, 1), np.concatenate([-sin, sin] * 2, 1)


def swap_halves(v):
    lane = lax.broadcasted_iota(jnp.int32, v.shape, 1)
    return jnp.where((lane & 32) == 0, pltpu.roll(v, 96, 1), pltpu.roll(v, 32, 1))


def rotate(v, cos, sin):
    return v * cos + swap_halves(v) * sin


def rotate_back(v, cos, sin):
    return v * cos - swap_halves(v) * sin


class Row:
    def __init__(self, d, width, ff):
        at = 0
        for name, size in (
            ("gain1", d), ("shift1", d), ("out_bias", d), ("gain2", d), ("shift2", d), ("down_bias", d),
            ("qkv", 3 * width), ("up", ff),
        ):
            setattr(self, name, slice(at, at + size))
            at += size


def pull(src, dst, sem):
    copy = pltpu.make_async_copy(src, dst, sem)
    copy.start()
    return copy


def arrange(bits, arrays, shapes, moves, name, after=(), mib=28):
    def kernel(bits_ref, *refs):
        ins, outs, sem = refs[: len(arrays)], refs[len(arrays) : -1], refs[-1]
        copies = [pull(src, dst, sem.at[i]) for i, (src, dst) in enumerate(moves(bits_ref, ins, outs))]
        for copy in copies:
            copy.wait()

    return call(
        kernel,
        after,
        prefetch=1,
        in_specs=[ANY] * len(arrays),
        out_specs=[whole_out(shape) for shape in shapes],
        out_shape=[struct(shape, BF) for shape in shapes],
        scratch=[pltpu.SemaphoreType.DMA((8,))],
        estimate=EST["move"],
        name=name,
        mib=mib,
    )(bits, *arrays)


def block(bit, size):
    return pl.ds(pl.multiple_of(bit * size, size), size)


def fold(bits, parts, rows, outs, name, after=(), width=None):
    arrays = [p[0] for p in parts]
    width = width or arrays[0].shape[1]
    dtype = arrays[0].dtype
    half = rows // 2
    shapes = [(half, width)] * 2 if isinstance(outs, int) else [(n, width) for _, n in outs]

    def kernel(bits_ref, *refs):
        ins, outs_r, acc = refs[: len(parts)], refs[len(parts) : -1], refs[-1]
        seen = []
        for ref, (_, src, dst, n) in zip(ins, parts):
            value = ref[src : src + n, 0:width].astype(F32)
            fresh = not any(dst < b and a < dst + n for a, b in seen)
            acc[dst : dst + n, :] = value if fresh else acc[dst : dst + n, :] + value
            seen.append((dst, dst + n))
        if isinstance(outs, int):
            bit = bits_ref[outs]
            for ref, at in zip(outs_r, (1 - bit, bit)):
                ref[...] = acc[pl.ds(pl.multiple_of(at * half, 8 if half % 8 == 0 else 1), half), :].astype(dtype)
        else:
            for ref, (start, n) in zip(outs_r, outs):
                ref[...] = acc[start : start + n, :].astype(dtype)

    return call(
        kernel,
        after,
        prefetch=1,
        in_specs=[whole(a.shape) for a in arrays],
        out_specs=[whole_out(shape) for shape in shapes],
        out_shape=[struct(shape, dtype) for shape in shapes],
        scratch=[pltpu.VMEM((rows, width), F32)],
        estimate=EST["move"],
        name=name,
    )(bits, *arrays)


def put_qkv(pre, cos, sin, q_ref, k_ref, v_ref):
    width = q_ref.shape[1]
    for i in range(width // 128):
        sl = slice(i * 128, (i + 1) * 128)
        q_ref[:, sl] = (rotate(pre[0][:, sl], cos, sin) * (LOG2E / 8.0)).astype(BF)
        k_ref[:, sl] = rotate(pre[1][:, sl], cos, sin).astype(BF)
        v_ref[:, sl] = pre[2][:, sl].astype(BF)


def split3(v):
    hi = v.astype(BF)
    rest = v - hi.astype(F32)
    mid = rest.astype(BF)
    lo = rest - mid.astype(F32)
    return hi.astype(F32), mid.astype(F32), lo


def spread(lane, first, one, two):
    out = jnp.where(lane == 0, first, 0.0)
    for at, part in enumerate((*split3(one), *split3(two))):
        out = jnp.where(lane == at + 1, part, out)
    return out.astype(BF)


def attend_pair(length, q_ref, k_ref, v_ref, ctx_ref, aug_ref):
    bq = 256
    rows = q_ref.shape[0]
    lane1 = lax.broadcasted_iota(jnp.int32, (1, 128), 1)
    krow = lax.broadcasted_iota(jnp.int32, (rows, 128), 0)
    klane = lax.broadcasted_iota(jnp.int32, (rows, 128), 1)
    lane = lax.broadcasted_iota(jnp.int32, (bq, 128), 1)
    qrow = lax.broadcasted_iota(jnp.int32, (bq, 128), 0)
    kaug = jnp.where((klane == 0) & (krow >= length), BIG, 0.0).astype(BF)
    k = jnp.concatenate([k_ref[...], kaug], 1)
    v = jnp.concatenate([v_ref[...], jnp.ones((rows, 128), BF)], 1)
    qaug = jnp.where(lane == 0, 1.0, 0.0).astype(BF)
    for i in range(rows // bq):
        sl = slice(i * bq, (i + 1) * bq)
        q = q_ref[sl, :]
        outs, totals = [], []
        for h in range(2):
            keep = ((lane1 < 64) if h == 0 else (lane1 >= 64)).astype(BF)
            s = dot(jnp.concatenate([q * keep, qaug], 1), k, 1, 1)
            top = jnp.max(s, axis=1, keepdims=True)
            p = jnp.exp2(s - top).astype(BF)
            o = dot(p, v)
            total = o[:, 128:]
            outs.append(o[:, :128] / total)
            totals.append(top + jnp.log2(total))
        ctx = jnp.where(lane < 64, outs[0], outs[1])
        ctx_ref[sl, :] = jnp.where(qrow + i * bq < length, ctx, 0.0).astype(BF)
        aug_ref[sl, :] = spread(lane, 1.0, totals[0], totals[1])


def attend_all(length, q, k, v, ctx, aug):
    @pl.loop(0, q.shape[1] // 128)
    def _(p):
        sl = pl.ds(pl.multiple_of(p * 128, 128), 128)
        attend_pair(length, *(ref.at[:, sl] for ref in (q, k, v, ctx, aug)))


def heads_own_kernel(
    at, cut, bits_ref, len_ref, x_ref, vec_ref, wq_ref, wk_ref, wv_ref, cos_ref, sin_ref, wu_h, wd_h,
    n_h, nt_h, q_h, k_h, v_h, ctx_h, aug_h, near_h, rest_h,
    n_s, nt_s, q_s, k_s, v_s, ctx_s, aug_s, near_s, rest_s, sem,
):
    rows = x_ref.shape[0]
    width = q_s.shape[1]
    loads = [
        pull(src, dst, sem.at[i]) for i, (src, dst) in enumerate(cut(bits_ref, (wu_h, wd_h), (near_s, rest_s)))
    ]
    blk = 256
    bias = vec_ref[:, at.qkv]
    for i in range(rows // blk):
        sl = slice(i * blk, (i + 1) * blk)
        n, _ = norm_rows(x_ref[sl, :].astype(F32))
        low = (n * vec_ref[:, at.gain1] + vec_ref[:, at.shift1]).astype(BF)
        n_s[sl, :] = low
        nt_s[:, sl] = low.T
        pre = [
            dot(low, w[...]) + bias[:, j * width : (j + 1) * width] for j, w in enumerate((wq_ref, wk_ref, wv_ref))
        ]
        put_qkv(pre, cos_ref[sl, :], sin_ref[sl, :], *(ref.at[sl, :] for ref in (q_s, k_s, v_s)))
    for load in loads:
        load.wait()
    pairs = [
        (near_s, near_h), (rest_s, rest_h), (n_s, n_h), (nt_s, nt_h), (q_s, q_h), (k_s, k_h), (v_s, v_h)
    ]
    stores = [pull(src, dst, sem.at[8 + i]) for i, (src, dst) in enumerate(pairs)]
    attend_all(len_ref[0], q_s, k_s, v_s, ctx_s, aug_s)
    stores += [pull(ctx_s, ctx_h, sem.at[15]), pull(aug_s, aug_h, sem.at[16])]
    for store in stores:
        store.wait()


def heads_own(at, cut, shapes, bits, length, x, vec, wq, wk, wv, cos, sin, wu, wd, after=()):
    rows, d = x.shape
    width = wq.shape[1]
    outs = [(rows, d), (d, rows)] + [(rows, width)] * 5 + list(shapes)
    return call(
        lambda *refs: heads_own_kernel(at, cut, *refs),
        after,
        prefetch=2,
        in_specs=[whole(a.shape) for a in (x, vec, wq, wk, wv, cos, sin)] + [ANY] * 2,
        out_specs=[ANY] * len(outs),
        out_shape=[struct(shape, BF) for shape in outs],
        scratch=[pltpu.VMEM(shape, BF) for shape in outs] + [pltpu.SemaphoreType.DMA((17,))],
        estimate=EST["heads_own"],
        name="heads_own",
        mib=56,
    )(bits, length, x, vec, wq, wk, wv, cos, sin, wu, wd)


def heads_other_kernel(
    bits_ref, len_ref, n_ref, wm_ref, wf_ref, b_ref, cos_ref, sin_ref, q_h, k_h, v_h, ctx_h, aug_h,
    q_s, k_s, v_s, ctx_s, aug_s, sem,
):
    rows = n_ref.shape[0]
    width = q_s.shape[1]
    half = wm_ref.shape[0]
    c = bits_ref[0]
    blk = 256
    for i in range(rows // blk):
        sl = slice(i * blk, (i + 1) * blk)
        pre = dot(n_ref[sl, block(c, half)], wm_ref[...]) + dot(n_ref[sl, block(1 - c, half)], wf_ref[...])
        pre = pre + b_ref[:, : 3 * width]
        put_qkv(
            [pre[:, j * width : (j + 1) * width] for j in range(3)], cos_ref[sl, :], sin_ref[sl, :],
            *(ref.at[sl, :] for ref in (q_s, k_s, v_s)),
        )
    stores = [pull(src, dst, sem.at[i]) for i, (src, dst) in enumerate(((q_s, q_h), (k_s, k_h), (v_s, v_h)))]
    attend_all(len_ref[0], q_s, k_s, v_s, ctx_s, aug_s)
    stores += [pull(ctx_s, ctx_h, sem.at[3]), pull(aug_s, aug_h, sem.at[4])]
    for store in stores:
        store.wait()


def heads_other(bits, length, n, w_mine, w_far, bias, cos, sin, after=()):
    rows = n.shape[0]
    width = w_mine.shape[1] // 3
    outs = [(rows, width)] * 5
    return call(
        heads_other_kernel,
        after,
        prefetch=2,
        in_specs=[whole(a.shape) for a in (n, w_mine, w_far, bias, cos, sin)],
        out_specs=[ANY] * 5,
        out_shape=[struct(shape, BF) for shape in outs],
        scratch=[pltpu.VMEM(shape, BF) for shape in outs] + [pltpu.SemaphoreType.DMA((5,))],
        estimate=EST["heads_other"],
        name="heads_other",
        mib=56,
    )(bits, length, n, w_mine, w_far, bias, cos, sin)


def attend_back_kernel(
    bq, bits_ref, len_ref, q_ref, k_ref, v_ref, g_ref, ctx_ref, aug_ref, cos_ref, sin_ref, nt_ref, wo_ref,
    d_ref, sum_ref, send_ref, keep_ref, dqt, dall,
):
    rows = q_ref.shape[0]
    length = len_ref[0]
    lane1 = lax.broadcasted_iota(jnp.int32, (1, 128), 1)
    krow = lax.broadcasted_iota(jnp.int32, (rows, 128), 0)
    klane = lax.broadcasted_iota(jnp.int32, (rows, 128), 1)
    lane = lax.broadcasted_iota(jnp.int32, (bq, 128), 1)
    k = k_ref[...]
    v = v_ref[...]
    kt = k.T
    dks, dvs = [], []
    for h in range(2):
        keep = ((lane1 < 64) if h == 0 else (lane1 >= 64)).astype(BF)
        first = 1 + 3 * h
        mine = jnp.where((klane >= first) & (klane < first + 3), -1.0, 0.0)
        kaug = jnp.where((klane == 0) & (krow >= length), BIG, mine).astype(BF)
        kh = jnp.concatenate([k * keep, kaug], 1)
        vh = jnp.concatenate([v * keep, mine.astype(BF)], 1)
        dk = jnp.zeros((rows, 128), F32)
        dv = jnp.zeros((rows, 128), F32)
        for i in range(rows // bq):
            sl = slice(i * bq, (i + 1) * bq)
            q = q_ref[sl, :]
            g = g_ref[sl, :]
            prod = g.astype(F32) * ctx_ref[sl, :].astype(F32)
            d0 = jnp.sum(jnp.where(lane < 64, prod, 0.0), 1, keepdims=True)
            d1 = jnp.sum(jnp.where(lane < 64, 0.0, prod), 1, keepdims=True)
            gaug = spread(lane, 0.0, d0, d1)
            st = dot(kh, jnp.concatenate([q, aug_ref[sl, :]], 1), 1, 1)
            pt = jnp.exp2(st)
            dpt = dot(vh, jnp.concatenate([g, gaug], 1), 1, 1)
            ds = (pt * dpt).astype(BF)
            dv = dv + dot(pt.astype(BF), g)
            dk = dk + dot(ds, q)
            dqt[h * 64 : (h + 1) * 64, sl] = dot(kt[h * 64 : (h + 1) * 64, :], ds)
        dks.append(dk)
        dvs.append(dv)
    cos = cos_ref[...]
    sin = sin_ref[...]
    dq = rotate_back(dqt[...].T * (1.0 / 8.0), cos, sin).astype(BF)
    dk = rotate_back(jnp.where(klane < 64, dks[0], dks[1]) * LN2, cos, sin).astype(BF)
    dv = jnp.where(klane < 64, dvs[0], dvs[1]).astype(BF)
    for at, val in enumerate((dq, dk, dv)):
        sl = slice(at * 128, (at + 1) * 128)
        d_ref[:, sl] = val
        sum_ref[:, sl] = jnp.sum(val.astype(F32), axis=0, keepdims=True)
    j = pl.program_id(0)
    dall[:, block(j, 384)] = jnp.concatenate([dq, dk, dv], 1)

    @pl.when(j == pl.num_programs(0) - 1)
    def _():
        half = send_ref.shape[0]
        c = bits_ref[0]
        for ref, part in ((send_ref, 1 - c), (keep_ref, c)):
            width = dall.shape[1]
            ref[:, 0:width] = dot(nt_ref[block(part, half), :], dall[...]).astype(BF)
            ref[:, width:] = wo_ref[block(part, half), :]


def attend_back(bits, length, q, k, v, g, ctx, aug, cos, sin, nt, wo, after=(), est=100):
    rows, width = q.shape
    d = 2 * width
    bs = pl.BlockSpec((rows, 128), lambda j, *_: (0, j))
    return call(
        lambda *refs: attend_back_kernel(256, *refs),
        after,
        prefetch=2,
        grid=(width // 128,),
        in_specs=[bs] * 6 + [whole((rows, 128))] * 2 + [whole(nt.shape), whole(wo.shape)],
        out_specs=[pl.BlockSpec((rows, 384), lambda j, *_: (0, j)), pl.BlockSpec((1, 384), lambda j, *_: (0, j))]
        + [whole_out((d // 2, 4 * width))] * 2,
        out_shape=[struct((rows, 3 * width), BF), struct((1, 3 * width), F32)] + [struct((d // 2, 4 * width), BF)] * 2,
        scratch=[pltpu.VMEM((128, rows), F32), pltpu.VMEM((rows, 3 * width), BF)],
        estimate=busy(est),
        name="attend_back",
        mib=56,
    )(bits, length, q, k, v, g, ctx, aug, cos, sin, nt, wo)


def gelu_pair(h):
    z = jnp.abs(h) * (0.3275911 / math.sqrt(2.0)) + 1.0
    t = pl.reciprocal(z, approx=True)
    t = t * (2.0 - z * t)
    e = jnp.exp2(h * h * (-0.5 * LOG2E))
    poly = 0.5 * 1.061405429 * t - 0.5 * 1.453152027
    poly = poly * t + 0.5 * 1.421413741
    poly = poly * t - 0.5 * 0.284496736
    poly = poly * t + 0.5 * 0.254829592
    w = poly * t * e
    cdf = jnp.where(h >= 0.0, 1.0 - w, w)
    return h * cdf, cdf + h * e * (1.0 / math.sqrt(2.0 * math.pi))


def ffn_quarter(n2, n2t, og, wu, wd, bias, out_acc, dn_acc, act_s, dh_s, gd, gu, first, before=None, done=None):
    rows, d = og.shape
    part = wd.shape[0]
    blk = 256
    dbias = jnp.zeros((1, part), F32)
    if before is not None:
        before(0, blk)
    for i in range(rows // blk):
        sl = slice(i * blk, (i + 1) * blk)
        if before is not None and i + 1 < rows // blk:
            before(i + 1, blk)
        h = dot(n2[sl, :], wu[...]) + bias
        act, slope = gelu_pair(h)
        act = act.astype(BF)
        dh = (slope * dot(og[sl, :], wd[...], 1, 1)).astype(BF)
        act_s[sl, :] = act
        dh_s[sl, :] = dh
        dbias = dbias + jnp.sum(dh.astype(F32), axis=0, keepdims=True)
        o = dot(act, wd[...])
        e = dot(dh, wu[...], 1, 1)
        out_acc[sl, :] = o if first else out_acc[sl, :] + o
        dn_acc[sl, :] = e if first else dn_acc[sl, :] + e
        if done is not None and i > 0:
            done(i - 1, blk)
    if done is not None:
        done(rows // blk - 1, blk)
    gd[...] = dot(act_s[...], og[...], 0, 0).astype(BF)
    gu[...] = dot(n2t[...], dh_s[...]).astype(BF)
    return dbias


def ffn_own_kernel(
    at, bits_ref, x_ref, co_ref, cx_ref, woo_ref, wox, vec_ref, og_h, wu_h, wd_h,
    mid_h, n2_h, n2t_h, out_h, dn_h, send_h, keep_h, db_ref,
    og, wu, wd, mid, n2, n2t, out, dn, outb, dnb, act_s, dh_s, gd, gu, sem,
):
    rows, d = x_ref.shape
    part = wu_h.shape[1] // 2
    c = bits_ref[0]
    cols = [block(p, part) for p in (1 - c, c)]
    biases = [pl.ds(pl.multiple_of(at.up.start + p * part, 128), part) for p in (1 - c, c)]
    loads = [pull(og_h, og, sem.at[0])]
    for q in range(2):
        loads.append(pull(wu_h.at[:, cols[q]], wu.at[q], sem.at[1 + 2 * q]))
        loads.append(pull(wd_h.at[cols[q], :], wd.at[q], sem.at[2 + 2 * q]))
    stores = []

    def enter(i, blk):
        sl = slice(i * blk, (i + 1) * blk)
        att = dot(co_ref[sl, :], woo_ref[...]) + dot(cx_ref[sl, :], wox[...])
        v = x_ref[sl, :].astype(F32) + att + vec_ref[:, at.out_bias]
        mid[sl, :] = v
        n, _ = norm_rows(v)
        low = (n * vec_ref[:, at.gain2] + vec_ref[:, at.shift2]).astype(BF)
        n2[sl, :] = low
        n2t[:, sl] = low.T
        if i == 0:
            for load in loads:
                load.wait()
        if (i + 1) * blk == rows:
            stores.extend([pull(mid, mid_h, sem.at[5]), pull(n2, n2_h, sem.at[6]), pull(n2t, n2t_h, sem.at[7])])

    def flush(i, blk):
        sl = pl.ds(i * blk, blk)
        outb[sl, :] = out[sl, :].astype(BF)
        dnb[sl, :] = dn[sl, :].astype(BF)
        stores.append(pull(outb.at[sl, :], out_h.at[sl, :], sem.at[8 + i]))
        stores.append(pull(dnb.at[sl, :], dn_h.at[sl, :], sem.at[12 + i]))

    for q in range(2):
        db_ref[:, cols[q]] = ffn_quarter(
            n2, n2t, og, wu.at[q], wd.at[q], vec_ref[:, biases[q]], out, dn, act_s, dh_s, gd.at[q], gu.at[q], q == 0,
            enter if q == 0 else None, flush if q == 1 else None,
        )
        stores.append(pull(gd.at[q], (send_h, keep_h)[q].at[0:part, :], sem.at[16 + q]))
        stores.append(pull(gu.at[q], (send_h, keep_h)[q].at[part:, :], sem.at[20 + q]))
    for store in stores:
        store.wait()


def ffn_own(at, bits, x, ctx_own, ctx_other, wo_own, wo_other, vec, og, wu, wd, after=()):
    rows, d = x.shape
    ff = wu.shape[1]
    part = ff // 2
    half = ctx_own.shape[1]
    return call(
        lambda *refs: ffn_own_kernel(at, *refs),
        after,
        prefetch=1,
        in_specs=[
            whole((rows, d)), whole((rows, half)), whole((rows, half)), whole((half, d)), whole((half, d)), whole(vec.shape),
        ] + [ANY] * 3,
        out_specs=[ANY] * 7 + [whole_out((1, ff))],
        scratch=[
            pltpu.VMEM((rows, d), BF), pltpu.VMEM((2, d, part), BF), pltpu.VMEM((2, part, d), BF),
            pltpu.VMEM((rows, d), F32), pltpu.VMEM((rows, d), BF), pltpu.VMEM((d, rows), BF),
            pltpu.VMEM((rows, d), F32), pltpu.VMEM((rows, d), F32), pltpu.VMEM((rows, d), BF), pltpu.VMEM((rows, d), BF),
            pltpu.VMEM((rows, part), BF), pltpu.VMEM((rows, part), BF),
            pltpu.VMEM((2, part, d), BF), pltpu.VMEM((2, d, part), BF),
            pltpu.SemaphoreType.DMA((22,)),
        ],
        out_shape=[
            struct((rows, d), F32), struct((rows, d), BF), struct((d, rows), BF), struct((rows, d), BF),
            struct((rows, d), BF), struct((part + d, d), BF), struct((part + d, d), BF),
            struct((1, ff), F32),
        ],
        estimate=EST["ffn_own"],
        name="ffn_own",
        mib=56,
    )(bits, x, ctx_own, ctx_other, wo_own, wo_other, vec, og, wu, wd)


BLOCK_BITS = 4


def sub_block(s, q, x, n):
    out = q + 2 * x
    for k in range(2, n):
        out = out + (((s >> (n - 1 - k)) & 1) << k)
    return out


def put_blocks(grads, stack, q, n, sem, at):
    count = 1 << (n - 2)
    size = grads[0].shape[0] // count
    return [
        pull(
            grads[x].at[s * size : (s + 1) * size, :],
            stack.at[pl.ds(pl.multiple_of(sub_block(s, q, x, n) * size, size), size), :],
            sem.at[at + x * count + s],
        )
        for x in range(2)
        for s in range(count)
    ]


def gather_weights(bits_ref, near, near_x, rest, w, sem, at):
    rows = near.shape[0]
    b = bits_ref[1]
    return [
        pull(near, w.at[block(b, rows), :], sem.at[at]),
        pull(near_x, w.at[block(1 - b, rows), :], sem.at[at + 1]),
        pull(rest, w.at[2 * rows :, :], sem.at[at + 2]),
    ]


def ffn_mine_kernel(
    n, bits_ref, n2_ref, b_ref, near_h, near_x_h, rest_h, og_h, n2t_h, out_h, dn_h, stack_h, db_ref,
    w_ref, og, n2t, out, dn, outb, dnb, act_s, dh_s, gd, gu, sem,
):
    d = og.shape[1]
    part = w_ref.shape[0] - d
    c = bits_ref[0]
    bias_at = b_ref.shape[1] - 2 * part
    at = 10 + (1 << (n - 1))
    loads = gather_weights(bits_ref, near_h, near_x_h, rest_h, w_ref, sem, at)
    loads += [pull(og_h, og, sem.at[0]), pull(n2t_h, n2t, sem.at[1])]
    for load in loads:
        load.wait()
    stores = []

    def flush(i, blk):
        sl = pl.ds(i * blk, blk)
        outb[sl, :] = out[sl, :].astype(BF)
        dnb[sl, :] = dn[sl, :].astype(BF)
        stores.append(pull(outb.at[sl, :], out_h.at[sl, :], sem.at[2 + i]))
        stores.append(pull(dnb.at[sl, :], dn_h.at[sl, :], sem.at[6 + i]))

    bias = b_ref[:, pl.ds(pl.multiple_of(bias_at + c * part, 128), part)]
    db_ref[...] = ffn_quarter(
        n2_ref, n2t, og, w_ref.at[0:d, :], w_ref.at[d:, :], bias, out, dn, act_s, dh_s, gd, gu, True, None, flush
    )
    stores += put_blocks((gd, gu), stack_h, c, n, sem, 10)
    for store in stores:
        store.wait()


def ffn_mine(bits, n2, near, near_x, rest, bias, og, n2t, after=()):
    rows, d = og.shape
    part = 2 * near.shape[0] + rest.shape[0] - d
    n = min(bits.shape[0], BLOCK_BITS)
    return call(
        lambda *refs: ffn_mine_kernel(n, *refs),
        after,
        prefetch=1,
        in_specs=[whole((rows, d)), whole(bias.shape)] + [ANY] * 5,
        out_specs=[ANY] * 3 + [whole_out((1, part))],
        scratch=[
            pltpu.VMEM((d + part, d), BF),
            pltpu.VMEM((rows, d), BF), pltpu.VMEM((d, rows), BF), pltpu.VMEM((rows, d), F32), pltpu.VMEM((rows, d), F32),
            pltpu.VMEM((rows, d), BF), pltpu.VMEM((rows, d), BF),
            pltpu.VMEM((rows, part), BF), pltpu.VMEM((rows, part), BF), pltpu.VMEM((part, d), BF), pltpu.VMEM((d, part), BF),
            pltpu.SemaphoreType.DMA((13 + (1 << (n - 1)),)),
        ],
        out_shape=[
            struct((rows, d), BF), struct((rows, d), BF), struct((4 * part, d), BF), struct((1, part), F32),
        ],
        estimate=EST["ffn_mine"],
        name="ffn_mine",
        mib=56,
    )(bits, n2, bias, near, near_x, rest, og, n2t)


def ffn_far_kernel(
    at, n, bits_ref, len_ref, n2_ref, b_ref, vec_ref, near_h, near_x_h, rest_h, og_h, n2t_h, mid_h, out1_h, dn1_h, out2_h, dn2_h,
    co_h, cx_h, woo_h, wox_h, stack_in,
    lay_h, gm_h, dco_h, dcx_h, stack_h, dwoo_h, dwox_h, sums_ref, db_ref,
    w_ref, og, n2t, mid, out1, dn1, out2, dn2, co, cx, woo, wox, out, dn, act_s, dh_s, gd, gu, lay, gmb, dco, dcx, dwoo, dwox, sem,
):
    rows, d = og.shape
    part = w_ref.shape[0] - d
    half = co.shape[1]
    c = bits_ref[0]
    length = len_ref[0]
    bias_at = b_ref.shape[1] - 2 * part
    first = gather_weights(bits_ref, near_h, near_x_h, rest_h, w_ref, sem, 18 + (1 << (n - 1)))
    loads = [
        pull(src, dst, sem.at[i])
        for i, (src, dst) in enumerate((
            (og_h, og), (n2t_h, n2t), (mid_h, mid), (dn1_h, dn1), (dn2_h, dn2), (out1_h, out1), (out2_h, out2),
            (woo_h, woo), (wox_h, wox), (co_h, co), (cx_h, cx),
        ))
    ]
    for load in first + loads[:1]:
        load.wait()
    sums_ref[...] = jnp.zeros_like(sums_ref)
    stores = []

    def finish(i, blk):
        if i == 0:
            for load in loads[1:]:
                load.wait()
        sl = slice(i * blk, (i + 1) * blk)
        v = mid[sl, :]
        out_sum = out1[sl, :].astype(F32) + out2[sl, :].astype(F32) + out[sl, :]
        lay[sl, :] = (v + out_sum + vec_ref[:, at.down_bias]).astype(BF)
        unit, r = norm_rows(v)
        gn = dn1[sl, :].astype(F32) + dn2[sl, :].astype(F32) + dn[sl, :]
        o = og[sl, :].astype(F32)
        g = o + norm_back(gn * vec_ref[:, at.gain2], unit, r)
        mid[sl, :] = g
        low = g.astype(BF)
        gmb[sl, :] = low
        for k, val in enumerate((g, gn * unit, gn, o)):
            sums_ref[k : k + 1, :] += jnp.sum(val, axis=0, keepdims=True)
        valid = lax.broadcasted_iota(jnp.int32, (blk, 1), 0) + i * blk < length
        dco[sl, :] = jnp.where(valid, dot(low, woo[...], 1, 1), 0.0).astype(BF)
        dcx[sl, :] = jnp.where(valid, dot(low, wox[...], 1, 1), 0.0).astype(BF)

    bias = b_ref[:, pl.ds(pl.multiple_of(bias_at + (1 - c) * part, 128), part)]
    db_ref[...] = ffn_quarter(
        n2_ref, n2t, og, w_ref.at[0:d, :], w_ref.at[d:, :], bias, out, dn, act_s, dh_s, gd, gu, True, None, finish
    )
    stores = put_blocks((gd, gu), stack_h, 1 - c, n, sem, 18)
    stores += [
        pull(src, dst, sem.at[12 + k])
        for k, (src, dst) in enumerate(((lay, lay_h), (mid, gm_h), (dco, dco_h), (dcx, dcx_h)))
    ]
    dwoo[...] = dot(gmb[...], co[...], 0, 0).astype(BF)
    dwox[...] = dot(gmb[...], cx[...], 0, 0).astype(BF)
    stores += [pull(dwoo, dwoo_h, sem.at[16]), pull(dwox, dwox_h, sem.at[17])]
    for store in stores:
        store.wait()


def ffn_far(
    at, bits, length, n2, near, near_x, rest, bias, vec, og, n2t, mid, out1, dn1, out2, dn2, ctx_own, ctx_other, wo_own,
    wo_other, stack, after=(),
):
    rows, d = og.shape
    part = 2 * near.shape[0] + rest.shape[0] - d
    n = min(bits.shape[0], BLOCK_BITS)
    half = ctx_own.shape[1]
    bf = lambda *shape: pltpu.VMEM(shape, BF)
    f32 = lambda *shape: pltpu.VMEM(shape, F32)
    return call(
        lambda *refs: ffn_far_kernel(at, n, *refs),
        after,
        prefetch=2,
        in_specs=[whole((rows, d)), whole(bias.shape), whole(vec.shape)] + [ANY] * 15,
        out_specs=[ANY] * 7 + [whole_out((8, d)), whole_out((1, part))],
        scratch=[
            bf(d + part, d), bf(rows, d), bf(d, rows), f32(rows, d), bf(rows, d), bf(rows, d), bf(rows, d), bf(rows, d),
            bf(rows, half), bf(rows, half), bf(half, d), bf(half, d), f32(rows, d), f32(rows, d),
            bf(rows, part), bf(rows, part), bf(part, d), bf(d, part), bf(rows, d), bf(rows, d), bf(rows, half),
            bf(rows, half), bf(d, half), bf(d, half), pltpu.SemaphoreType.DMA((21 + (1 << (n - 1)),)),
        ],
        out_shape=[
            struct((rows, d), BF), struct((rows, d), F32), struct((rows, half), BF), struct((rows, half), BF),
            struct(stack.shape, BF), struct((d, half), BF), struct((d, half), BF), struct((8, d), F32), struct((1, part), F32),
        ],
        alias={19: 4},
        estimate=EST["ffn_far"],
        name="ffn_far",
        mib=56,
    )(
        bits, length, n2, bias, vec, near, near_x, rest, og, n2t, mid, out1, dn1, out2, dn2, ctx_own, ctx_other, wo_own,
        wo_other, stack,
    )


def by_pairs(wcat, matrices, rows, width):
    for p in range(width // 128):
        for i in range(3):
            to = slice((3 * p + i) * 128, (3 * p + i + 1) * 128)
            ref, base = matrices[i]
            wcat[rows, to] = ref[:, base + p * 128 : base + (p + 1) * 128]


def share_kernel(bits_ref, g_ref, wm, wf, out_ref, wcat):
    width = g_ref.shape[1] // 3
    c = bits_ref[0]
    half = wm.shape[0]

    @pl.when(pl.program_id(0) == 0)
    def _():
        for ref, part in ((wm, c), (wf, 1 - c)):
            by_pairs(wcat, [(ref, i * width) for i in range(3)], block(part, half), width)

    out_ref[...] = dot(g_ref[...], wcat[...], 1, 1).astype(BF)


def input_share(bits, g, w_mine, w_far, after=()):
    rows, cols = g.shape
    d = 2 * w_mine.shape[0]
    blk = 512
    row = lambda w: pl.BlockSpec((blk, w), lambda i, *_: (i, 0))
    return call(
        share_kernel, after, prefetch=1, grid=(rows // blk,),
        in_specs=[row(cols), whole(w_mine.shape), whole(w_far.shape)], out_specs=row(d),
        out_shape=struct((rows, d), BF), scratch=[pltpu.VMEM((d, cols), BF)],
        estimate=EST["share"], name="input_share", mib=56,
    )(bits, g, w_mine, w_far)


def input_grad_kernel(at, x_ref, gm_ref, vec_ref, g_ref, share_ref, wq, wk, wv, out_ref, sums_ref, wcat):
    width = wq.shape[1]

    @pl.when(pl.program_id(0) == 0)
    def _():
        sums_ref[...] = jnp.zeros_like(sums_ref)
        by_pairs(wcat, [(ref, 0) for ref in (wq, wk, wv)], slice(None), width)

    gn = dot(g_ref[...], wcat[...], 1, 1) + share_ref[...].astype(F32)
    n, r = norm_rows(x_ref[...].astype(F32))
    out_ref[...] = (gm_ref[...] + norm_back(gn * vec_ref[:, at.gain1], n, r)).astype(BF)
    sums_ref[0:1, :] += jnp.sum(gn * n, axis=0, keepdims=True)
    sums_ref[1:2, :] += jnp.sum(gn, axis=0, keepdims=True)


def input_grad(at, x, gm, vec, g, share, wq, wk, wv, after=()):
    rows, d = x.shape
    width = wq.shape[1]
    blk = 256
    row = lambda w: pl.BlockSpec((blk, w), lambda i, *_: (i, 0))
    return call(
        lambda *refs: input_grad_kernel(at, *refs),
        after,
        grid=(rows // blk,),
        in_specs=[row(d), row(d), whole(vec.shape), row(3 * width), row(d)] + [whole((d, width))] * 3,
        out_specs=[row(d), whole_out((8, d))],
        out_shape=[struct((rows, d), BF), struct((8, d), F32)],
        scratch=[pltpu.VMEM((d, 3 * width), BF)],
        estimate=EST["input_grad"],
        name="input_grad",
        mib=56,
    )(x, gm, vec, g, share, wq, wk, wv)


def wide_qkv(bits, mine, other, after=()):
    half, width = mine.shape
    width //= 4

    def kernel(bits_ref, m_ref, o_ref, *outs):
        c = bits_ref[0]

        def put(ref):
            for i, out in enumerate(outs[:3]):
                for p in range(width // 128):
                    out[:, p * 128 : (p + 1) * 128] = ref[:, (3 * p + i) * 128 : (3 * p + i + 1) * 128].astype(F32)
            outs[3][...] = ref[:, 3 * width :].astype(F32).T

        own = pl.program_id(0) == c

        @pl.when(own)
        def _():
            put(m_ref)

        @pl.when(jnp.logical_not(own))
        def _():
            put(o_ref)

    return call(
        kernel, after, prefetch=1, grid=(2,),
        in_specs=[whole(mine.shape)] * 2,
        out_specs=[pl.BlockSpec((half, width), lambda i, *_: (i, 0))] * 3
        + [pl.BlockSpec((width, half), lambda i, *_: (0, i))],
        out_shape=[struct((2 * half, width), F32)] * 3 + [struct((width, 2 * half), F32)],
        estimate=EST["move"], name="wide_qkv", mib=56,
    )(bits, mine, other)


def wide_ffn(bits, stack, after=()):
    rows, d = stack.shape
    n = min(bits.shape[0], BLOCK_BITS)
    part = rows // 4
    count = 1 << (n - 2)
    size = part // count

    def kernel(bits_ref, d_ref, u_ref, down_ref, up_ref):
        down_ref[...] = d_ref[...].astype(F32)
        up_ref[...] = u_ref[...].astype(F32)

    def place(x):
        return lambda t, *_: (sub_block(lax.rem(t, count), t // count, x, n), 0)

    return call(
        kernel, after, prefetch=1, grid=(2 * count,),
        in_specs=[pl.BlockSpec((size, d), place(0)), pl.BlockSpec((size, d), place(1))],
        out_specs=[
            pl.BlockSpec((size, d), lambda t, *_: (t, 0)),
            pl.BlockSpec((size, d), lambda t, *_: (lax.rem(t, count), t // count)),
        ],
        out_shape=[struct((2 * part, d), F32), struct((part, 2 * d), F32)],
        estimate=EST["move"], name="wide_ffn", mib=56,
    )(bits, stack, stack)


class Links:
    def __init__(self, dp_size):
        self.size = dp_size
        self.bits = dp_size.bit_length() - 1
        index = lax.axis_index("dp")
        self.value = jnp.stack([(index >> i) & 1 for i in range(self.bits)]).astype(jnp.int32)

    def swap(self, value, at):
        return lax.ppermute(value, "dp", [(i, i ^ (1 << at)) for i in range(self.size)])

    def across(self, value):
        return lax.ppermute(value, "tensor", [(0, 1), (1, 0)])

    def join(self, mine, other, at, after=()):
        half, width = mine.shape
        if half % 16:
            low = self.value[at] == 0
            return jnp.concatenate([jnp.where(low, mine, other), jnp.where(low, other, mine)], 0)

        def moves(bits, ins, outs):
            return [
                (ins[0], outs[0].at[block(bits[at], half), :]), (ins[1], outs[0].at[block(1 - bits[at], half), :])
            ]

        return arrange(self.value, [mine, other], [(2 * half, width)], moves, "join", after)[0]


def halve(bits, keep, recv, bit, after=()):
    keep, recv, *_ = lax.optimization_barrier((keep, recv, *after))
    size = keep.shape[0] // 2

    def half(at):
        a, b = (lax.dynamic_slice_in_dim(v, at * size, size, 0).astype(F32) for v in (keep, recv))
        return (a + b).astype(BF)

    return half(1 - bits[bit]), half(bits[bit])


class Halve:
    def __init__(self, links, keep, recv):
        self.links, self.keep, self.recv, self.at = links, keep, recv, 0
        low = min(links.bits, BLOCK_BITS)
        self.order = [*range(low), *reversed(range(low, links.bits))]
        self.done = False

    def advance(self, after):
        links, size = self.links, self.keep.shape[0]
        self.at += 1
        self.done = self.at == links.bits
        if self.done:
            parts = [(self.keep, 0, 0, size), (self.recv, 0, 0, size)]
            self.keep, = fold(links.value, parts, size, [(0, size)], "fold_own", after)
            return
        bit = self.order[self.at]
        send, self.keep = halve(links.value, self.keep, self.recv, bit, after)
        self.recv = links.swap(send, bit)


RIDE = 32


def ride_kernel(rows, cut, bits_ref, *refs):
    *ins, small_ref, send_ref, keep_ref, next_ref, acc = refs
    width = small_ref.shape[1]
    small = small_ref[...]
    total = None
    for ref in ins:
        value = ref[0:rows, :].astype(F32)
        total = value if total is None else total + value
        if ref.shape[0] > rows:
            riding = ref[rows : rows + RIDE, :].astype(F32)
            small = small + riding[0:8] + riding[8:16] + riding[16:24]
    next_ref[...] = small
    if send_ref is None:
        keep_ref[...] = total.astype(BF)
        return
    acc[...] = total
    if cut is None:
        size = rows
        send_ref[0:size, :] = total.astype(BF)
        keep_ref[...] = total.astype(BF)
    else:
        size = rows // 2
        bit = bits_ref[cut]
        low, high = acc[0:size, :], acc[size : 2 * size, :]
        send_ref[0:size, :] = jnp.where(bit == 0, high, low).astype(BF)
        keep_ref[...] = jnp.where(bit == 0, low, high).astype(BF)
    parts = [p.astype(BF) for p in split3(small)] + [jnp.zeros((RIDE - 24, width), BF)]
    send_ref[size:, :] = jnp.concatenate(parts, 0)


def ride(bits, parts, small, cut, last, after=()):
    rows = parts[0].shape[0]
    width = small.shape[1]
    size = rows // 2 if cut is not None else rows
    shapes = [struct((size, width), BF), struct(small.shape, F32)]
    if not last:
        shapes.insert(0, struct((size + RIDE, width), BF))

    def kernel(bits_ref, *refs):
        refs = list(refs)
        if last:
            refs.insert(len(parts) + 1, None)
        ride_kernel(rows, cut, bits_ref, *refs)

    out = call(
        kernel, after, prefetch=1, in_specs=[whole(a.shape) for a in (*parts, small)],
        out_specs=[whole_out(t.shape) for t in shapes], out_shape=shapes,
        scratch=[pltpu.VMEM((rows, width), F32)], estimate=EST["move"], name="ride",
    )(bits, *parts, small)
    return (None, *out) if last else out


def layer(
    dp_size, inputs, lengths, norm1_gain, norm1_shift, query_weight, query_bias, key_weight, key_bias, value_weight,
    value_bias, out_weight, out_bias, norm2_gain, norm2_shift, up_weight, up_bias, down_weight, down_bias, out_grad,
):
    rows, d = inputs.shape
    width = query_weight.shape[1]
    ff = up_weight.shape[1]
    part = ff // 2
    links = Links(dp_size)
    bits = links.value
    tensor = lax.axis_index("tensor")
    length = lax.dynamic_slice_in_dim(lengths, tensor, 1, 0)
    cos, sin = (jnp.asarray(t) for t in rotary_tables(rows))
    at = Row(d, width, ff)
    vec = jnp.concatenate(
        [norm1_gain, norm1_shift, out_bias, norm2_gain, norm2_shift, down_bias, query_bias, key_bias, value_bias, up_bias]
    ).reshape(1, -1)

    def qkv_moves(bits_ref, ins, outs):
        return [
            (w.at[block(bits_ref[0], d // 2), :], outs[0].at[:, i * width : (i + 1) * width]) for i, w in enumerate(ins)
        ]

    near_rows = 5 * d // 12
    half = width // 2
    def cut_moves(bits_ref, ins, outs):
        c, b = bits_ref[0], bits_ref[1]
        wu, wd = ins
        near, rest = outs
        cols = block(c, part)
        return [
            (wu.at[block(b, near_rows), cols], near),
            (wu.at[2 * near_rows :, cols], rest.at[0 : d - 2 * near_rows, :]),
            (wd.at[block(c, part), :], rest.at[d - 2 * near_rows :, :]),
        ]

    qkv_mine, = arrange(bits, [query_weight, key_weight, value_weight], [(d // 2, 3 * width)], qkv_moves, "cut_qkv", mib=56)
    qkv_mine = links.across(qkv_mine)
    normed, normed_t, *own, ctx_own, aug_own, near, rest = heads_own(
        at, cut_moves, [(near_rows, d), (d + part - 2 * near_rows, d)], bits, length, inputs, vec, query_weight,
        key_weight, value_weight, cos, sin, up_weight, down_weight,
    )
    bias_x = links.across(vec[:, at.qkv.start :])
    near, out_x = links.across(near), links.across(out_weight)
    qkv_mine, _ = lax.optimization_barrier((qkv_mine, ctx_own))
    qkv_far = links.swap(qkv_mine, 0)
    *other, ctx_x, aug_x = heads_other(bits, length, normed, qkv_mine, qkv_far, bias_x, cos, sin, after=(ctx_own,))
    near, out_x, rest, ctx_x = lax.optimization_barrier((near, out_x, rest, ctx_x))
    rest = links.across(rest)
    near_x = links.swap(near, 1)
    near_far = links.swap(near, 0)
    mid, n2, n2t, out1, dn1, w_send, w_keep, dbu = ffn_own(
        at, bits, inputs, ctx_own, ctx_x, out_weight, out_x, vec, out_grad, up_weight, down_weight
    )

    w_recv = links.swap(w_send, 0)
    near_x_far, rest_far = links.swap(near_x, 0), links.swap(rest, 0)
    out2, dn2, stack, dbu_mine = ffn_mine(bits, n2, near, near_x, rest, bias_x, out_grad, n2t, after=(mid,))
    own_sum = Halve(links, w_keep, w_recv)
    own_sum.advance((out2,))
    layer_out, gm, g_own, g_x, stack, dwo, dwo_x, sums2, dbu_far = ffn_far(
        at, bits, length, n2, near_far, near_x_far, rest_far, bias_x, vec, out_grad, n2t, mid, out1, dn1, out2, dn2,
        ctx_own, ctx_x, out_weight, out_x, stack, after=(own_sum.keep,),
    )
    blocks = min(dp_size, 1 << BLOCK_BITS)

    def turned(rows_, first, second):
        return rows_.reshape(first, second, -1, d).swapaxes(0, 1).reshape(-1, d)

    if dp_size > blocks:
        stack = turned(stack, blocks, dp_size // blocks)
    stack = lax.psum_scatter(stack, "dp", scatter_dimension=0, tiled=True)
    n = d // 2
    gx, sums_x, qx_s, qx_k = attend_back(
        bits, length, *other, g_x, ctx_x, aug_x, cos, sin, normed_t, dwo_x
    )
    qx_r = links.swap(qx_s, 0)
    own_sum.advance((qx_k,))
    share = input_share(bits, gx, qkv_mine, qkv_far, after=(own_sum.keep,))
    qx, = fold(bits, [(qx_k, 0, 0, n), (qx_r, 0, 0, n)], n, [(0, n)], "fold_qkv_core", after=(share,))
    qx_y = links.across(qx)
    go, sums_o, qo_s, qo_k = attend_back(
        bits, length, *own, g_own, ctx_own, aug_own, cos, sin, normed_t, dwo, after=(qx,), est=12
    )
    own_sum.advance((qo_k,))
    qo_r = links.swap(qo_s, 0)
    input_grad_out, sums1 = input_grad(
        at, inputs, gm, vec, go, share, query_weight, key_weight, value_weight, after=(own_sum.keep,)
    )
    q, = fold(bits, [(qo_k, 0, 0, n), (qx_y, 0, 0, n)], n, [(0, n)], "fold_qkv_y", after=(sums1,))
    q_s, q_k = halve(bits, q, qo_r, 1)
    q_r = links.swap(q_s, 1)
    stack, q_k = lax.optimization_barrier((stack, q_k))
    stack_r = links.across(stack)
    while not own_sum.done:
        own_sum.advance((q_k,))
    size = stack.shape[0]
    parts = [(stack_r, 0, 0, size), (own_sum.keep, 0, 0, size)]
    stack, = fold(bits, parts, size, [(0, size)], "fold_stack", after=(own_sum.keep,))
    gathered = lax.all_gather(stack, "dp", axis=0, tiled=True)
    if dp_size > blocks:
        gathered = turned(gathered, dp_size // blocks, blocks)

    c = bits[0]
    halves = lambda a, b: [jnp.where(tensor == 0, a, b), jnp.where(tensor == 0, b, a)]
    mine_up, far_up = jnp.where(c == 0, dbu_mine, dbu_far), jnp.where(c == 0, dbu_far, dbu_mine)
    small = jnp.concatenate(
        [sums1[:2].reshape(-1), sums2[:4].reshape(-1)]
        + halves(
            jnp.concatenate([v.reshape(-1) for v in (sums_o, dbu)]),
            jnp.concatenate([v.reshape(-1) for v in (sums_x, mine_up, far_up)]),
        )
    )
    used = small.shape[0]
    cols = q.shape[1]
    small = jnp.pad(small, (0, 8 * cols - used)).reshape(8, cols)

    last = links.bits - 1
    parts = [q_k, q_r]
    after = (stack,)
    for bit in range(2, links.bits):
        send, keep, small = ride(bits, parts, small, bit if bit < last else None, False, after)
        after = ()
        parts = [keep, links.swap(send, bit)]
    _, q, small = ride(bits, parts, small, None, True)
    small_r = links.across(small)
    others = [0, 1]
    for bit in reversed(range(1, last)):
        q_r = links.swap(q, bit)
        after = ()
        if others:
            size = small.shape[0]
            small, = fold(bits, [(small, 0, 0, size), (small_r, 0, 0, size)], size, [(0, size)], "fold_small", after=(q,))
            small_r = links.swap(small, others.pop(0))
            after = (small,)
        if bit == 1:
            grad_down, grad_up = wide_ffn(bits, gathered, after=after)
            after = (grad_up,)
        q = links.join(q, q_r, bit, after=after)
    q_far = links.swap(q, 0)
    small = small + small_r
    for bit in others:
        small = small + links.swap(small, bit)
    grad_q, grad_k, grad_v, grad_out = wide_qkv(bits, q, q_far)

    small = small.reshape(-1)
    gain1, shift1, out_b, gain2, shift2, down_b = (small[i * d : (i + 1) * d] for i in range(6))
    side = 3 * width + ff
    mine = lax.dynamic_slice_in_dim(small, 6 * d + tensor * side, side, 0)
    qkv_bias = mine[: 3 * width].reshape(-1, 3, 128)
    return (
        layer_out, input_grad_out, gain1, shift1,
        grad_q, qkv_bias[:, 0].reshape(-1), grad_k, qkv_bias[:, 1].reshape(-1), grad_v, qkv_bias[:, 2].reshape(-1),
        grad_out, out_b, gain2, shift2, grad_up, mine[3 * width :], grad_down, down_b,
    )


def solution(mesh):
    rows = P(("dp", "tensor"), None)
    cols = P(None, "tensor")
    tens = P("tensor")
    return jax.shard_map(
        lambda *args: layer(mesh.shape["dp"], *args),
        mesh=mesh,
        in_specs=(
            rows, P("dp"), P(), P(), cols, tens, cols, tens, cols, tens, P("tensor", None), P(), P(), P(), cols, tens,
            P("tensor", None), P(), rows,
        ),
        out_specs=(
            rows, rows, P(), P(), cols, tens, cols, tens, cols, tens, P("tensor", None), P(), P(), P(), cols, tens,
            P("tensor", None), P(),
        ),
        check_vma=False,
    )
```

```python
import math

import jax
import jax.numpy as jnp
import numpy as np
from jax import lax
from jax.experimental import pallas as pl
from jax.experimental.pallas import tpu as pltpu
from jax.sharding import PartitionSpec as P

HEAD_DIM = 64
EPS = 1e-05
LOG2E = math.log2(math.e)
LN2 = math.log(2.0)
F32 = jnp.float32
BF = jnp.bfloat16
BIG = -1e30


def dot(a, b, ca=1, cb=0):
    return lax.dot_general(a, b, (((ca,), (cb,)), ((), ())), preferred_element_type=F32)


def cost(macs, nbytes, exps=0):
    return pl.CostEstimate(flops=int(2 * macs), bytes_accessed=int(nbytes), transcendentals=int(exps))


def busy(micros):
    return pl.CostEstimate(flops=int(micros * 1.1e9), bytes_accessed=1000, transcendentals=0)


EST = {
    "move": busy(0.01),
    "heads_own": busy(16),
    "heads_other": busy(100),
    "ffn_own": busy(0.01),
    "ffn_mine": busy(100),
    "ffn_far": busy(100),
    "share": busy(8),
    "input_grad": busy(8),
    "halve": busy(20),
}


def struct(shape, dtype):
    return jax.ShapeDtypeStruct(shape, dtype)


def whole(shape):
    return pl.BlockSpec(shape, lambda *_: (0,) * len(shape), pipeline_mode=pl.Buffered(1))


def whole_out(shape):
    return pl.BlockSpec(shape, lambda *_: (0,) * len(shape))


ANY = pl.BlockSpec(memory_space=pl.ANY)


def call(kernel, after, *, in_specs, out_specs, out_shape, estimate, name, grid=(1,), prefetch=0, scratch=(), alias=None, mib=28):
    after = tuple(after)
    n_in = prefetch + len(in_specs)

    def body(*refs):
        kernel(*refs[:n_in], *refs[n_in + len(after) :])

    run = pl.pallas_call(
        body,
        grid_spec=pltpu.PrefetchScalarGridSpec(
            num_scalar_prefetch=prefetch,
            grid=grid,
            in_specs=list(in_specs) + [ANY] * len(after),
            out_specs=out_specs,
            scratch_shapes=list(scratch),
        ),
        out_shape=out_shape,
        compiler_params=pltpu.CompilerParams(vmem_limit_bytes=mib << 20),
        input_output_aliases=alias or {},
        cost_estimate=estimate,
        name=name,
    )
    return lambda *args: run(*args, *after)


def norm_rows(v):
    mean = jnp.mean(v, axis=1, keepdims=True)
    cent = v - mean
    var = jnp.mean(cent * cent, axis=1, keepdims=True)
    r = lax.rsqrt(var + EPS)
    return cent * r, r


def norm_back(e, n, r):
    return r * (e - jnp.mean(e, axis=1, keepdims=True) - n * jnp.mean(e * n, axis=1, keepdims=True))


def rotary_tables(rows):
    half = HEAD_DIM // 2
    freq = (10000.0 ** (-2.0 * np.arange(half, dtype=np.float32) / HEAD_DIM)).astype(np.float32)
    ang = (np.arange(rows, dtype=np.float32)[:, None] * freq[None, :]).astype(np.float64)
    cos = np.cos(ang).astype(np.float32)
    sin = np.sin(ang).astype(np.float32)
    return np.concatenate([cos] * 4, 1), np.concatenate([-sin, sin] * 2, 1)


def swap_halves(v):
    lane = lax.broadcasted_iota(jnp.int32, v.shape, 1)
    return jnp.where((lane & 32) == 0, pltpu.roll(v, 96, 1), pltpu.roll(v, 32, 1))


def rotate(v, cos, sin):
    return v * cos + swap_halves(v) * sin


def rotate_back(v, cos, sin):
    return v * cos - swap_halves(v) * sin


class Row:
    def __init__(self, d, width, ff):
        at = 0
        for name, size in (
            ("gain1", d), ("shift1", d), ("out_bias", d), ("gain2", d), ("shift2", d), ("down_bias", d),
            ("qkv", 3 * width), ("up", ff),
        ):
            setattr(self, name, slice(at, at + size))
            at += size


def pull(src, dst, sem):
    copy = pltpu.make_async_copy(src, dst, sem)
    copy.start()
    return copy


def arrange(bits, arrays, shapes, moves, name, after=(), mib=28):
    def kernel(bits_ref, *refs):
        ins, outs, sem = refs[: len(arrays)], refs[len(arrays) : -1], refs[-1]
        copies = [pull(src, dst, sem.at[i]) for i, (src, dst) in enumerate(moves(bits_ref, ins, outs))]
        for copy in copies:
            copy.wait()

    return call(
        kernel,
        after,
        prefetch=1,
        in_specs=[ANY] * len(arrays),
        out_specs=[whole_out(shape) for shape in shapes],
        out_shape=[struct(shape, BF) for shape in shapes],
        scratch=[pltpu.SemaphoreType.DMA((8,))],
        estimate=EST["move"],
        name=name,
        mib=mib,
    )(bits, *arrays)


def block(bit, size):
    return pl.ds(pl.multiple_of(bit * size, size), size)


def fold(bits, parts, rows, outs, name, after=(), width=None):
    arrays = [p[0] for p in parts]
    width = width or arrays[0].shape[1]
    dtype = arrays[0].dtype
    half = rows // 2
    shapes = [(half, width)] * 2 if isinstance(outs, int) else [(n, width) for _, n in outs]

    def kernel(bits_ref, *refs):
        ins, outs_r, acc = refs[: len(parts)], refs[len(parts) : -1], refs[-1]
        seen = []
        for ref, (_, src, dst, n) in zip(ins, parts):
            value = ref[src : src + n, 0:width].astype(F32)
            fresh = not any(dst < b and a < dst + n for a, b in seen)
            acc[dst : dst + n, :] = value if fresh else acc[dst : dst + n, :] + value
            seen.append((dst, dst + n))
        if isinstance(outs, int):
            bit = bits_ref[outs]
            for ref, at in zip(outs_r, (1 - bit, bit)):
                ref[...] = acc[pl.ds(pl.multiple_of(at * half, 8 if half % 8 == 0 else 1), half), :].astype(dtype)
        else:
            for ref, (start, n) in zip(outs_r, outs):
                ref[...] = acc[start : start + n, :].astype(dtype)

    return call(
        kernel,
        after,
        prefetch=1,
        in_specs=[whole(a.shape) for a in arrays],
        out_specs=[whole_out(shape) for shape in shapes],
        out_shape=[struct(shape, dtype) for shape in shapes],
        scratch=[pltpu.VMEM((rows, width), F32)],
        estimate=EST["move"],
        name=name,
    )(bits, *arrays)


def put_qkv(pre, cos, sin, q_ref, k_ref, v_ref):
    width = q_ref.shape[1]
    for i in range(width // 128):
        sl = slice(i * 128, (i + 1) * 128)
        q_ref[:, sl] = (rotate(pre[0][:, sl], cos, sin) * (LOG2E / 8.0)).astype(BF)
        k_ref[:, sl] = rotate(pre[1][:, sl], cos, sin).astype(BF)
        v_ref[:, sl] = pre[2][:, sl].astype(BF)


def split3(v):
    hi = v.astype(BF)
    rest = v - hi.astype(F32)
    mid = rest.astype(BF)
    lo = rest - mid.astype(F32)
    return hi.astype(F32), mid.astype(F32), lo


def spread(lane, first, one, two):
    out = jnp.where(lane == 0, first, 0.0)
    for at, part in enumerate((*split3(one), *split3(two))):
        out = jnp.where(lane == at + 1, part, out)
    return out.astype(BF)


def attend_pair(length, q_ref, k_ref, v_ref, ctx_ref, aug_ref):
    bq = 256
    rows = q_ref.shape[0]
    lane1 = lax.broadcasted_iota(jnp.int32, (1, 128), 1)
    krow = lax.broadcasted_iota(jnp.int32, (rows, 128), 0)
    klane = lax.broadcasted_iota(jnp.int32, (rows, 128), 1)
    lane = lax.broadcasted_iota(jnp.int32, (bq, 128), 1)
    qrow = lax.broadcasted_iota(jnp.int32, (bq, 128), 0)
    kaug = jnp.where((klane == 0) & (krow >= length), BIG, 0.0).astype(BF)
    k = jnp.concatenate([k_ref[...], kaug], 1)
    v = jnp.concatenate([v_ref[...], jnp.ones((rows, 128), BF)], 1)
    qaug = jnp.where(lane == 0, 1.0, 0.0).astype(BF)
    for i in range(rows // bq):
        sl = slice(i * bq, (i + 1) * bq)
        q = q_ref[sl, :]
        outs, totals = [], []
        for h in range(2):
            keep = ((lane1 < 64) if h == 0 else (lane1 >= 64)).astype(BF)
            s = dot(jnp.concatenate([q * keep, qaug], 1), k, 1, 1)
            top = jnp.max(s, axis=1, keepdims=True)
            p = jnp.exp2(s - top).astype(BF)
            o = dot(p, v)
            total = o[:, 128:]
            outs.append(o[:, :128] / total)
            totals.append(top + jnp.log2(total))
        ctx = jnp.where(lane < 64, outs[0], outs[1])
        ctx_ref[sl, :] = jnp.where(qrow + i * bq < length, ctx, 0.0).astype(BF)
        aug_ref[sl, :] = spread(lane, 1.0, totals[0], totals[1])


def attend_all(length, q, k, v, ctx, aug):
    @pl.loop(0, q.shape[1] // 128)
    def _(p):
        sl = pl.ds(pl.multiple_of(p * 128, 128), 128)
        attend_pair(length, *(ref.at[:, sl] for ref in (q, k, v, ctx, aug)))


def heads_own_kernel(
    at, cut, bits_ref, len_ref, x_ref, vec_ref, wq_ref, wk_ref, wv_ref, cos_ref, sin_ref, wu_h, wd_h,
    n_h, nt_h, q_h, k_h, v_h, ctx_h, aug_h, near_h, rest_h,
    n_s, nt_s, q_s, k_s, v_s, ctx_s, aug_s, near_s, rest_s, sem,
):
    rows = x_ref.shape[0]
    width = q_s.shape[1]
    loads = [
        pull(src, dst, sem.at[i]) for i, (src, dst) in enumerate(cut(bits_ref, (wu_h, wd_h), (near_s, rest_s)))
    ]
    blk = 256
    bias = vec_ref[:, at.qkv]
    for i in range(rows // blk):
        sl = slice(i * blk, (i + 1) * blk)
        n, _ = norm_rows(x_ref[sl, :].astype(F32))
        low = (n * vec_ref[:, at.gain1] + vec_ref[:, at.shift1]).astype(BF)
        n_s[sl, :] = low
        nt_s[:, sl] = low.T
        pre = [
            dot(low, w[...]) + bias[:, j * width : (j + 1) * width] for j, w in enumerate((wq_ref, wk_ref, wv_ref))
        ]
        put_qkv(pre, cos_ref[sl, :], sin_ref[sl, :], *(ref.at[sl, :] for ref in (q_s, k_s, v_s)))
    for load in loads:
        load.wait()
    pairs = [
        (near_s, near_h), (rest_s, rest_h), (n_s, n_h), (nt_s, nt_h), (q_s, q_h), (k_s, k_h), (v_s, v_h)
    ]
    stores = [pull(src, dst, sem.at[8 + i]) for i, (src, dst) in enumerate(pairs)]
    attend_all(len_ref[0], q_s, k_s, v_s, ctx_s, aug_s)
    stores += [pull(ctx_s, ctx_h, sem.at[15]), pull(aug_s, aug_h, sem.at[16])]
    for store in stores:
        store.wait()


def heads_own(at, cut, shapes, bits, length, x, vec, wq, wk, wv, cos, sin, wu, wd, after=()):
    rows, d = x.shape
    width = wq.shape[1]
    outs = [(rows, d), (d, rows)] + [(rows, width)] * 5 + list(shapes)
    return call(
        lambda *refs: heads_own_kernel(at, cut, *refs),
        after,
        prefetch=2,
        in_specs=[whole(a.shape) for a in (x, vec, wq, wk, wv, cos, sin)] + [ANY] * 2,
        out_specs=[ANY] * len(outs),
        out_shape=[struct(shape, BF) for shape in outs],
        scratch=[pltpu.VMEM(shape, BF) for shape in outs] + [pltpu.SemaphoreType.DMA((17,))],
        estimate=EST["heads_own"],
        name="heads_own",
        mib=56,
    )(bits, length, x, vec, wq, wk, wv, cos, sin, wu, wd)


def heads_other_kernel(
    at, bits_ref, len_ref, n_ref, wm_ref, wf_ref, b_ref, cos_ref, sin_ref, q_h, k_h, v_h, ctx_h, aug_h,
    q_s, k_s, v_s, ctx_s, aug_s, sem,
):
    rows = n_ref.shape[0]
    width = q_s.shape[1]
    half = wm_ref.shape[0]
    c = bits_ref[0]
    blk = 256
    for i in range(rows // blk):
        sl = slice(i * blk, (i + 1) * blk)
        pre = dot(n_ref[sl, block(c, half)], wm_ref[...]) + dot(n_ref[sl, block(1 - c, half)], wf_ref[...])
        pre = pre + b_ref[:, at.qkv]
        put_qkv(
            [pre[:, j * width : (j + 1) * width] for j in range(3)], cos_ref[sl, :], sin_ref[sl, :],
            *(ref.at[sl, :] for ref in (q_s, k_s, v_s)),
        )
    stores = [pull(src, dst, sem.at[i]) for i, (src, dst) in enumerate(((q_s, q_h), (k_s, k_h), (v_s, v_h)))]
    attend_all(len_ref[0], q_s, k_s, v_s, ctx_s, aug_s)
    stores += [pull(ctx_s, ctx_h, sem.at[3]), pull(aug_s, aug_h, sem.at[4])]
    for store in stores:
        store.wait()


def heads_other(at, bits, length, n, w_mine, w_far, bias, cos, sin, after=()):
    rows = n.shape[0]
    width = w_mine.shape[1] // 3
    outs = [(rows, width)] * 5
    return call(
        lambda *refs: heads_other_kernel(at, *refs),
        after,
        prefetch=2,
        in_specs=[whole(a.shape) for a in (n, w_mine, w_far, bias, cos, sin)],
        out_specs=[ANY] * 5,
        out_shape=[struct(shape, BF) for shape in outs],
        scratch=[pltpu.VMEM(shape, BF) for shape in outs] + [pltpu.SemaphoreType.DMA((5,))],
        estimate=EST["heads_other"],
        name="heads_other",
        mib=56,
    )(bits, length, n, w_mine, w_far, bias, cos, sin)


def attend_back_kernel(
    bq, bits_ref, len_ref, q_ref, k_ref, v_ref, g_ref, ctx_ref, aug_ref, cos_ref, sin_ref, nt_ref, wo_ref,
    d_ref, sum_ref, send_ref, keep_ref, dqt, dall,
):
    rows = q_ref.shape[0]
    length = len_ref[0]
    lane1 = lax.broadcasted_iota(jnp.int32, (1, 128), 1)
    krow = lax.broadcasted_iota(jnp.int32, (rows, 128), 0)
    klane = lax.broadcasted_iota(jnp.int32, (rows, 128), 1)
    lane = lax.broadcasted_iota(jnp.int32, (bq, 128), 1)
    k = k_ref[...]
    v = v_ref[...]
    kt = k.T
    dks, dvs = [], []
    for h in range(2):
        keep = ((lane1 < 64) if h == 0 else (lane1 >= 64)).astype(BF)
        first = 1 + 3 * h
        mine = jnp.where((klane >= first) & (klane < first + 3), -1.0, 0.0)
        kaug = jnp.where((klane == 0) & (krow >= length), BIG, mine).astype(BF)
        kh = jnp.concatenate([k * keep, kaug], 1)
        vh = jnp.concatenate([v * keep, mine.astype(BF)], 1)
        dk = jnp.zeros((rows, 128), F32)
        dv = jnp.zeros((rows, 128), F32)
        for i in range(rows // bq):
            sl = slice(i * bq, (i + 1) * bq)
            q = q_ref[sl, :]
            g = g_ref[sl, :]
            prod = g.astype(F32) * ctx_ref[sl, :].astype(F32)
            d0 = jnp.sum(jnp.where(lane < 64, prod, 0.0), 1, keepdims=True)
            d1 = jnp.sum(jnp.where(lane < 64, 0.0, prod), 1, keepdims=True)
            gaug = spread(lane, 0.0, d0, d1)
            st = dot(kh, jnp.concatenate([q, aug_ref[sl, :]], 1), 1, 1)
            pt = jnp.exp2(st)
            dpt = dot(vh, jnp.concatenate([g, gaug], 1), 1, 1)
            ds = (pt * dpt).astype(BF)
            dv = dv + dot(pt.astype(BF), g)
            dk = dk + dot(ds, q)
            dqt[h * 64 : (h + 1) * 64, sl] = dot(kt[h * 64 : (h + 1) * 64, :], ds)
        dks.append(dk)
        dvs.append(dv)
    cos = cos_ref[...]
    sin = sin_ref[...]
    dq = rotate_back(dqt[...].T * (1.0 / 8.0), cos, sin).astype(BF)
    dk = rotate_back(jnp.where(klane < 64, dks[0], dks[1]) * LN2, cos, sin).astype(BF)
    dv = jnp.where(klane < 64, dvs[0], dvs[1]).astype(BF)
    for at, val in enumerate((dq, dk, dv)):
        sl = slice(at * 128, (at + 1) * 128)
        d_ref[:, sl] = val
        sum_ref[:, sl] = jnp.sum(val.astype(F32), axis=0, keepdims=True)
    j = pl.program_id(0)
    dall[:, block(j, 384)] = jnp.concatenate([dq, dk, dv], 1)

    @pl.when(j == pl.num_programs(0) - 1)
    def _():
        half = send_ref.shape[0]
        c = bits_ref[0]
        for ref, part in ((send_ref, 1 - c), (keep_ref, c)):
            width = dall.shape[1]
            ref[:, 0:width] = dot(nt_ref[block(part, half), :], dall[...]).astype(BF)
            ref[:, width:] = wo_ref[block(part, half), :]


def attend_back(bits, length, q, k, v, g, ctx, aug, cos, sin, nt, wo, after=(), est=100):
    rows, width = q.shape
    d = 2 * width
    bs = pl.BlockSpec((rows, 128), lambda j, *_: (0, j))
    return call(
        lambda *refs: attend_back_kernel(256, *refs),
        after,
        prefetch=2,
        grid=(width // 128,),
        in_specs=[bs] * 6 + [whole((rows, 128))] * 2 + [whole(nt.shape), whole(wo.shape)],
        out_specs=[pl.BlockSpec((rows, 384), lambda j, *_: (0, j)), pl.BlockSpec((1, 384), lambda j, *_: (0, j))]
        + [whole_out((d // 2, 4 * width))] * 2,
        out_shape=[struct((rows, 3 * width), BF), struct((1, 3 * width), F32)] + [struct((d // 2, 4 * width), BF)] * 2,
        scratch=[pltpu.VMEM((128, rows), F32), pltpu.VMEM((rows, 3 * width), BF)],
        estimate=busy(est),
        name="attend_back",
        mib=56,
    )(bits, length, q, k, v, g, ctx, aug, cos, sin, nt, wo)


def gelu_pair(h):
    z = jnp.abs(h) * (0.3275911 / math.sqrt(2.0)) + 1.0
    t = pl.reciprocal(z, approx=True)
    t = t * (2.0 - z * t)
    e = jnp.exp2(h * h * (-0.5 * LOG2E))
    poly = 0.5 * 1.061405429 * t - 0.5 * 1.453152027
    poly = poly * t + 0.5 * 1.421413741
    poly = poly * t - 0.5 * 0.284496736
    poly = poly * t + 0.5 * 0.254829592
    w = poly * t * e
    cdf = jnp.where(h >= 0.0, 1.0 - w, w)
    return h * cdf, cdf + h * e * (1.0 / math.sqrt(2.0 * math.pi))


def ffn_quarter(n2, n2t, og, wu, wd, bias, out_acc, dn_acc, act_s, dh_s, gd, gu, first, before=None, done=None):
    rows, d = og.shape
    part = wd.shape[0]
    blk = 256
    dbias = jnp.zeros((1, part), F32)
    if before is not None:
        before(0, blk)
    for i in range(rows // blk):
        sl = slice(i * blk, (i + 1) * blk)
        if before is not None and i + 1 < rows // blk:
            before(i + 1, blk)
        h = dot(n2[sl, :], wu[...]) + bias
        act, slope = gelu_pair(h)
        act = act.astype(BF)
        dh = (slope * dot(og[sl, :], wd[...], 1, 1)).astype(BF)
        act_s[sl, :] = act
        dh_s[sl, :] = dh
        dbias = dbias + jnp.sum(dh.astype(F32), axis=0, keepdims=True)
        o = dot(act, wd[...])
        e = dot(dh, wu[...], 1, 1)
        out_acc[sl, :] = o if first else out_acc[sl, :] + o
        dn_acc[sl, :] = e if first else dn_acc[sl, :] + e
        if done is not None and i > 0:
            done(i - 1, blk)
    if done is not None:
        done(rows // blk - 1, blk)
    gd[...] = dot(act_s[...], og[...], 0, 0).astype(BF)
    gu[...] = dot(n2t[...], dh_s[...]).astype(BF)
    return dbias


def ffn_own_kernel(
    at, bits_ref, x_ref, co_ref, cx_ref, woo_ref, wox, vec_ref, og_h, wu_h, wd_h,
    mid_h, n2_h, n2t_h, out_h, dn_h, send_h, keep_h, db_ref,
    og, wu, wd, mid, n2, n2t, out, dn, outb, dnb, act_s, dh_s, gd, gu, sem,
):
    rows, d = x_ref.shape
    part = wu_h.shape[1] // 2
    c = bits_ref[0]
    cols = [block(p, part) for p in (1 - c, c)]
    biases = [pl.ds(pl.multiple_of(at.up.start + p * part, 128), part) for p in (1 - c, c)]
    loads = [pull(og_h, og, sem.at[0])]
    for q in range(2):
        loads.append(pull(wu_h.at[:, cols[q]], wu.at[q], sem.at[1 + 2 * q]))
        loads.append(pull(wd_h.at[cols[q], :], wd.at[q], sem.at[2 + 2 * q]))
    stores = []

    def enter(i, blk):
        sl = slice(i * blk, (i + 1) * blk)
        att = dot(co_ref[sl, :], woo_ref[...]) + dot(cx_ref[sl, :], wox[...])
        v = x_ref[sl, :].astype(F32) + att + vec_ref[:, at.out_bias]
        mid[sl, :] = v
        n, _ = norm_rows(v)
        low = (n * vec_ref[:, at.gain2] + vec_ref[:, at.shift2]).astype(BF)
        n2[sl, :] = low
        n2t[:, sl] = low.T
        if i == 0:
            for load in loads:
                load.wait()
        if (i + 1) * blk == rows:
            stores.extend([pull(mid, mid_h, sem.at[5]), pull(n2, n2_h, sem.at[6]), pull(n2t, n2t_h, sem.at[7])])

    def flush(i, blk):
        sl = pl.ds(i * blk, blk)
        outb[sl, :] = out[sl, :].astype(BF)
        dnb[sl, :] = dn[sl, :].astype(BF)
        stores.append(pull(outb.at[sl, :], out_h.at[sl, :], sem.at[8 + i]))
        stores.append(pull(dnb.at[sl, :], dn_h.at[sl, :], sem.at[12 + i]))

    for q in range(2):
        db_ref[:, cols[q]] = ffn_quarter(
            n2, n2t, og, wu.at[q], wd.at[q], vec_ref[:, biases[q]], out, dn, act_s, dh_s, gd.at[q], gu.at[q], q == 0,
            enter if q == 0 else None, flush if q == 1 else None,
        )
        stores.append(pull(gd.at[q], (send_h, keep_h)[q].at[0:part, :], sem.at[16 + q]))
        stores.append(pull(gu.at[q], (send_h, keep_h)[q].at[part:, :], sem.at[20 + q]))
    for store in stores:
        store.wait()


def ffn_own(at, bits, x, ctx_own, ctx_other, wo_own, wo_other, vec, og, wu, wd, after=()):
    rows, d = x.shape
    ff = wu.shape[1]
    part = ff // 2
    half = ctx_own.shape[1]
    return call(
        lambda *refs: ffn_own_kernel(at, *refs),
        after,
        prefetch=1,
        in_specs=[
            whole((rows, d)), whole((rows, half)), whole((rows, half)), whole((half, d)), whole((half, d)), whole(vec.shape),
        ] + [ANY] * 3,
        out_specs=[ANY] * 7 + [whole_out((1, ff))],
        scratch=[
            pltpu.VMEM((rows, d), BF), pltpu.VMEM((2, d, part), BF), pltpu.VMEM((2, part, d), BF),
            pltpu.VMEM((rows, d), F32), pltpu.VMEM((rows, d), BF), pltpu.VMEM((d, rows), BF),
            pltpu.VMEM((rows, d), F32), pltpu.VMEM((rows, d), F32), pltpu.VMEM((rows, d), BF), pltpu.VMEM((rows, d), BF),
            pltpu.VMEM((rows, part), BF), pltpu.VMEM((rows, part), BF),
            pltpu.VMEM((2, part, d), BF), pltpu.VMEM((2, d, part), BF),
            pltpu.SemaphoreType.DMA((22,)),
        ],
        out_shape=[
            struct((rows, d), F32), struct((rows, d), BF), struct((d, rows), BF), struct((rows, d), BF),
            struct((rows, d), BF), struct((part + d, d), BF), struct((part + d, d), BF),
            struct((1, ff), F32),
        ],
        estimate=EST["ffn_own"],
        name="ffn_own",
        mib=56,
    )(bits, x, ctx_own, ctx_other, wo_own, wo_other, vec, og, wu, wd)


BLOCK_BITS = 4


def sub_block(s, q, x, n):
    out = q + 2 * x
    for k in range(2, n):
        out = out + (((s >> (n - 1 - k)) & 1) << k)
    return out


def put_blocks(grads, stack, q, n, sem, at):
    count = 1 << (n - 2)
    size = grads[0].shape[0] // count
    return [
        pull(
            grads[x].at[s * size : (s + 1) * size, :],
            stack.at[pl.ds(pl.multiple_of(sub_block(s, q, x, n) * size, size), size), :],
            sem.at[at + x * count + s],
        )
        for x in range(2)
        for s in range(count)
    ]


def gather_weights(bits_ref, near, near_x, rest, w, sem, at):
    rows = near.shape[0]
    b = bits_ref[1]
    return [
        pull(near, w.at[block(b, rows), :], sem.at[at]),
        pull(near_x, w.at[block(1 - b, rows), :], sem.at[at + 1]),
        pull(rest, w.at[2 * rows :, :], sem.at[at + 2]),
    ]


def ffn_mine_kernel(
    n, bits_ref, n2_ref, b_ref, near_h, near_x_h, rest_h, og_h, n2t_h, out_h, dn_h, stack_h, db_ref,
    w_ref, og, n2t, out, dn, outb, dnb, act_s, dh_s, gd, gu, sem,
):
    d = og.shape[1]
    part = w_ref.shape[0] - d
    c = bits_ref[0]
    bias_at = b_ref.shape[1] - 2 * part
    at = 10 + (1 << (n - 1))
    loads = gather_weights(bits_ref, near_h, near_x_h, rest_h, w_ref, sem, at)
    loads += [pull(og_h, og, sem.at[0]), pull(n2t_h, n2t, sem.at[1])]
    for load in loads:
        load.wait()
    stores = []

    def flush(i, blk):
        sl = pl.ds(i * blk, blk)
        outb[sl, :] = out[sl, :].astype(BF)
        dnb[sl, :] = dn[sl, :].astype(BF)
        stores.append(pull(outb.at[sl, :], out_h.at[sl, :], sem.at[2 + i]))
        stores.append(pull(dnb.at[sl, :], dn_h.at[sl, :], sem.at[6 + i]))

    bias = b_ref[:, pl.ds(pl.multiple_of(bias_at + c * part, 128), part)]
    db_ref[...] = ffn_quarter(
        n2_ref, n2t, og, w_ref.at[0:d, :], w_ref.at[d:, :], bias, out, dn, act_s, dh_s, gd, gu, True, None, flush
    )
    stores += put_blocks((gd, gu), stack_h, c, n, sem, 10)
    for store in stores:
        store.wait()


def ffn_mine(bits, n2, near, near_x, rest, bias, og, n2t, after=()):
    rows, d = og.shape
    part = 2 * near.shape[0] + rest.shape[0] - d
    n = min(bits.shape[0], BLOCK_BITS)
    return call(
        lambda *refs: ffn_mine_kernel(n, *refs),
        after,
        prefetch=1,
        in_specs=[whole((rows, d)), whole(bias.shape)] + [ANY] * 5,
        out_specs=[ANY] * 3 + [whole_out((1, part))],
        scratch=[
            pltpu.VMEM((d + part, d), BF),
            pltpu.VMEM((rows, d), BF), pltpu.VMEM((d, rows), BF), pltpu.VMEM((rows, d), F32), pltpu.VMEM((rows, d), F32),
            pltpu.VMEM((rows, d), BF), pltpu.VMEM((rows, d), BF),
            pltpu.VMEM((rows, part), BF), pltpu.VMEM((rows, part), BF), pltpu.VMEM((part, d), BF), pltpu.VMEM((d, part), BF),
            pltpu.SemaphoreType.DMA((13 + (1 << (n - 1)),)),
        ],
        out_shape=[
            struct((rows, d), BF), struct((rows, d), BF), struct((4 * part, d), BF), struct((1, part), F32),
        ],
        estimate=EST["ffn_mine"],
        name="ffn_mine",
        mib=56,
    )(bits, n2, bias, near, near_x, rest, og, n2t)


def ffn_far_kernel(
    at, n, bits_ref, len_ref, n2_ref, b_ref, vec_ref, near_h, near_x_h, rest_h, og_h, n2t_h, mid_h, out1_h, dn1_h, out2_h, dn2_h,
    co_h, cx_h, woo_h, wox_h, stack_in,
    lay_h, gm_h, dco_h, dcx_h, stack_h, dwoo_h, dwox_h, sums_ref, db_ref,
    w_ref, og, n2t, mid, out1, dn1, out2, dn2, co, cx, woo, wox, out, dn, act_s, dh_s, gd, gu, lay, gmb, dco, dcx, dwoo, dwox, sem,
):
    rows, d = og.shape
    part = w_ref.shape[0] - d
    half = co.shape[1]
    c = bits_ref[0]
    length = len_ref[0]
    bias_at = b_ref.shape[1] - 2 * part
    first = gather_weights(bits_ref, near_h, near_x_h, rest_h, w_ref, sem, 18 + (1 << (n - 1)))
    loads = [
        pull(src, dst, sem.at[i])
        for i, (src, dst) in enumerate((
            (og_h, og), (n2t_h, n2t), (mid_h, mid), (dn1_h, dn1), (dn2_h, dn2), (out1_h, out1), (out2_h, out2),
            (woo_h, woo), (wox_h, wox), (co_h, co), (cx_h, cx),
        ))
    ]
    for load in first + loads[:1]:
        load.wait()
    sums_ref[...] = jnp.zeros_like(sums_ref)
    stores = []

    def finish(i, blk):
        if i == 0:
            for load in loads[1:]:
                load.wait()
        sl = slice(i * blk, (i + 1) * blk)
        v = mid[sl, :]
        out_sum = out1[sl, :].astype(F32) + out2[sl, :].astype(F32) + out[sl, :]
        lay[sl, :] = (v + out_sum + vec_ref[:, at.down_bias]).astype(BF)
        unit, r = norm_rows(v)
        gn = dn1[sl, :].astype(F32) + dn2[sl, :].astype(F32) + dn[sl, :]
        o = og[sl, :].astype(F32)
        g = o + norm_back(gn * vec_ref[:, at.gain2], unit, r)
        mid[sl, :] = g
        low = g.astype(BF)
        gmb[sl, :] = low
        for k, val in enumerate((g, gn * unit, gn, o)):
            sums_ref[k : k + 1, :] += jnp.sum(val, axis=0, keepdims=True)
        valid = lax.broadcasted_iota(jnp.int32, (blk, 1), 0) + i * blk < length
        dco[sl, :] = jnp.where(valid, dot(low, woo[...], 1, 1), 0.0).astype(BF)
        dcx[sl, :] = jnp.where(valid, dot(low, wox[...], 1, 1), 0.0).astype(BF)

    bias = b_ref[:, pl.ds(pl.multiple_of(bias_at + (1 - c) * part, 128), part)]
    db_ref[...] = ffn_quarter(
        n2_ref, n2t, og, w_ref.at[0:d, :], w_ref.at[d:, :], bias, out, dn, act_s, dh_s, gd, gu, True, None, finish
    )
    stores = put_blocks((gd, gu), stack_h, 1 - c, n, sem, 18)
    stores += [
        pull(src, dst, sem.at[12 + k])
        for k, (src, dst) in enumerate(((lay, lay_h), (mid, gm_h), (dco, dco_h), (dcx, dcx_h)))
    ]
    dwoo[...] = dot(gmb[...], co[...], 0, 0).astype(BF)
    dwox[...] = dot(gmb[...], cx[...], 0, 0).astype(BF)
    stores += [pull(dwoo, dwoo_h, sem.at[16]), pull(dwox, dwox_h, sem.at[17])]
    for store in stores:
        store.wait()


def ffn_far(
    at, bits, length, n2, near, near_x, rest, bias, vec, og, n2t, mid, out1, dn1, out2, dn2, ctx_own, ctx_other, wo_own,
    wo_other, stack, after=(),
):
    rows, d = og.shape
    part = 2 * near.shape[0] + rest.shape[0] - d
    n = min(bits.shape[0], BLOCK_BITS)
    half = ctx_own.shape[1]
    bf = lambda *shape: pltpu.VMEM(shape, BF)
    f32 = lambda *shape: pltpu.VMEM(shape, F32)
    return call(
        lambda *refs: ffn_far_kernel(at, n, *refs),
        after,
        prefetch=2,
        in_specs=[whole((rows, d)), whole(bias.shape), whole(vec.shape)] + [ANY] * 15,
        out_specs=[ANY] * 7 + [whole_out((8, d)), whole_out((1, part))],
        scratch=[
            bf(d + part, d), bf(rows, d), bf(d, rows), f32(rows, d), bf(rows, d), bf(rows, d), bf(rows, d), bf(rows, d),
            bf(rows, half), bf(rows, half), bf(half, d), bf(half, d), f32(rows, d), f32(rows, d),
            bf(rows, part), bf(rows, part), bf(part, d), bf(d, part), bf(rows, d), bf(rows, d), bf(rows, half),
            bf(rows, half), bf(d, half), bf(d, half), pltpu.SemaphoreType.DMA((21 + (1 << (n - 1)),)),
        ],
        out_shape=[
            struct((rows, d), BF), struct((rows, d), F32), struct((rows, half), BF), struct((rows, half), BF),
            struct(stack.shape, BF), struct((d, half), BF), struct((d, half), BF), struct((8, d), F32), struct((1, part), F32),
        ],
        alias={19: 4},
        estimate=EST["ffn_far"],
        name="ffn_far",
        mib=56,
    )(
        bits, length, n2, bias, vec, near, near_x, rest, og, n2t, mid, out1, dn1, out2, dn2, ctx_own, ctx_other, wo_own,
        wo_other, stack,
    )


def by_pairs(wcat, matrices, rows, width):
    for p in range(width // 128):
        for i in range(3):
            to = slice((3 * p + i) * 128, (3 * p + i + 1) * 128)
            ref, base = matrices[i]
            wcat[rows, to] = ref[:, base + p * 128 : base + (p + 1) * 128]


def share_kernel(bits_ref, g_ref, wm, wf, out_ref, wcat):
    width = g_ref.shape[1] // 3
    c = bits_ref[0]
    half = wm.shape[0]

    @pl.when(pl.program_id(0) == 0)
    def _():
        for ref, part in ((wm, c), (wf, 1 - c)):
            by_pairs(wcat, [(ref, i * width) for i in range(3)], block(part, half), width)

    out_ref[...] = dot(g_ref[...], wcat[...], 1, 1).astype(BF)


def input_share(bits, g, w_mine, w_far, after=()):
    rows, cols = g.shape
    d = 2 * w_mine.shape[0]
    blk = 512
    row = lambda w: pl.BlockSpec((blk, w), lambda i, *_: (i, 0))
    return call(
        share_kernel, after, prefetch=1, grid=(rows // blk,),
        in_specs=[row(cols), whole(w_mine.shape), whole(w_far.shape)], out_specs=row(d),
        out_shape=struct((rows, d), BF), scratch=[pltpu.VMEM((d, cols), BF)],
        estimate=EST["share"], name="input_share", mib=56,
    )(bits, g, w_mine, w_far)


def input_grad_kernel(at, x_ref, gm_ref, vec_ref, g_ref, share_ref, wq, wk, wv, out_ref, sums_ref, wcat):
    width = wq.shape[1]

    @pl.when(pl.program_id(0) == 0)
    def _():
        sums_ref[...] = jnp.zeros_like(sums_ref)
        by_pairs(wcat, [(ref, 0) for ref in (wq, wk, wv)], slice(None), width)

    gn = dot(g_ref[...], wcat[...], 1, 1) + share_ref[...].astype(F32)
    n, r = norm_rows(x_ref[...].astype(F32))
    out_ref[...] = (gm_ref[...] + norm_back(gn * vec_ref[:, at.gain1], n, r)).astype(BF)
    sums_ref[0:1, :] += jnp.sum(gn * n, axis=0, keepdims=True)
    sums_ref[1:2, :] += jnp.sum(gn, axis=0, keepdims=True)


def input_grad(at, x, gm, vec, g, share, wq, wk, wv, after=()):
    rows, d = x.shape
    width = wq.shape[1]
    blk = 256
    row = lambda w: pl.BlockSpec((blk, w), lambda i, *_: (i, 0))
    return call(
        lambda *refs: input_grad_kernel(at, *refs),
        after,
        grid=(rows // blk,),
        in_specs=[row(d), row(d), whole(vec.shape), row(3 * width), row(d)] + [whole((d, width))] * 3,
        out_specs=[row(d), whole_out((8, d))],
        out_shape=[struct((rows, d), BF), struct((8, d), F32)],
        scratch=[pltpu.VMEM((d, 3 * width), BF)],
        estimate=EST["input_grad"],
        name="input_grad",
        mib=56,
    )(x, gm, vec, g, share, wq, wk, wv)


def wide_qkv(bits, near, far, after=()):
    size, width = near[0].shape
    width //= 4

    def kernel(bits_ref, *refs):
        ins, outs, turn = refs[:4], refs[4:8], refs[8]
        base = (pl.program_id(0) != bits_ref[0]).astype(jnp.int32) * 2
        for half in range(2):
            want = base + (half != bits_ref[1]).astype(jnp.int32)
            rows = slice(half * size, (half + 1) * size)
            for k in range(4):

                @pl.when(want == k)
                def _():
                    ref = ins[k]
                    for i, out in enumerate(outs[:3]):
                        for p in range(width // 128):
                            src = slice((3 * p + i) * 128, (3 * p + i + 1) * 128)
                            out[rows, p * 128 : (p + 1) * 128] = ref[:, src].astype(F32)
                    turn[rows, :] = ref[:, 3 * width :].astype(F32)

        outs[3][...] = turn[...].T

    return call(
        kernel, after, prefetch=1, grid=(2,),
        in_specs=[whole((size, 4 * width))] * 4,
        out_specs=[pl.BlockSpec((2 * size, width), lambda i, *_: (i, 0))] * 3
        + [pl.BlockSpec((width, 2 * size), lambda i, *_: (0, i))],
        out_shape=[struct((4 * size, width), F32)] * 3 + [struct((width, 4 * size), F32)],
        scratch=[pltpu.VMEM((2 * size, width), F32)], estimate=EST["move"], name="wide_qkv", mib=56,
    )(bits, *near, *far)


def wide_ffn(bits, stack, after=()):
    rows, d = stack.shape
    n = min(bits.shape[0], BLOCK_BITS)
    part = rows // 4
    count = 1 << (n - 2)
    size = part // count

    def kernel(bits_ref, *refs):
        for x in range(2):
            for k in range(2):
                refs[4 + x][k * size : (k + 1) * size, :] = refs[2 * x + k][...].astype(F32)

    def place(x, k):
        return lambda q, t, *_: (sub_block(2 * t + k, q, x, n), 0)

    return call(
        kernel, after, prefetch=1, grid=(2, count // 2),
        in_specs=[pl.BlockSpec((size, d), place(x, k)) for x in range(2) for k in range(2)],
        out_specs=[
            pl.BlockSpec((2 * size, d), lambda q, t, *_: (q * (count // 2) + t, 0)),
            pl.BlockSpec((2 * size, d), lambda q, t, *_: (t, q)),
        ],
        out_shape=[struct((2 * part, d), F32), struct((part, 2 * d), F32)],
        estimate=EST["move"], name="wide_ffn", mib=56,
    )(bits, stack, stack, stack, stack)


class Links:
    def __init__(self, dp_size):
        self.size = dp_size
        self.bits = dp_size.bit_length() - 1
        index = lax.axis_index("dp")
        self.value = jnp.stack([(index >> i) & 1 for i in range(self.bits)]).astype(jnp.int32)

    def swap(self, value, at):
        return lax.ppermute(value, "dp", [(i, i ^ (1 << at)) for i in range(self.size)])

    def across(self, value):
        return lax.ppermute(value, "tensor", [(0, 1), (1, 0)])

    def join(self, mine, other, at, after=()):
        half, width = mine.shape
        if half % 16:
            low = self.value[at] == 0
            return jnp.concatenate([jnp.where(low, mine, other), jnp.where(low, other, mine)], 0)

        def moves(bits, ins, outs):
            return [
                (ins[0], outs[0].at[block(bits[at], half), :]), (ins[1], outs[0].at[block(1 - bits[at], half), :])
            ]

        return arrange(self.value, [mine, other], [(2 * half, width)], moves, "join", after)[0]


def halve(bits, keep, recv, bit, after=()):
    keep, recv, *_ = lax.optimization_barrier((keep, recv, *after))
    size = keep.shape[0] // 2

    def half(at):
        a, b = (lax.dynamic_slice_in_dim(v, at * size, size, 0).astype(F32) for v in (keep, recv))
        return (a + b).astype(BF)

    return half(1 - bits[bit]), half(bits[bit])


class Halve:
    def __init__(self, links, keep, recv):
        self.links, self.keep, self.recv, self.at = links, keep, recv, 0
        low = min(links.bits, BLOCK_BITS)
        self.order = [*range(low), *reversed(range(low, links.bits))]
        self.done = False

    def advance(self, after):
        links, size = self.links, self.keep.shape[0]
        self.at += 1
        self.done = self.at == links.bits
        if self.done:
            parts = [(self.keep, 0, 0, size), (self.recv, 0, 0, size)]
            self.keep, = fold(links.value, parts, size, [(0, size)], "fold_own", after)
            return
        bit = self.order[self.at]
        send, self.keep = halve(links.value, self.keep, self.recv, bit, after)
        self.recv = links.swap(send, bit)


RIDE = 32


def ride_kernel(rows, cut, bits_ref, *refs):
    *ins, small_ref, send_ref, keep_ref, next_ref, acc = refs
    width = small_ref.shape[1]
    small = small_ref[...]
    total = None
    for ref in ins:
        value = ref[0:rows, :].astype(F32)
        total = value if total is None else total + value
        if ref.shape[0] > rows:
            riding = ref[rows : rows + RIDE, :].astype(F32)
            small = small + riding[0:8] + riding[8:16] + riding[16:24]
    next_ref[...] = small
    if send_ref is None:
        keep_ref[...] = total.astype(BF)
        return
    acc[...] = total
    if cut is None:
        size = rows
        send_ref[0:size, :] = total.astype(BF)
        keep_ref[...] = total.astype(BF)
    else:
        size = rows // 2
        bit = bits_ref[cut]
        low, high = acc[0:size, :], acc[size : 2 * size, :]
        send_ref[0:size, :] = jnp.where(bit == 0, high, low).astype(BF)
        keep_ref[...] = jnp.where(bit == 0, low, high).astype(BF)
    parts = [p.astype(BF) for p in split3(small)] + [jnp.zeros((RIDE - 24, width), BF)]
    send_ref[size:, :] = jnp.concatenate(parts, 0)


def ride(bits, parts, small, cut, last, after=()):
    rows = parts[0].shape[0]
    width = small.shape[1]
    size = rows // 2 if cut is not None else rows
    shapes = [struct((size, width), BF), struct(small.shape, F32)]
    if not last:
        shapes.insert(0, struct((size + RIDE, width), BF))

    def kernel(bits_ref, *refs):
        refs = list(refs)
        if last:
            refs.insert(len(parts) + 1, None)
        ride_kernel(rows, cut, bits_ref, *refs)

    out = call(
        kernel, after, prefetch=1, in_specs=[whole(a.shape) for a in (*parts, small)],
        out_specs=[whole_out(t.shape) for t in shapes], out_shape=shapes,
        scratch=[pltpu.VMEM((rows, width), F32)], estimate=EST["move"], name="ride",
    )(bits, *parts, small)
    return (None, *out) if last else out


def layer(
    dp_size, inputs, lengths, norm1_gain, norm1_shift, query_weight, query_bias, key_weight, key_bias, value_weight,
    value_bias, out_weight, out_bias, norm2_gain, norm2_shift, up_weight, up_bias, down_weight, down_bias, out_grad,
):
    rows, d = inputs.shape
    width = query_weight.shape[1]
    ff = up_weight.shape[1]
    part = ff // 2
    links = Links(dp_size)
    bits = links.value
    tensor = lax.axis_index("tensor")
    length = lax.dynamic_slice_in_dim(lengths, tensor, 1, 0)
    cos, sin = (jnp.asarray(t) for t in rotary_tables(rows))
    at = Row(d, width, ff)
    vec = jnp.concatenate(
        [norm1_gain, norm1_shift, out_bias, norm2_gain, norm2_shift, down_bias, query_bias, key_bias, value_bias, up_bias]
    ).reshape(1, -1)

    def qkv_moves(bits_ref, ins, outs):
        return [
            (w.at[block(bits_ref[0], d // 2), :], outs[0].at[:, i * width : (i + 1) * width]) for i, w in enumerate(ins)
        ]

    near_rows = 5 * d // 12
    half = width // 2
    def cut_moves(bits_ref, ins, outs):
        c, b = bits_ref[0], bits_ref[1]
        wu, wd = ins
        near, rest = outs
        cols = block(c, part)
        return [
            (wu.at[block(b, near_rows), cols], near),
            (wu.at[2 * near_rows :, cols], rest.at[0 : d - 2 * near_rows, :]),
            (wd.at[block(c, part), :], rest.at[d - 2 * near_rows :, :]),
        ]

    qkv_mine, = arrange(bits, [query_weight, key_weight, value_weight], [(d // 2, 3 * width)], qkv_moves, "cut_qkv", mib=56)
    qkv_mine = links.across(qkv_mine)
    normed, normed_t, *own, ctx_own, aug_own, near, rest = heads_own(
        at, cut_moves, [(near_rows, d), (d + part - 2 * near_rows, d)], bits, length, inputs, vec, query_weight,
        key_weight, value_weight, cos, sin, up_weight, down_weight,
    )
    bias_x = links.across(vec)
    near, out_x = links.across(near), links.across(out_weight)
    qkv_mine, _ = lax.optimization_barrier((qkv_mine, ctx_own))
    qkv_far = links.swap(qkv_mine, 0)
    *other, ctx_x, aug_x = heads_other(at, bits, length, normed, qkv_mine, qkv_far, bias_x, cos, sin, after=(ctx_own,))
    near, out_x, rest, ctx_x = lax.optimization_barrier((near, out_x, rest, ctx_x))
    rest = links.across(rest)
    near_x = links.swap(near, 1)
    near_far = links.swap(near, 0)
    mid, n2, n2t, out1, dn1, w_send, w_keep, dbu = ffn_own(
        at, bits, inputs, ctx_own, ctx_x, out_weight, out_x, vec, out_grad, up_weight, down_weight
    )

    w_recv = links.swap(w_send, 0)
    near_x_far, rest_far = links.swap(near_x, 0), links.swap(rest, 0)
    out2, dn2, stack, dbu_mine = ffn_mine(bits, n2, near, near_x, rest, bias_x, out_grad, n2t, after=(mid,))
    own_sum = Halve(links, w_keep, w_recv)
    own_sum.advance((out2,))
    layer_out, gm, g_own, g_x, stack, dwo, dwo_x, sums2, dbu_far = ffn_far(
        at, bits, length, n2, near_far, near_x_far, rest_far, bias_x, vec, out_grad, n2t, mid, out1, dn1, out2, dn2,
        ctx_own, ctx_x, out_weight, out_x, stack, after=(own_sum.keep,),
    )
    blocks = min(dp_size, 1 << BLOCK_BITS)

    def turned(rows_, first, second):
        return rows_.reshape(first, second, -1, d).swapaxes(0, 1).reshape(-1, d)

    if dp_size > blocks:
        stack = turned(stack, blocks, dp_size // blocks)
    stack = lax.psum_scatter(stack, "dp", scatter_dimension=0, tiled=True)
    n = d // 2
    gx, sums_x, qx_s, qx_k = attend_back(
        bits, length, *other, g_x, ctx_x, aug_x, cos, sin, normed_t, dwo_x
    )
    qx_r = links.swap(qx_s, 0)
    own_sum.advance((qx_k,))
    share = input_share(bits, gx, qkv_mine, qkv_far, after=(own_sum.keep,))
    qx, = fold(bits, [(qx_k, 0, 0, n), (qx_r, 0, 0, n)], n, [(0, n)], "fold_qkv_core", after=(share,))
    qx_y = links.across(qx)
    go, sums_o, qo_s, qo_k = attend_back(
        bits, length, *own, g_own, ctx_own, aug_own, cos, sin, normed_t, dwo, after=(qx,), est=12
    )
    own_sum.advance((qo_k,))
    qo_r = links.swap(qo_s, 0)
    input_grad_out, sums1 = input_grad(
        at, inputs, gm, vec, go, share, query_weight, key_weight, value_weight, after=(own_sum.keep,)
    )
    q, = fold(bits, [(qo_k, 0, 0, n), (qx_y, 0, 0, n)], n, [(0, n)], "fold_qkv_y", after=(sums1,))
    q_s, q_k = halve(bits, q, qo_r, 1)
    q_r = links.swap(q_s, 1)
    stack, q_k = lax.optimization_barrier((stack, q_k))
    stack_r = links.across(stack)
    while not own_sum.done:
        own_sum.advance((q_k,))
    size = stack.shape[0]
    parts = [(stack_r, 0, 0, size), (own_sum.keep, 0, 0, size)]
    stack, = fold(bits, parts, size, [(0, size)], "fold_stack", after=(own_sum.keep, q_r))
    gathered = lax.all_gather(stack, "dp", axis=0, tiled=True)
    if dp_size > blocks:
        gathered = turned(gathered, dp_size // blocks, blocks)

    c = bits[0]
    halves = lambda a, b: [jnp.where(tensor == 0, a, b), jnp.where(tensor == 0, b, a)]
    mine_up, far_up = jnp.where(c == 0, dbu_mine, dbu_far), jnp.where(c == 0, dbu_far, dbu_mine)
    small = jnp.concatenate(
        [sums1[:2].reshape(-1), sums2[:4].reshape(-1)]
        + halves(
            jnp.concatenate([v.reshape(-1) for v in (sums_o, dbu)]),
            jnp.concatenate([v.reshape(-1) for v in (sums_x, mine_up, far_up)]),
        )
    )
    used = small.shape[0]
    cols = q.shape[1]
    small = jnp.pad(small, (0, 8 * cols - used)).reshape(8, cols)

    last = links.bits - 1
    parts = [q_k, q_r]
    after = (stack,)
    for bit in range(2, links.bits):
        send, keep, small = ride(bits, parts, small, bit if bit < last else None, False, after)
        after = ()
        parts = [keep, links.swap(send, bit)]
    _, q, small = ride(bits, parts, small, None, True)
    for bit in reversed(range(2, last)):
        q_r = links.swap(q, bit)
        if bit == last - 1:
            size = small.shape[0]
            for swap in (links.across, lambda v: links.swap(v, 0), lambda v: links.swap(v, 1)):
                parts = [(small, 0, 0, size), (swap(small), 0, 0, size)]
                small, = fold(bits, parts, size, [(0, size)], "fold_small", after=(q,))
        q = links.join(q, q_r, bit, after=(small,))
    q_r = links.swap(q, 1)
    q_far = links.swap(q, 0)
    grad_down, grad_up = wide_ffn(bits, gathered, after=(q,))
    q_r, grad_up = lax.optimization_barrier((q_r, grad_up))
    q_r_far = links.swap(q_r, 0)
    grad_q, grad_k, grad_v, grad_out = wide_qkv(bits, (q, q_r), (q_far, q_r_far), after=(grad_up,))

    small = small.reshape(-1)
    gain1, shift1, out_b, gain2, shift2, down_b = (small[i * d : (i + 1) * d] for i in range(6))
    side = 3 * width + ff
    mine = lax.dynamic_slice_in_dim(small, 6 * d + tensor * side, side, 0)
    qkv_bias = mine[: 3 * width].reshape(-1, 3, 128)
    return (
        layer_out, input_grad_out, gain1, shift1,
        grad_q, qkv_bias[:, 0].reshape(-1), grad_k, qkv_bias[:, 1].reshape(-1), grad_v, qkv_bias[:, 2].reshape(-1),
        grad_out, out_b, gain2, shift2, grad_up, mine[3 * width :], grad_down, down_b,
    )


def solution(mesh):
    rows = P(("dp", "tensor"), None)
    cols = P(None, "tensor")
    tens = P("tensor")
    return jax.shard_map(
        lambda *args: layer(mesh.shape["dp"], *args),
        mesh=mesh,
        in_specs=(
            rows, P("dp"), P(), P(), cols, tens, cols, tens, cols, tens, P("tensor", None), P(), P(), P(), cols, tens,
            P("tensor", None), P(), rows,
        ),
        out_specs=(
            rows, rows, P(), P(), cols, tens, cols, tens, cols, tens, P("tensor", None), P(), P(), P(), cols, tens,
            P("tensor", None), P(),
        ),
        check_vma=False,
    )
```

```python
import math

import jax
import jax.numpy as jnp
import numpy as np
from jax import lax
from jax.experimental import pallas as pl
from jax.experimental.pallas import tpu as pltpu
from jax.sharding import PartitionSpec as P

HEAD_DIM = 64
EPS = 1e-05
LOG2E = math.log2(math.e)
LN2 = math.log(2.0)
F32 = jnp.float32
BF = jnp.bfloat16
BIG = -1e30


def dot(a, b, ca=1, cb=0):
    return lax.dot_general(a, b, (((ca,), (cb,)), ((), ())), preferred_element_type=F32)


def cost(macs, nbytes, exps=0):
    return pl.CostEstimate(flops=int(2 * macs), bytes_accessed=int(nbytes), transcendentals=int(exps))


def busy(micros):
    return pl.CostEstimate(flops=int(micros * 1.1e9), bytes_accessed=1000, transcendentals=0)


EST = {
    "move": busy(0.01),
    "heads_own": busy(16),
    "heads_other": busy(100),
    "ffn_own": busy(0.01),
    "ffn_mine": busy(100),
    "ffn_far": busy(100),
    "share": busy(8),
    "input_grad": busy(8),
    "halve": busy(20),
}


def struct(shape, dtype):
    return jax.ShapeDtypeStruct(shape, dtype)


def whole(shape):
    return pl.BlockSpec(shape, lambda *_: (0,) * len(shape), pipeline_mode=pl.Buffered(1))


def whole_out(shape):
    return pl.BlockSpec(shape, lambda *_: (0,) * len(shape))


ANY = pl.BlockSpec(memory_space=pl.ANY)


def call(kernel, after, *, in_specs, out_specs, out_shape, estimate, name, grid=(1,), prefetch=0, scratch=(), alias=None, mib=28):
    after = tuple(after)
    n_in = prefetch + len(in_specs)

    def body(*refs):
        kernel(*refs[:n_in], *refs[n_in + len(after) :])

    run = pl.pallas_call(
        body,
        grid_spec=pltpu.PrefetchScalarGridSpec(
            num_scalar_prefetch=prefetch,
            grid=grid,
            in_specs=list(in_specs) + [ANY] * len(after),
            out_specs=out_specs,
            scratch_shapes=list(scratch),
        ),
        out_shape=out_shape,
        compiler_params=pltpu.CompilerParams(vmem_limit_bytes=mib << 20),
        input_output_aliases=alias or {},
        cost_estimate=estimate,
        name=name,
    )
    return lambda *args: run(*args, *after)


def norm_rows(v):
    mean = jnp.mean(v, axis=1, keepdims=True)
    cent = v - mean
    var = jnp.mean(cent * cent, axis=1, keepdims=True)
    r = lax.rsqrt(var + EPS)
    return cent * r, r


def norm_back(e, n, r):
    return r * (e - jnp.mean(e, axis=1, keepdims=True) - n * jnp.mean(e * n, axis=1, keepdims=True))


def rotary_tables(rows):
    half = HEAD_DIM // 2
    freq = (10000.0 ** (-2.0 * np.arange(half, dtype=np.float32) / HEAD_DIM)).astype(np.float32)
    ang = (np.arange(rows, dtype=np.float32)[:, None] * freq[None, :]).astype(np.float64)
    cos = np.cos(ang).astype(np.float32)
    sin = np.sin(ang).astype(np.float32)
    return np.concatenate([cos] * 4, 1), np.concatenate([-sin, sin] * 2, 1)


def swap_halves(v):
    lane = lax.broadcasted_iota(jnp.int32, v.shape, 1)
    return jnp.where((lane & 32) == 0, pltpu.roll(v, 96, 1), pltpu.roll(v, 32, 1))


def rotate(v, cos, sin):
    return v * cos + swap_halves(v) * sin


def rotate_back(v, cos, sin):
    return v * cos - swap_halves(v) * sin


class Row:
    def __init__(self, d, width, ff):
        at = 0
        for name, size in (
            ("gain1", d), ("shift1", d), ("out_bias", d), ("gain2", d), ("shift2", d), ("down_bias", d),
            ("qkv", 3 * width), ("up", ff),
        ):
            setattr(self, name, slice(at, at + size))
            at += size


def pull(src, dst, sem):
    copy = pltpu.make_async_copy(src, dst, sem)
    copy.start()
    return copy


def arrange(bits, arrays, shapes, moves, name, after=(), mib=28):
    def kernel(bits_ref, *refs):
        ins, outs, sem = refs[: len(arrays)], refs[len(arrays) : -1], refs[-1]
        copies = [pull(src, dst, sem.at[i]) for i, (src, dst) in enumerate(moves(bits_ref, ins, outs))]
        for copy in copies:
            copy.wait()

    return call(
        kernel,
        after,
        prefetch=1,
        in_specs=[ANY] * len(arrays),
        out_specs=[whole_out(shape) for shape in shapes],
        out_shape=[struct(shape, BF) for shape in shapes],
        scratch=[pltpu.SemaphoreType.DMA((8,))],
        estimate=EST["move"],
        name=name,
        mib=mib,
    )(bits, *arrays)


def block(bit, size):
    return pl.ds(pl.multiple_of(bit * size, size), size)


def fold(bits, parts, rows, outs, name, after=(), width=None):
    arrays = [p[0] for p in parts]
    width = width or arrays[0].shape[1]
    dtype = arrays[0].dtype
    half = rows // 2
    shapes = [(half, width)] * 2 if isinstance(outs, int) else [(n, width) for _, n in outs]

    def kernel(bits_ref, *refs):
        ins, outs_r, acc = refs[: len(parts)], refs[len(parts) : -1], refs[-1]
        seen = []
        for ref, (_, src, dst, n) in zip(ins, parts):
            value = ref[src : src + n, 0:width].astype(F32)
            fresh = not any(dst < b and a < dst + n for a, b in seen)
            acc[dst : dst + n, :] = value if fresh else acc[dst : dst + n, :] + value
            seen.append((dst, dst + n))
        if isinstance(outs, int):
            bit = bits_ref[outs]
            for ref, at in zip(outs_r, (1 - bit, bit)):
                ref[...] = acc[pl.ds(pl.multiple_of(at * half, 8 if half % 8 == 0 else 1), half), :].astype(dtype)
        else:
            for ref, (start, n) in zip(outs_r, outs):
                ref[...] = acc[start : start + n, :].astype(dtype)

    return call(
        kernel,
        after,
        prefetch=1,
        in_specs=[whole(a.shape) for a in arrays],
        out_specs=[whole_out(shape) for shape in shapes],
        out_shape=[struct(shape, dtype) for shape in shapes],
        scratch=[pltpu.VMEM((rows, width), F32)],
        estimate=EST["move"],
        name=name,
    )(bits, *arrays)


def put_qkv(pre, cos, sin, q_ref, k_ref, v_ref):
    width = q_ref.shape[1]
    for i in range(width // 128):
        sl = slice(i * 128, (i + 1) * 128)
        q_ref[:, sl] = (rotate(pre[0][:, sl], cos, sin) * (LOG2E / 8.0)).astype(BF)
        k_ref[:, sl] = rotate(pre[1][:, sl], cos, sin).astype(BF)
        v_ref[:, sl] = pre[2][:, sl].astype(BF)


def split3(v):
    hi = v.astype(BF)
    rest = v - hi.astype(F32)
    mid = rest.astype(BF)
    lo = rest - mid.astype(F32)
    return hi.astype(F32), mid.astype(F32), lo


def spread(lane, first, one, two):
    out = jnp.where(lane == 0, first, 0.0)
    for at, part in enumerate((*split3(one), *split3(two))):
        out = jnp.where(lane == at + 1, part, out)
    return out.astype(BF)


def attend_pair(length, q_ref, k_ref, v_ref, ctx_ref, aug_ref):
    bq = 256
    rows = q_ref.shape[0]
    lane1 = lax.broadcasted_iota(jnp.int32, (1, 128), 1)
    krow = lax.broadcasted_iota(jnp.int32, (rows, 128), 0)
    klane = lax.broadcasted_iota(jnp.int32, (rows, 128), 1)
    lane = lax.broadcasted_iota(jnp.int32, (bq, 128), 1)
    qrow = lax.broadcasted_iota(jnp.int32, (bq, 128), 0)
    kaug = jnp.where((klane == 0) & (krow >= length), BIG, 0.0).astype(BF)
    k = jnp.concatenate([k_ref[...], kaug], 1)
    v = jnp.concatenate([v_ref[...], jnp.ones((rows, 128), BF)], 1)
    qaug = jnp.where(lane == 0, 1.0, 0.0).astype(BF)
    for i in range(rows // bq):
        sl = slice(i * bq, (i + 1) * bq)
        q = q_ref[sl, :]
        outs, totals = [], []
        for h in range(2):
            keep = ((lane1 < 64) if h == 0 else (lane1 >= 64)).astype(BF)
            s = dot(jnp.concatenate([q * keep, qaug], 1), k, 1, 1)
            top = jnp.max(s, axis=1, keepdims=True)
            p = jnp.exp2(s - top).astype(BF)
            o = dot(p, v)
            total = o[:, 128:]
            outs.append(o[:, :128] / total)
            totals.append(top + jnp.log2(total))
        ctx = jnp.where(lane < 64, outs[0], outs[1])
        ctx_ref[sl, :] = jnp.where(qrow + i * bq < length, ctx, 0.0).astype(BF)
        aug_ref[sl, :] = spread(lane, 1.0, totals[0], totals[1])


def attend_all(length, q, k, v, ctx, aug):
    for p in range(q.shape[1] // 128):
        sl = slice(p * 128, (p + 1) * 128)
        attend_pair(length, *(ref.at[:, sl] for ref in (q, k, v, ctx, aug)))


def heads_own_kernel(
    at, cut, bits_ref, len_ref, x_ref, vec_ref, wq_ref, wk_ref, wv_ref, cos_ref, sin_ref, wu_h, wd_h,
    n_h, nt_h, q_h, k_h, v_h, ctx_h, aug_h, near_h, rest_h,
    n_s, nt_s, q_s, k_s, v_s, ctx_s, aug_s, near_s, rest_s, sem,
):
    rows = x_ref.shape[0]
    width = q_s.shape[1]
    loads = [
        pull(src, dst, sem.at[i]) for i, (src, dst) in enumerate(cut(bits_ref, (wu_h, wd_h), (near_s, rest_s)))
    ]
    blk = 256
    bias = vec_ref[:, at.qkv]
    for i in range(rows // blk):
        sl = slice(i * blk, (i + 1) * blk)
        n, _ = norm_rows(x_ref[sl, :].astype(F32))
        low = (n * vec_ref[:, at.gain1] + vec_ref[:, at.shift1]).astype(BF)
        n_s[sl, :] = low
        nt_s[:, sl] = low.T
        pre = [
            dot(low, w[...]) + bias[:, j * width : (j + 1) * width] for j, w in enumerate((wq_ref, wk_ref, wv_ref))
        ]
        put_qkv(pre, cos_ref[sl, :], sin_ref[sl, :], *(ref.at[sl, :] for ref in (q_s, k_s, v_s)))
    for load in loads:
        load.wait()
    pairs = [
        (near_s, near_h), (rest_s, rest_h), (n_s, n_h), (nt_s, nt_h), (q_s, q_h), (k_s, k_h), (v_s, v_h)
    ]
    stores = [pull(src, dst, sem.at[8 + i]) for i, (src, dst) in enumerate(pairs)]
    attend_all(len_ref[0], q_s, k_s, v_s, ctx_s, aug_s)
    stores += [pull(ctx_s, ctx_h, sem.at[15]), pull(aug_s, aug_h, sem.at[16])]
    for store in stores:
        store.wait()


def heads_own(at, cut, shapes, bits, length, x, vec, wq, wk, wv, cos, sin, wu, wd, after=()):
    rows, d = x.shape
    width = wq.shape[1]
    outs = [(rows, d), (d, rows)] + [(rows, width)] * 5 + list(shapes)
    return call(
        lambda *refs: heads_own_kernel(at, cut, *refs),
        after,
        prefetch=2,
        in_specs=[whole(a.shape) for a in (x, vec, wq, wk, wv, cos, sin)] + [ANY] * 2,
        out_specs=[ANY] * len(outs),
        out_shape=[struct(shape, BF) for shape in outs],
        scratch=[pltpu.VMEM(shape, BF) for shape in outs] + [pltpu.SemaphoreType.DMA((17,))],
        estimate=EST["heads_own"],
        name="heads_own",
        mib=56,
    )(bits, length, x, vec, wq, wk, wv, cos, sin, wu, wd)


def heads_other_kernel(
    at, bits_ref, len_ref, n_ref, wm_ref, wf_ref, b_ref, cos_ref, sin_ref, q_h, k_h, v_h, ctx_h, aug_h,
    q_s, k_s, v_s, ctx_s, aug_s, sem,
):
    rows = n_ref.shape[0]
    width = q_s.shape[1]
    half = wm_ref.shape[0]
    c = bits_ref[0]
    blk = 256
    for i in range(rows // blk):
        sl = slice(i * blk, (i + 1) * blk)
        pre = dot(n_ref[sl, block(c, half)], wm_ref[...]) + dot(n_ref[sl, block(1 - c, half)], wf_ref[...])
        pre = pre + b_ref[:, at.qkv]
        put_qkv(
            [pre[:, j * width : (j + 1) * width] for j in range(3)], cos_ref[sl, :], sin_ref[sl, :],
            *(ref.at[sl, :] for ref in (q_s, k_s, v_s)),
        )
    stores = [pull(src, dst, sem.at[i]) for i, (src, dst) in enumerate(((q_s, q_h), (k_s, k_h), (v_s, v_h)))]
    attend_all(len_ref[0], q_s, k_s, v_s, ctx_s, aug_s)
    stores += [pull(ctx_s, ctx_h, sem.at[3]), pull(aug_s, aug_h, sem.at[4])]
    for store in stores:
        store.wait()


def heads_other(at, bits, length, n, w_mine, w_far, bias, cos, sin, after=()):
    rows = n.shape[0]
    width = w_mine.shape[1] // 3
    outs = [(rows, width)] * 5
    return call(
        lambda *refs: heads_other_kernel(at, *refs),
        after,
        prefetch=2,
        in_specs=[whole(a.shape) for a in (n, w_mine, w_far, bias, cos, sin)],
        out_specs=[ANY] * 5,
        out_shape=[struct(shape, BF) for shape in outs],
        scratch=[pltpu.VMEM(shape, BF) for shape in outs] + [pltpu.SemaphoreType.DMA((5,))],
        estimate=EST["heads_other"],
        name="heads_other",
        mib=56,
    )(bits, length, n, w_mine, w_far, bias, cos, sin)


def attend_back_kernel(
    bq, bits_ref, len_ref, q_ref, k_ref, v_ref, g_ref, ctx_ref, aug_ref, cos_ref, sin_ref, nt_ref, wo_ref,
    d_ref, sum_ref, send_ref, keep_ref, dqt, dall,
):
    rows = q_ref.shape[0]
    length = len_ref[0]
    lane1 = lax.broadcasted_iota(jnp.int32, (1, 128), 1)
    krow = lax.broadcasted_iota(jnp.int32, (rows, 128), 0)
    klane = lax.broadcasted_iota(jnp.int32, (rows, 128), 1)
    lane = lax.broadcasted_iota(jnp.int32, (bq, 128), 1)
    k = k_ref[...]
    v = v_ref[...]
    kt = k.T
    dks, dvs = [], []
    for h in range(2):
        keep = ((lane1 < 64) if h == 0 else (lane1 >= 64)).astype(BF)
        first = 1 + 3 * h
        mine = jnp.where((klane >= first) & (klane < first + 3), -1.0, 0.0)
        kaug = jnp.where((klane == 0) & (krow >= length), BIG, mine).astype(BF)
        kh = jnp.concatenate([k * keep, kaug], 1)
        vh = jnp.concatenate([v * keep, mine.astype(BF)], 1)
        dk = jnp.zeros((rows, 128), F32)
        dv = jnp.zeros((rows, 128), F32)
        for i in range(rows // bq):
            sl = slice(i * bq, (i + 1) * bq)
            q = q_ref[sl, :]
            g = g_ref[sl, :]
            prod = g.astype(F32) * ctx_ref[sl, :].astype(F32)
            d0 = jnp.sum(jnp.where(lane < 64, prod, 0.0), 1, keepdims=True)
            d1 = jnp.sum(jnp.where(lane < 64, 0.0, prod), 1, keepdims=True)
            gaug = spread(lane, 0.0, d0, d1)
            st = dot(kh, jnp.concatenate([q, aug_ref[sl, :]], 1), 1, 1)
            pt = jnp.exp2(st)
            dpt = dot(vh, jnp.concatenate([g, gaug], 1), 1, 1)
            ds = (pt * dpt).astype(BF)
            dv = dv + dot(pt.astype(BF), g)
            dk = dk + dot(ds, q)
            dqt[h * 64 : (h + 1) * 64, sl] = dot(kt[h * 64 : (h + 1) * 64, :], ds)
        dks.append(dk)
        dvs.append(dv)
    cos = cos_ref[...]
    sin = sin_ref[...]
    dq = rotate_back(dqt[...].T * (1.0 / 8.0), cos, sin).astype(BF)
    dk = rotate_back(jnp.where(klane < 64, dks[0], dks[1]) * LN2, cos, sin).astype(BF)
    dv = jnp.where(klane < 64, dvs[0], dvs[1]).astype(BF)
    for at, val in enumerate((dq, dk, dv)):
        sl = slice(at * 128, (at + 1) * 128)
        d_ref[:, sl] = val
        sum_ref[:, sl] = jnp.sum(val.astype(F32), axis=0, keepdims=True)
    j = pl.program_id(0)
    dall[:, block(j, 384)] = jnp.concatenate([dq, dk, dv], 1)

    @pl.when(j == pl.num_programs(0) - 1)
    def _():
        half = send_ref.shape[0]
        c = bits_ref[0]
        for ref, part in ((send_ref, 1 - c), (keep_ref, c)):
            width = dall.shape[1]
            ref[:, 0:width] = dot(nt_ref[block(part, half), :], dall[...]).astype(BF)
            ref[:, width:] = wo_ref[block(part, half), :]


def attend_back(bits, length, q, k, v, g, ctx, aug, cos, sin, nt, wo, after=(), est=100):
    rows, width = q.shape
    d = 2 * width
    bs = pl.BlockSpec((rows, 128), lambda j, *_: (0, j))
    return call(
        lambda *refs: attend_back_kernel(256, *refs),
        after,
        prefetch=2,
        grid=(width // 128,),
        in_specs=[bs] * 6 + [whole((rows, 128))] * 2 + [whole(nt.shape), whole(wo.shape)],
        out_specs=[pl.BlockSpec((rows, 384), lambda j, *_: (0, j)), pl.BlockSpec((1, 384), lambda j, *_: (0, j))]
        + [whole_out((d // 2, 4 * width))] * 2,
        out_shape=[struct((rows, 3 * width), BF), struct((1, 3 * width), F32)] + [struct((d // 2, 4 * width), BF)] * 2,
        scratch=[pltpu.VMEM((128, rows), F32), pltpu.VMEM((rows, 3 * width), BF)],
        estimate=busy(est),
        name="attend_back",
        mib=56,
    )(bits, length, q, k, v, g, ctx, aug, cos, sin, nt, wo)


def gelu_pair(h):
    z = jnp.abs(h) * (0.3275911 / math.sqrt(2.0)) + 1.0
    t = pl.reciprocal(z, approx=True)
    t = t * (2.0 - z * t)
    e = jnp.exp2(h * h * (-0.5 * LOG2E))
    poly = 0.5 * 1.061405429 * t - 0.5 * 1.453152027
    poly = poly * t + 0.5 * 1.421413741
    poly = poly * t - 0.5 * 0.284496736
    poly = poly * t + 0.5 * 0.254829592
    w = poly * t * e
    cdf = jnp.where(h >= 0.0, 1.0 - w, w)
    return h * cdf, cdf + h * e * (1.0 / math.sqrt(2.0 * math.pi))


def ffn_quarter(n2, n2t, og, wu, wd, bias, out_acc, dn_acc, act_s, dh_s, gd, gu, first, before=None, done=None):
    rows, d = og.shape
    part = wd.shape[0]
    blk = 256
    dbias = jnp.zeros((1, part), F32)
    if before is not None:
        before(0, blk)
    for i in range(rows // blk):
        sl = slice(i * blk, (i + 1) * blk)
        if before is not None and i + 1 < rows // blk:
            before(i + 1, blk)
        h = dot(n2[sl, :], wu[...]) + bias
        act, slope = gelu_pair(h)
        act = act.astype(BF)
        dh = (slope * dot(og[sl, :], wd[...], 1, 1)).astype(BF)
        act_s[sl, :] = act
        dh_s[sl, :] = dh
        dbias = dbias + jnp.sum(dh.astype(F32), axis=0, keepdims=True)
        o = dot(act, wd[...])
        e = dot(dh, wu[...], 1, 1)
        out_acc[sl, :] = o if first else out_acc[sl, :] + o
        dn_acc[sl, :] = e if first else dn_acc[sl, :] + e
        if done is not None and i > 0:
            done(i - 1, blk)
    if done is not None:
        done(rows // blk - 1, blk)
    gd[...] = dot(act_s[...], og[...], 0, 0).astype(BF)
    gu[...] = dot(n2t[...], dh_s[...]).astype(BF)
    return dbias


def ffn_own_kernel(
    at, bits_ref, x_ref, co_ref, cx_ref, woo_ref, wox, vec_ref, og_h, wu_h, wd_h,
    mid_h, n2_h, n2t_h, out_h, dn_h, send_h, keep_h, db_ref,
    og, wu, wd, mid, n2, n2t, out, dn, outb, dnb, act_s, dh_s, gd, gu, sem,
):
    rows, d = x_ref.shape
    part = wu_h.shape[1] // 2
    c = bits_ref[0]
    cols = [block(p, part) for p in (1 - c, c)]
    biases = [pl.ds(pl.multiple_of(at.up.start + p * part, 128), part) for p in (1 - c, c)]
    loads = [pull(og_h, og, sem.at[0])]
    for q in range(2):
        loads.append(pull(wu_h.at[:, cols[q]], wu.at[q], sem.at[1 + 2 * q]))
        loads.append(pull(wd_h.at[cols[q], :], wd.at[q], sem.at[2 + 2 * q]))
    stores = []

    def enter(i, blk):
        sl = slice(i * blk, (i + 1) * blk)
        att = dot(co_ref[sl, :], woo_ref[...]) + dot(cx_ref[sl, :], wox[...])
        v = x_ref[sl, :].astype(F32) + att + vec_ref[:, at.out_bias]
        mid[sl, :] = v
        n, _ = norm_rows(v)
        low = (n * vec_ref[:, at.gain2] + vec_ref[:, at.shift2]).astype(BF)
        n2[sl, :] = low
        n2t[:, sl] = low.T
        if i == 0:
            for load in loads:
                load.wait()
        if (i + 1) * blk == rows:
            stores.extend([pull(mid, mid_h, sem.at[5]), pull(n2, n2_h, sem.at[6]), pull(n2t, n2t_h, sem.at[7])])

    def flush(i, blk):
        sl = pl.ds(i * blk, blk)
        outb[sl, :] = out[sl, :].astype(BF)
        dnb[sl, :] = dn[sl, :].astype(BF)
        stores.append(pull(outb.at[sl, :], out_h.at[sl, :], sem.at[8 + i]))
        stores.append(pull(dnb.at[sl, :], dn_h.at[sl, :], sem.at[12 + i]))

    for q in range(2):
        db_ref[:, cols[q]] = ffn_quarter(
            n2, n2t, og, wu.at[q], wd.at[q], vec_ref[:, biases[q]], out, dn, act_s, dh_s, gd.at[q], gu.at[q], q == 0,
            enter if q == 0 else None, flush if q == 1 else None,
        )
        stores.append(pull(gd.at[q], (send_h, keep_h)[q].at[0:part, :], sem.at[16 + q]))
        stores.append(pull(gu.at[q], (send_h, keep_h)[q].at[part:, :], sem.at[20 + q]))
    for store in stores:
        store.wait()


def ffn_own(at, bits, x, ctx_own, ctx_other, wo_own, wo_other, vec, og, wu, wd, after=()):
    rows, d = x.shape
    ff = wu.shape[1]
    part = ff // 2
    half = ctx_own.shape[1]
    return call(
        lambda *refs: ffn_own_kernel(at, *refs),
        after,
        prefetch=1,
        in_specs=[
            whole((rows, d)), whole((rows, half)), whole((rows, half)), whole((half, d)), whole((half, d)), whole(vec.shape),
        ] + [ANY] * 3,
        out_specs=[ANY] * 7 + [whole_out((1, ff))],
        scratch=[
            pltpu.VMEM((rows, d), BF), pltpu.VMEM((2, d, part), BF), pltpu.VMEM((2, part, d), BF),
            pltpu.VMEM((rows, d), F32), pltpu.VMEM((rows, d), BF), pltpu.VMEM((d, rows), BF),
            pltpu.VMEM((rows, d), F32), pltpu.VMEM((rows, d), F32), pltpu.VMEM((rows, d), BF), pltpu.VMEM((rows, d), BF),
            pltpu.VMEM((rows, part), BF), pltpu.VMEM((rows, part), BF),
            pltpu.VMEM((2, part, d), BF), pltpu.VMEM((2, d, part), BF),
            pltpu.SemaphoreType.DMA((22,)),
        ],
        out_shape=[
            struct((rows, d), F32), struct((rows, d), BF), struct((d, rows), BF), struct((rows, d), BF),
            struct((rows, d), BF), struct((part + d, d), BF), struct((part + d, d), BF),
            struct((1, ff), F32),
        ],
        estimate=EST["ffn_own"],
        name="ffn_own",
        mib=56,
    )(bits, x, ctx_own, ctx_other, wo_own, wo_other, vec, og, wu, wd)


BLOCK_BITS = 4


def sub_block(s, q, x, n):
    out = q + 2 * x
    for k in range(2, n):
        out = out + (((s >> (n - 1 - k)) & 1) << k)
    return out


def put_blocks(grads, stack, q, n, sem, at):
    count = 1 << (n - 2)
    size = grads[0].shape[0] // count
    return [
        pull(
            grads[x].at[s * size : (s + 1) * size, :],
            stack.at[pl.ds(pl.multiple_of(sub_block(s, q, x, n) * size, size), size), :],
            sem.at[at + x * count + s],
        )
        for x in range(2)
        for s in range(count)
    ]


def gather_weights(bits_ref, near, near_x, rest, w, sem, at):
    rows = near.shape[0]
    b = bits_ref[1]
    return [
        pull(near, w.at[block(b, rows), :], sem.at[at]),
        pull(near_x, w.at[block(1 - b, rows), :], sem.at[at + 1]),
        pull(rest, w.at[2 * rows :, :], sem.at[at + 2]),
    ]


def ffn_mine_kernel(
    n, bits_ref, n2_ref, b_ref, near_h, near_x_h, rest_h, og_h, n2t_h, out_h, dn_h, stack_h, db_ref,
    w_ref, og, n2t, out, dn, outb, dnb, act_s, dh_s, gd, gu, sem,
):
    d = og.shape[1]
    part = w_ref.shape[0] - d
    c = bits_ref[0]
    bias_at = b_ref.shape[1] - 2 * part
    at = 10 + (1 << (n - 1))
    loads = gather_weights(bits_ref, near_h, near_x_h, rest_h, w_ref, sem, at)
    loads += [pull(og_h, og, sem.at[0]), pull(n2t_h, n2t, sem.at[1])]
    for load in loads:
        load.wait()
    stores = []

    def flush(i, blk):
        sl = pl.ds(i * blk, blk)
        outb[sl, :] = out[sl, :].astype(BF)
        dnb[sl, :] = dn[sl, :].astype(BF)
        stores.append(pull(outb.at[sl, :], out_h.at[sl, :], sem.at[2 + i]))
        stores.append(pull(dnb.at[sl, :], dn_h.at[sl, :], sem.at[6 + i]))

    bias = b_ref[:, pl.ds(pl.multiple_of(bias_at + c * part, 128), part)]
    db_ref[...] = ffn_quarter(
        n2_ref, n2t, og, w_ref.at[0:d, :], w_ref.at[d:, :], bias, out, dn, act_s, dh_s, gd, gu, True, None, flush
    )
    stores += put_blocks((gd, gu), stack_h, c, n, sem, 10)
    for store in stores:
        store.wait()


def ffn_mine(bits, n2, near, near_x, rest, bias, og, n2t, after=()):
    rows, d = og.shape
    part = 2 * near.shape[0] + rest.shape[0] - d
    n = min(bits.shape[0], BLOCK_BITS)
    return call(
        lambda *refs: ffn_mine_kernel(n, *refs),
        after,
        prefetch=1,
        in_specs=[whole((rows, d)), whole(bias.shape)] + [ANY] * 5,
        out_specs=[ANY] * 3 + [whole_out((1, part))],
        scratch=[
            pltpu.VMEM((d + part, d), BF),
            pltpu.VMEM((rows, d), BF), pltpu.VMEM((d, rows), BF), pltpu.VMEM((rows, d), F32), pltpu.VMEM((rows, d), F32),
            pltpu.VMEM((rows, d), BF), pltpu.VMEM((rows, d), BF),
            pltpu.VMEM((rows, part), BF), pltpu.VMEM((rows, part), BF), pltpu.VMEM((part, d), BF), pltpu.VMEM((d, part), BF),
            pltpu.SemaphoreType.DMA((13 + (1 << (n - 1)),)),
        ],
        out_shape=[
            struct((rows, d), BF), struct((rows, d), BF), struct((4 * part, d), BF), struct((1, part), F32),
        ],
        estimate=EST["ffn_mine"],
        name="ffn_mine",
        mib=56,
    )(bits, n2, bias, near, near_x, rest, og, n2t)


def ffn_far_kernel(
    at, n, bits_ref, len_ref, n2_ref, b_ref, vec_ref, near_h, near_x_h, rest_h, og_h, n2t_h, mid_h, out1_h, dn1_h, out2_h, dn2_h,
    co_h, cx_h, woo_h, wox_h, stack_in,
    lay_h, gm_h, dco_h, dcx_h, stack_h, dwoo_h, dwox_h, sums_ref, db_ref,
    w_ref, og, n2t, mid, out1, dn1, out2, dn2, co, cx, woo, wox, out, dn, act_s, dh_s, gd, gu, lay, gmb, dco, dcx, dwoo, dwox, sem,
):
    rows, d = og.shape
    part = w_ref.shape[0] - d
    half = co.shape[1]
    c = bits_ref[0]
    length = len_ref[0]
    bias_at = b_ref.shape[1] - 2 * part
    first = gather_weights(bits_ref, near_h, near_x_h, rest_h, w_ref, sem, 18 + (1 << (n - 1)))
    loads = [
        pull(src, dst, sem.at[i])
        for i, (src, dst) in enumerate((
            (og_h, og), (n2t_h, n2t), (mid_h, mid), (dn1_h, dn1), (dn2_h, dn2), (out1_h, out1), (out2_h, out2),
            (woo_h, woo), (wox_h, wox), (co_h, co), (cx_h, cx),
        ))
    ]
    for load in first + loads[:1]:
        load.wait()
    sums_ref[...] = jnp.zeros_like(sums_ref)
    stores = []

    def finish(i, blk):
        if i == 0:
            for load in loads[1:]:
                load.wait()
        sl = slice(i * blk, (i + 1) * blk)
        v = mid[sl, :]
        out_sum = out1[sl, :].astype(F32) + out2[sl, :].astype(F32) + out[sl, :]
        lay[sl, :] = (v + out_sum + vec_ref[:, at.down_bias]).astype(BF)
        unit, r = norm_rows(v)
        gn = dn1[sl, :].astype(F32) + dn2[sl, :].astype(F32) + dn[sl, :]
        o = og[sl, :].astype(F32)
        g = o + norm_back(gn * vec_ref[:, at.gain2], unit, r)
        mid[sl, :] = g
        low = g.astype(BF)
        gmb[sl, :] = low
        for k, val in enumerate((g, gn * unit, gn, o)):
            sums_ref[k : k + 1, :] += jnp.sum(val, axis=0, keepdims=True)
        valid = lax.broadcasted_iota(jnp.int32, (blk, 1), 0) + i * blk < length
        dco[sl, :] = jnp.where(valid, dot(low, woo[...], 1, 1), 0.0).astype(BF)
        dcx[sl, :] = jnp.where(valid, dot(low, wox[...], 1, 1), 0.0).astype(BF)

    bias = b_ref[:, pl.ds(pl.multiple_of(bias_at + (1 - c) * part, 128), part)]
    db_ref[...] = ffn_quarter(
        n2_ref, n2t, og, w_ref.at[0:d, :], w_ref.at[d:, :], bias, out, dn, act_s, dh_s, gd, gu, True, None, finish
    )
    stores = put_blocks((gd, gu), stack_h, 1 - c, n, sem, 18)
    stores += [
        pull(src, dst, sem.at[12 + k])
        for k, (src, dst) in enumerate(((lay, lay_h), (mid, gm_h), (dco, dco_h), (dcx, dcx_h)))
    ]
    dwoo[...] = dot(gmb[...], co[...], 0, 0).astype(BF)
    dwox[...] = dot(gmb[...], cx[...], 0, 0).astype(BF)
    stores += [pull(dwoo, dwoo_h, sem.at[16]), pull(dwox, dwox_h, sem.at[17])]
    for store in stores:
        store.wait()


def ffn_far(
    at, bits, length, n2, near, near_x, rest, bias, vec, og, n2t, mid, out1, dn1, out2, dn2, ctx_own, ctx_other, wo_own,
    wo_other, stack, after=(),
):
    rows, d = og.shape
    part = 2 * near.shape[0] + rest.shape[0] - d
    n = min(bits.shape[0], BLOCK_BITS)
    half = ctx_own.shape[1]
    bf = lambda *shape: pltpu.VMEM(shape, BF)
    f32 = lambda *shape: pltpu.VMEM(shape, F32)
    return call(
        lambda *refs: ffn_far_kernel(at, n, *refs),
        after,
        prefetch=2,
        in_specs=[whole((rows, d)), whole(bias.shape), whole(vec.shape)] + [ANY] * 15,
        out_specs=[ANY] * 7 + [whole_out((8, d)), whole_out((1, part))],
        scratch=[
            bf(d + part, d), bf(rows, d), bf(d, rows), f32(rows, d), bf(rows, d), bf(rows, d), bf(rows, d), bf(rows, d),
            bf(rows, half), bf(rows, half), bf(half, d), bf(half, d), f32(rows, d), f32(rows, d),
            bf(rows, part), bf(rows, part), bf(part, d), bf(d, part), bf(rows, d), bf(rows, d), bf(rows, half),
            bf(rows, half), bf(d, half), bf(d, half), pltpu.SemaphoreType.DMA((21 + (1 << (n - 1)),)),
        ],
        out_shape=[
            struct((rows, d), BF), struct((rows, d), F32), struct((rows, half), BF), struct((rows, half), BF),
            struct(stack.shape, BF), struct((d, half), BF), struct((d, half), BF), struct((8, d), F32), struct((1, part), F32),
        ],
        alias={19: 4},
        estimate=EST["ffn_far"],
        name="ffn_far",
        mib=56,
    )(
        bits, length, n2, bias, vec, near, near_x, rest, og, n2t, mid, out1, dn1, out2, dn2, ctx_own, ctx_other, wo_own,
        wo_other, stack,
    )


def by_pairs(wcat, matrices, rows, width):
    for p in range(width // 128):
        for i in range(3):
            to = slice((3 * p + i) * 128, (3 * p + i + 1) * 128)
            ref, base = matrices[i]
            wcat[rows, to] = ref[:, base + p * 128 : base + (p + 1) * 128]


def share_kernel(bits_ref, g_ref, wm, wf, out_ref, wcat):
    width = g_ref.shape[1] // 3
    c = bits_ref[0]
    half = wm.shape[0]

    @pl.when(pl.program_id(0) == 0)
    def _():
        for ref, part in ((wm, c), (wf, 1 - c)):
            by_pairs(wcat, [(ref, i * width) for i in range(3)], block(part, half), width)

    out_ref[...] = dot(g_ref[...], wcat[...], 1, 1).astype(BF)


def input_share(bits, g, w_mine, w_far, after=()):
    rows, cols = g.shape
    d = 2 * w_mine.shape[0]
    blk = 512
    row = lambda w: pl.BlockSpec((blk, w), lambda i, *_: (i, 0))
    return call(
        share_kernel, after, prefetch=1, grid=(rows // blk,),
        in_specs=[row(cols), whole(w_mine.shape), whole(w_far.shape)], out_specs=row(d),
        out_shape=struct((rows, d), BF), scratch=[pltpu.VMEM((d, cols), BF)],
        estimate=EST["share"], name="input_share", mib=56,
    )(bits, g, w_mine, w_far)


def input_grad_kernel(at, x_ref, gm_ref, vec_ref, g_ref, share_ref, wq, wk, wv, out_ref, sums_ref, wcat):
    width = wq.shape[1]

    @pl.when(pl.program_id(0) == 0)
    def _():
        sums_ref[...] = jnp.zeros_like(sums_ref)
        by_pairs(wcat, [(ref, 0) for ref in (wq, wk, wv)], slice(None), width)

    gn = dot(g_ref[...], wcat[...], 1, 1) + share_ref[...].astype(F32)
    n, r = norm_rows(x_ref[...].astype(F32))
    out_ref[...] = (gm_ref[...] + norm_back(gn * vec_ref[:, at.gain1], n, r)).astype(BF)
    sums_ref[0:1, :] += jnp.sum(gn * n, axis=0, keepdims=True)
    sums_ref[1:2, :] += jnp.sum(gn, axis=0, keepdims=True)


def input_grad(at, x, gm, vec, g, share, wq, wk, wv, after=()):
    rows, d = x.shape
    width = wq.shape[1]
    blk = 256
    row = lambda w: pl.BlockSpec((blk, w), lambda i, *_: (i, 0))
    return call(
        lambda *refs: input_grad_kernel(at, *refs),
        after,
        grid=(rows // blk,),
        in_specs=[row(d), row(d), whole(vec.shape), row(3 * width), row(d)] + [whole((d, width))] * 3,
        out_specs=[row(d), whole_out((8, d))],
        out_shape=[struct((rows, d), BF), struct((8, d), F32)],
        scratch=[pltpu.VMEM((d, 3 * width), BF)],
        estimate=EST["input_grad"],
        name="input_grad",
        mib=56,
    )(x, gm, vec, g, share, wq, wk, wv)


def wide_qkv(bits, near, far, after=()):
    size, width = near[0].shape
    width //= 4

    def kernel(bits_ref, *refs):
        ins, outs, turn = refs[:4], refs[4:8], refs[8]
        base = (pl.program_id(0) != bits_ref[0]).astype(jnp.int32) * 2
        for half in range(2):
            want = base + (half != bits_ref[1]).astype(jnp.int32)
            rows = slice(half * size, (half + 1) * size)
            for k in range(4):

                @pl.when(want == k)
                def _():
                    ref = ins[k]
                    for i, out in enumerate(outs[:3]):
                        for p in range(width // 128):
                            src = slice((3 * p + i) * 128, (3 * p + i + 1) * 128)
                            out[rows, p * 128 : (p + 1) * 128] = ref[:, src].astype(F32)
                    turn[rows, :] = ref[:, 3 * width :].astype(F32)

        outs[3][...] = turn[...].T

    return call(
        kernel, after, prefetch=1, grid=(2,),
        in_specs=[whole((size, 4 * width))] * 4,
        out_specs=[pl.BlockSpec((2 * size, width), lambda i, *_: (i, 0))] * 3
        + [pl.BlockSpec((width, 2 * size), lambda i, *_: (0, i))],
        out_shape=[struct((4 * size, width), F32)] * 3 + [struct((width, 4 * size), F32)],
        scratch=[pltpu.VMEM((2 * size, width), F32)], estimate=EST["move"], name="wide_qkv", mib=56,
    )(bits, *near, *far)


def wide_ffn(bits, stack, after=()):
    rows, d = stack.shape
    n = min(bits.shape[0], BLOCK_BITS)
    part = rows // 4
    count = 1 << (n - 2)
    size = part // count

    def kernel(bits_ref, *refs):
        for x in range(2):
            for k in range(2):
                refs[4 + x][k * size : (k + 1) * size, :] = refs[2 * x + k][...].astype(F32)

    def place(x, k):
        return lambda q, t, *_: (sub_block(2 * t + k, q, x, n), 0)

    return call(
        kernel, after, prefetch=1, grid=(2, count // 2),
        in_specs=[pl.BlockSpec((size, d), place(x, k)) for x in range(2) for k in range(2)],
        out_specs=[
            pl.BlockSpec((2 * size, d), lambda q, t, *_: (q * (count // 2) + t, 0)),
            pl.BlockSpec((2 * size, d), lambda q, t, *_: (t, q)),
        ],
        out_shape=[struct((2 * part, d), F32), struct((part, 2 * d), F32)],
        estimate=EST["move"], name="wide_ffn", mib=56,
    )(bits, stack, stack, stack, stack)


def wide_both(bits, stack, pieces, after=()):
    rows, d = stack.shape
    n = min(bits.shape[0], BLOCK_BITS)
    part = rows // 2
    count = 1 << (n - 2)
    size = part // count // 2

    def kernel(bits_ref, *refs):
        blocks, ins, outs = refs[:4], refs[4:8], refs[8:]
        base = (pl.program_id(0) != bits_ref[0]).astype(jnp.int32) * 2
        t = pl.program_id(1)
        for x in range(2):
            for k in range(2):
                outs[x][2 * k * size : (2 * k + 1) * size, :] = blocks[2 * x + k][...].astype(F32)
            want = base + (x != bits_ref[1]).astype(jnp.int32)
            for p in range(4):

                @pl.when(want == p)
                def _():
                    for k in range(2):
                        src = pl.ds(pl.multiple_of((2 * t + k) * size, size), size)
                        outs[x][(2 * k + 1) * size : (2 * k + 2) * size, :] = ins[p][src, :].astype(F32)

    def place(x, k):
        return lambda q, t, *_: (sub_block(2 * t + k, q, x, n), 0)

    return call(
        kernel, after, prefetch=1, grid=(2, count // 2),
        in_specs=[pl.BlockSpec((size, d), place(x, k)) for x in range(2) for k in range(2)]
        + [whole(p.shape) for p in pieces],
        out_specs=[
            pl.BlockSpec((4 * size, d), lambda q, t, *_: (q * (count // 2) + t, 0)),
            pl.BlockSpec((4 * size, d), lambda q, t, *_: (t, q)),
        ],
        out_shape=[struct((2 * part, d), F32), struct((part, 2 * d), F32)],
        estimate=EST["move"], name="wide_both", mib=56,
    )(bits, stack, stack, stack, stack, *pieces)


class Links:
    def __init__(self, dp_size):
        self.size = dp_size
        self.bits = dp_size.bit_length() - 1
        index = lax.axis_index("dp")
        self.value = jnp.stack([(index >> i) & 1 for i in range(self.bits)]).astype(jnp.int32)

    def swap(self, value, at):
        return lax.ppermute(value, "dp", [(i, i ^ (1 << at)) for i in range(self.size)])

    def across(self, value):
        return lax.ppermute(value, "tensor", [(0, 1), (1, 0)])

    def join(self, mine, other, at, after=()):
        half, width = mine.shape
        if half % 16:
            low = self.value[at] == 0
            return jnp.concatenate([jnp.where(low, mine, other), jnp.where(low, other, mine)], 0)

        def moves(bits, ins, outs):
            return [
                (ins[0], outs[0].at[block(bits[at], half), :]), (ins[1], outs[0].at[block(1 - bits[at], half), :])
            ]

        return arrange(self.value, [mine, other], [(2 * half, width)], moves, "join", after)[0]


def halve(bits, parts, bit, after=()):
    count = len(parts)
    parts = lax.optimization_barrier((*parts, *after))[:count]
    size = parts[0].shape[0] // 2

    def half(at):
        return sum(lax.dynamic_slice_in_dim(v, at * size, size, 0).astype(F32) for v in parts).astype(BF)

    return half(1 - bits[bit]), half(bits[bit])


class Halve:
    def __init__(self, links, keep, recv):
        self.links, self.keep, self.recv, self.at = links, keep, recv, 0
        low = min(links.bits, BLOCK_BITS)
        self.order = [*range(low), *reversed(range(low, links.bits))]
        self.done = False

    def advance(self, after):
        links = self.links
        self.at += 1
        self.done = self.at == links.bits
        if self.done:
            return
        bit = self.order[self.at]
        send, self.keep = halve(links.value, (self.keep, self.recv), bit, after)
        self.recv = links.swap(send, bit)


RIDE = 32


def ride_kernel(rows, cut, bits_ref, *refs):
    *ins, small_ref, send_ref, keep_ref, next_ref, acc = refs
    width = small_ref.shape[1]
    small = small_ref[...]
    total = None
    for ref in ins:
        value = ref[0:rows, :].astype(F32)
        total = value if total is None else total + value
        if ref.shape[0] > rows:
            riding = ref[rows : rows + RIDE, :].astype(F32)
            small = small + riding[0:8] + riding[8:16] + riding[16:24]
    next_ref[...] = small
    if send_ref is None:
        keep_ref[...] = total.astype(BF)
        return
    acc[...] = total
    if cut is None:
        size = rows
        send_ref[0:size, :] = total.astype(BF)
        keep_ref[...] = total.astype(BF)
    else:
        size = rows // 2
        bit = bits_ref[cut]
        low, high = acc[0:size, :], acc[size : 2 * size, :]
        send_ref[0:size, :] = jnp.where(bit == 0, high, low).astype(BF)
        keep_ref[...] = jnp.where(bit == 0, low, high).astype(BF)
    parts = [p.astype(BF) for p in split3(small)] + [jnp.zeros((RIDE - 24, width), BF)]
    send_ref[size:, :] = jnp.concatenate(parts, 0)


def ride(bits, parts, small, cut, last, after=()):
    rows = parts[0].shape[0]
    width = small.shape[1]
    size = rows // 2 if cut is not None else rows
    shapes = [struct((size, width), BF), struct(small.shape, F32)]
    if not last:
        shapes.insert(0, struct((size + RIDE, width), BF))

    def kernel(bits_ref, *refs):
        refs = list(refs)
        if last:
            refs.insert(len(parts) + 1, None)
        ride_kernel(rows, cut, bits_ref, *refs)

    out = call(
        kernel, after, prefetch=1, in_specs=[whole(a.shape) for a in (*parts, small)],
        out_specs=[whole_out(t.shape) for t in shapes], out_shape=shapes,
        scratch=[pltpu.VMEM((rows, width), F32)], estimate=EST["move"], name="ride",
    )(bits, *parts, small)
    return (None, *out) if last else out


def layer(
    dp_size, inputs, lengths, norm1_gain, norm1_shift, query_weight, query_bias, key_weight, key_bias, value_weight,
    value_bias, out_weight, out_bias, norm2_gain, norm2_shift, up_weight, up_bias, down_weight, down_bias, out_grad,
):
    rows, d = inputs.shape
    width = query_weight.shape[1]
    ff = up_weight.shape[1]
    part = ff // 2
    links = Links(dp_size)
    bits = links.value
    tensor = lax.axis_index("tensor")
    length = jnp.where(tensor == 0, lengths[:1], lengths[1:])
    cos, sin = (jnp.asarray(t) for t in rotary_tables(rows))
    at = Row(d, width, ff)
    vec = [norm1_gain, norm1_shift, out_bias, norm2_gain, norm2_shift, down_bias, query_bias, key_bias, value_bias, up_bias]
    vec = jnp.concatenate([v.reshape(1, -1) for v in vec], 1)

    def qkv_moves(bits_ref, ins, outs):
        return [
            (w.at[block(bits_ref[0], d // 2), :], outs[0].at[:, i * width : (i + 1) * width]) for i, w in enumerate(ins)
        ]

    near_rows = 5 * d // 12
    half = width // 2
    def cut_moves(bits_ref, ins, outs):
        c, b = bits_ref[0], bits_ref[1]
        wu, wd = ins
        near, rest = outs
        cols = block(c, part)
        return [
            (wu.at[block(b, near_rows), cols], near),
            (wu.at[2 * near_rows :, cols], rest.at[0 : d - 2 * near_rows, :]),
            (wd.at[block(c, part), :], rest.at[d - 2 * near_rows :, :]),
        ]

    qkv_mine, = arrange(bits, [query_weight, key_weight, value_weight], [(d // 2, 3 * width)], qkv_moves, "cut_qkv", mib=56)
    qkv_mine = links.across(qkv_mine)
    normed, normed_t, *own, ctx_own, aug_own, near, rest = heads_own(
        at, cut_moves, [(near_rows, d), (d + part - 2 * near_rows, d)], bits, length, inputs, vec, query_weight,
        key_weight, value_weight, cos, sin, up_weight, down_weight,
    )
    bias_x = links.across(vec)
    near, out_x = links.across(near), links.across(out_weight)
    qkv_mine, _ = lax.optimization_barrier((qkv_mine, ctx_own))
    qkv_far = links.swap(qkv_mine, 0)
    *other, ctx_x, aug_x = heads_other(at, bits, length, normed, qkv_mine, qkv_far, bias_x, cos, sin, after=(ctx_own,))
    near, out_x, rest, ctx_x = lax.optimization_barrier((near, out_x, rest, ctx_x))
    rest = links.across(rest)
    near_x = links.swap(near, 1)
    near_far = links.swap(near, 0)
    mid, n2, n2t, out1, dn1, w_send, w_keep, dbu = ffn_own(
        at, bits, inputs, ctx_own, ctx_x, out_weight, out_x, vec, out_grad, up_weight, down_weight
    )

    w_recv = links.swap(w_send, 0)
    near_x_far, rest_far = links.swap(near_x, 0), links.swap(rest, 0)
    out2, dn2, stack, dbu_mine = ffn_mine(bits, n2, near, near_x, rest, bias_x, out_grad, n2t, after=(mid,))
    own_sum = Halve(links, w_keep, w_recv)
    own_sum.advance((out2,))
    layer_out, gm, g_own, g_x, stack, dwo, dwo_x, sums2, dbu_far = ffn_far(
        at, bits, length, n2, near_far, near_x_far, rest_far, bias_x, vec, out_grad, n2t, mid, out1, dn1, out2, dn2,
        ctx_own, ctx_x, out_weight, out_x, stack, after=(own_sum.keep,),
    )
    blocks = min(dp_size, 1 << BLOCK_BITS)

    def turned(rows_, first, second):
        return rows_.reshape(first, second, -1, d).swapaxes(0, 1).reshape(-1, d)

    if dp_size > blocks:
        stack = turned(stack, blocks, dp_size // blocks)
    stack = lax.psum_scatter(stack, "dp", scatter_dimension=0, tiled=True)
    n = d // 2
    gx, sums_x, qx_s, qx_k = attend_back(
        bits, length, *other, g_x, ctx_x, aug_x, cos, sin, normed_t, dwo_x
    )
    qx_r = links.swap(qx_s, 0)
    own_sum.advance((qx_k,))
    share = input_share(bits, gx, qkv_mine, qkv_far, after=(own_sum.keep,))
    qx_k, qx_r, _ = lax.optimization_barrier((qx_k, qx_r, share))
    qx = (qx_k.astype(F32) + qx_r.astype(F32)).astype(BF)
    qx_y = links.across(qx)
    go, sums_o, qo_s, qo_k = attend_back(
        bits, length, *own, g_own, ctx_own, aug_own, cos, sin, normed_t, dwo, after=(qx,), est=12
    )
    own_sum.advance((qo_k,))
    qo_r = links.swap(qo_s, 0)
    input_grad_out, sums1 = input_grad(
        at, inputs, gm, vec, go, share, query_weight, key_weight, value_weight, after=(own_sum.keep,)
    )
    q, = fold(bits, [(qo_k, 0, 0, n), (qx_y, 0, 0, n)], n, [(0, n)], "fold_qkv_y", after=(sums1,))
    q_s, q_k = halve(bits, (q, qo_r), 1)
    q_r = links.swap(q_s, 1)
    stack, q_k = lax.optimization_barrier((stack, q_k))
    stack_r = links.across(stack)
    c = bits[0]
    halves = lambda a, b: [jnp.where(tensor == 0, a, b), jnp.where(tensor == 0, b, a)]
    mine_up, far_up = jnp.where(c == 0, dbu_mine, dbu_far), jnp.where(c == 0, dbu_far, dbu_mine)
    small = jnp.concatenate(
        [sums1[:2].reshape(-1), sums2[:4].reshape(-1)]
        + halves(
            jnp.concatenate([v.reshape(-1) for v in (sums_o, dbu)]),
            jnp.concatenate([v.reshape(-1) for v in (sums_x, mine_up, far_up)]),
        )
    )
    used = small.shape[0]
    cols = q_k.shape[1]
    small = jnp.pad(small, (0, 8 * cols - used)).reshape(8, cols)

    last = links.bits - 1
    send, keep1, small = ride(bits, [q_k, q_r], small, 2 if last > 2 else None, False, (q_k,))
    q_parts = [keep1, links.swap(send, 2)]
    while not own_sum.done:
        own_sum.advance((keep1,))
    size = stack.shape[0]
    parts = [(v, 0, 0, size) for v in (stack, stack_r, own_sum.keep, own_sum.recv)][1:]
    split = dp_size == blocks
    cuts = [(0, size // 2), (size // 2, size // 2)] if split else [(0, size)]
    stack, *piece = fold(bits, parts, size, cuts, "fold_stack", after=(keep1,))
    gathered = lax.all_gather(stack, "dp", axis=0, tiled=True)
    if dp_size > blocks:
        gathered = turned(gathered, dp_size // blocks, blocks)
    piece_r = links.swap(piece[0], last) if split else None

    after = (stack,)
    parts = q_parts
    for bit in range(3, links.bits):
        send, keep, small = ride(bits, parts, small, bit if bit < last else None, False, after)
        after = ()
        parts = [keep, links.swap(send, bit)]
    if split:
        piece = piece[0]
        for bit in reversed(range(2, links.bits)):
            piece = links.join(piece, piece_r, bit, after=(keep,))
            piece_r = links.swap(piece, bit - 1)
        after = (piece,)
    _, q, small = ride(bits, parts, small, None, True, after)
    for bit in reversed(range(2, last)):
        q_r = links.swap(q, bit)
        if bit == last - 1:
            size = small.shape[0]
            for swap in (links.across, lambda v: links.swap(v, 0), lambda v: links.swap(v, 1)):
                parts = [(small, 0, 0, size), (swap(small), 0, 0, size)]
                small, = fold(bits, parts, size, [(0, size)], "fold_small", after=(q,))
        q = links.join(q, q_r, bit, after=(small,))
    q_r = links.swap(q, 1)
    q_far = links.swap(q, 0)
    if split:
        pieces = [piece, piece_r, links.swap(piece, 0), links.swap(piece_r, 0)]
        grad_down, grad_up = wide_both(bits, gathered, pieces, after=(q,))
    else:
        grad_down, grad_up = wide_ffn(bits, gathered, after=(q,))
    q_r, grad_up = lax.optimization_barrier((q_r, grad_up))
    q_r_far = links.swap(q_r, 0)
    grad_q, grad_k, grad_v, grad_out = wide_qkv(bits, (q, q_r), (q_far, q_r_far), after=(grad_up,))

    small = small.reshape(-1)
    gain1, shift1, out_b, gain2, shift2, down_b = (small[i * d : (i + 1) * d] for i in range(6))
    side = 3 * width + ff
    mine = lax.dynamic_slice_in_dim(small, 6 * d + tensor * side, side, 0)
    qkv_bias = mine[: 3 * width].reshape(-1, 3, 128)
    return (
        layer_out, input_grad_out, gain1, shift1,
        grad_q, qkv_bias[:, 0].reshape(-1), grad_k, qkv_bias[:, 1].reshape(-1), grad_v, qkv_bias[:, 2].reshape(-1),
        grad_out, out_b, gain2, shift2, grad_up, mine[3 * width :], grad_down, down_b,
    )


def solution(mesh):
    rows = P(("dp", "tensor"), None)
    cols = P(None, "tensor")
    tens = P("tensor")
    return jax.shard_map(
        lambda *args: layer(mesh.shape["dp"], *args),
        mesh=mesh,
        in_specs=(
            rows, P("dp"), P(), P(), cols, tens, cols, tens, cols, tens, P("tensor", None), P(), P(), P(), cols, tens,
            P("tensor", None), P(), rows,
        ),
        out_specs=(
            rows, rows, P(), P(), cols, tens, cols, tens, cols, tens, P("tensor", None), P(), P(), P(), cols, tens,
            P("tensor", None), P(),
        ),
        check_vma=False,
    )
```

```python
import math

import jax
import jax.numpy as jnp
import numpy as np
from jax import lax
from jax.experimental import pallas as pl
from jax.experimental.pallas import tpu as pltpu
from jax.sharding import PartitionSpec as P

HEAD_DIM = 64
EPS = 1e-05
LOG2E = math.log2(math.e)
LN2 = math.log(2.0)
F32 = jnp.float32
BF = jnp.bfloat16
BIG = -1e30


def dot(a, b, ca=1, cb=0):
    return lax.dot_general(a, b, (((ca,), (cb,)), ((), ())), preferred_element_type=F32)


def cost(macs, nbytes, exps=0):
    return pl.CostEstimate(flops=int(2 * macs), bytes_accessed=int(nbytes), transcendentals=int(exps))


def busy(micros):
    return pl.CostEstimate(flops=int(micros * 1.1e9), bytes_accessed=1000, transcendentals=0)


EST = {
    "move": busy(0.01),
    "heads_own": busy(16),
    "heads_other": busy(100),
    "ffn_own": busy(0.01),
    "ffn_mine": busy(100),
    "ffn_far": busy(100),
    "share": busy(8),
    "input_grad": busy(8),
    "halve": busy(20),
}


def struct(shape, dtype):
    return jax.ShapeDtypeStruct(shape, dtype)


def whole(shape):
    return pl.BlockSpec(shape, lambda *_: (0,) * len(shape), pipeline_mode=pl.Buffered(1))


def whole_out(shape):
    return pl.BlockSpec(shape, lambda *_: (0,) * len(shape))


ANY = pl.BlockSpec(memory_space=pl.ANY)


def call(kernel, after, *, in_specs, out_specs, out_shape, estimate, name, grid=(1,), prefetch=0, scratch=(), alias=None, mib=28):
    after = tuple(after)
    n_in = prefetch + len(in_specs)

    def body(*refs):
        kernel(*refs[:n_in], *refs[n_in + len(after) :])

    run = pl.pallas_call(
        body,
        grid_spec=pltpu.PrefetchScalarGridSpec(
            num_scalar_prefetch=prefetch,
            grid=grid,
            in_specs=list(in_specs) + [ANY] * len(after),
            out_specs=out_specs,
            scratch_shapes=list(scratch),
        ),
        out_shape=out_shape,
        compiler_params=pltpu.CompilerParams(vmem_limit_bytes=mib << 20),
        input_output_aliases=alias or {},
        cost_estimate=estimate,
        name=name,
    )
    return lambda *args: run(*args, *after)


def norm_rows(v):
    mean = jnp.mean(v, axis=1, keepdims=True)
    cent = v - mean
    var = jnp.mean(cent * cent, axis=1, keepdims=True)
    r = lax.rsqrt(var + EPS)
    return cent * r, r


def norm_back(e, n, r):
    return r * (e - jnp.mean(e, axis=1, keepdims=True) - n * jnp.mean(e * n, axis=1, keepdims=True))


def rotary_tables(rows):
    half = HEAD_DIM // 2
    freq = (10000.0 ** (-2.0 * np.arange(half, dtype=np.float32) / HEAD_DIM)).astype(np.float32)
    ang = (np.arange(rows, dtype=np.float32)[:, None] * freq[None, :]).astype(np.float64)
    cos = np.cos(ang).astype(np.float32)
    sin = np.sin(ang).astype(np.float32)
    return np.concatenate([cos] * 4, 1), np.concatenate([-sin, sin] * 2, 1)


def swap_halves(v):
    lane = lax.broadcasted_iota(jnp.int32, v.shape, 1)
    return jnp.where((lane & 32) == 0, pltpu.roll(v, 96, 1), pltpu.roll(v, 32, 1))


def rotate(v, cos, sin):
    return v * cos + swap_halves(v) * sin


def rotate_back(v, cos, sin):
    return v * cos - swap_halves(v) * sin


class Row:
    def __init__(self, d, width, ff):
        at = 0
        for name, size in (
            ("gain1", d), ("shift1", d), ("out_bias", d), ("gain2", d), ("shift2", d), ("down_bias", d),
            ("qkv", 3 * width), ("up", ff),
        ):
            setattr(self, name, slice(at, at + size))
            at += size


def pull(src, dst, sem):
    copy = pltpu.make_async_copy(src, dst, sem)
    copy.start()
    return copy


def arrange(bits, arrays, shapes, moves, name, after=(), mib=28):
    def kernel(bits_ref, *refs):
        ins, outs, sem = refs[: len(arrays)], refs[len(arrays) : -1], refs[-1]
        copies = [pull(src, dst, sem.at[i]) for i, (src, dst) in enumerate(moves(bits_ref, ins, outs))]
        for copy in copies:
            copy.wait()

    return call(
        kernel,
        after,
        prefetch=1,
        in_specs=[ANY] * len(arrays),
        out_specs=[whole_out(shape) for shape in shapes],
        out_shape=[struct(shape, BF) for shape in shapes],
        scratch=[pltpu.SemaphoreType.DMA((8,))],
        estimate=EST["move"],
        name=name,
        mib=mib,
    )(bits, *arrays)


def block(bit, size):
    return pl.ds(pl.multiple_of(bit * size, size), size)


def fold(bits, parts, rows, outs, name, after=(), width=None, est=EST["move"]):
    arrays = [p[0] for p in parts]
    width = width or arrays[0].shape[1]
    dtype = arrays[0].dtype
    half = rows // 2
    shapes = [(half, width)] * 2 if isinstance(outs, int) else [(n, width) for _, n in outs]

    def kernel(bits_ref, *refs):
        ins, outs_r, acc = refs[: len(parts)], refs[len(parts) : -1], refs[-1]
        seen = []
        for ref, (_, src, dst, n) in zip(ins, parts):
            value = ref[src : src + n, 0:width].astype(F32)
            fresh = not any(dst < b and a < dst + n for a, b in seen)
            acc[dst : dst + n, :] = value if fresh else acc[dst : dst + n, :] + value
            seen.append((dst, dst + n))
        if isinstance(outs, int):
            bit = bits_ref[outs]
            for ref, at in zip(outs_r, (1 - bit, bit)):
                ref[...] = acc[pl.ds(pl.multiple_of(at * half, 8 if half % 8 == 0 else 1), half), :].astype(dtype)
        else:
            for ref, (start, n) in zip(outs_r, outs):
                ref[...] = acc[start : start + n, :].astype(dtype)

    return call(
        kernel,
        after,
        prefetch=1,
        in_specs=[whole(a.shape) for a in arrays],
        out_specs=[whole_out(shape) for shape in shapes],
        out_shape=[struct(shape, dtype) for shape in shapes],
        scratch=[pltpu.VMEM((rows, width), F32)],
        estimate=est,
        name=name,
    )(bits, *arrays)


def put_qkv(pre, cos, sin, q_ref, k_ref, v_ref):
    width = q_ref.shape[1]
    for i in range(width // 128):
        sl = slice(i * 128, (i + 1) * 128)
        q_ref[:, sl] = (rotate(pre[0][:, sl], cos, sin) * (LOG2E / 8.0)).astype(BF)
        k_ref[:, sl] = rotate(pre[1][:, sl], cos, sin).astype(BF)
        v_ref[:, sl] = pre[2][:, sl].astype(BF)


def split3(v):
    hi = v.astype(BF)
    rest = v - hi.astype(F32)
    mid = rest.astype(BF)
    lo = rest - mid.astype(F32)
    return hi.astype(F32), mid.astype(F32), lo


def spread(lane, first, one, two):
    out = jnp.where(lane == 0, first, 0.0)
    for at, part in enumerate((*split3(one), *split3(two))):
        out = jnp.where(lane == at + 1, part, out)
    return out.astype(BF)


def attend_pair(length, q_ref, k_ref, v_ref, ctx_ref, aug_ref):
    bq = 256
    rows = q_ref.shape[0]
    lane1 = lax.broadcasted_iota(jnp.int32, (1, 128), 1)
    krow = lax.broadcasted_iota(jnp.int32, (rows, 128), 0)
    klane = lax.broadcasted_iota(jnp.int32, (rows, 128), 1)
    lane = lax.broadcasted_iota(jnp.int32, (bq, 128), 1)
    qrow = lax.broadcasted_iota(jnp.int32, (bq, 128), 0)
    kaug = jnp.where((klane == 0) & (krow >= length), BIG, 0.0).astype(BF)
    k = jnp.concatenate([k_ref[...], kaug], 1)
    v = jnp.concatenate([v_ref[...], jnp.ones((rows, 128), BF)], 1)
    qaug = jnp.where(lane == 0, 1.0, 0.0).astype(BF)
    for i in range(rows // bq):
        sl = slice(i * bq, (i + 1) * bq)
        q = q_ref[sl, :]
        outs, totals = [], []
        for h in range(2):
            keep = ((lane1 < 64) if h == 0 else (lane1 >= 64)).astype(BF)
            s = dot(jnp.concatenate([q * keep, qaug], 1), k, 1, 1)
            top = jnp.max(s, axis=1, keepdims=True)
            p = jnp.exp2(s - top).astype(BF)
            o = dot(p, v)
            total = o[:, 128:]
            outs.append(o[:, :128] / total)
            totals.append(top + jnp.log2(total))
        ctx = jnp.where(lane < 64, outs[0], outs[1])
        ctx_ref[sl, :] = jnp.where(qrow + i * bq < length, ctx, 0.0).astype(BF)
        aug_ref[sl, :] = spread(lane, 1.0, totals[0], totals[1])


def attend_all(length, q, k, v, ctx, aug):
    for p in range(q.shape[1] // 128):
        sl = slice(p * 128, (p + 1) * 128)
        attend_pair(length, *(ref.at[:, sl] for ref in (q, k, v, ctx, aug)))


def heads_own_kernel(
    at, cut, bits_ref, len_ref, x_ref, vec_ref, wq_ref, wk_ref, wv_ref, cos_ref, sin_ref, wu_h, wd_h,
    n_h, nt_h, q_h, k_h, v_h, ctx_h, aug_h, near_h, rest_h,
    n_s, nt_s, q_s, k_s, v_s, ctx_s, aug_s, near_s, rest_s, sem,
):
    rows = x_ref.shape[0]
    width = q_s.shape[1]
    loads = [
        pull(src, dst, sem.at[i]) for i, (src, dst) in enumerate(cut(bits_ref, (wu_h, wd_h), (near_s, rest_s)))
    ]
    blk = 256
    bias = vec_ref[:, at.qkv]
    for i in range(rows // blk):
        sl = slice(i * blk, (i + 1) * blk)
        n, _ = norm_rows(x_ref[sl, :].astype(F32))
        low = (n * vec_ref[:, at.gain1] + vec_ref[:, at.shift1]).astype(BF)
        n_s[sl, :] = low
        nt_s[:, sl] = low.T
        pre = [
            dot(low, w[...]) + bias[:, j * width : (j + 1) * width] for j, w in enumerate((wq_ref, wk_ref, wv_ref))
        ]
        put_qkv(pre, cos_ref[sl, :], sin_ref[sl, :], *(ref.at[sl, :] for ref in (q_s, k_s, v_s)))
    for load in loads:
        load.wait()
    pairs = [
        (near_s, near_h), (rest_s, rest_h), (n_s, n_h), (nt_s, nt_h), (q_s, q_h), (k_s, k_h), (v_s, v_h)
    ]
    stores = [pull(src, dst, sem.at[8 + i]) for i, (src, dst) in enumerate(pairs)]
    attend_all(len_ref[0], q_s, k_s, v_s, ctx_s, aug_s)
    stores += [pull(ctx_s, ctx_h, sem.at[15]), pull(aug_s, aug_h, sem.at[16])]
    for store in stores:
        store.wait()


def heads_own(at, cut, shapes, bits, length, x, vec, wq, wk, wv, cos, sin, wu, wd, after=()):
    rows, d = x.shape
    width = wq.shape[1]
    outs = [(rows, d), (d, rows)] + [(rows, width)] * 5 + list(shapes)
    return call(
        lambda *refs: heads_own_kernel(at, cut, *refs),
        after,
        prefetch=2,
        in_specs=[whole(a.shape) for a in (x, vec, wq, wk, wv, cos, sin)] + [ANY] * 2,
        out_specs=[ANY] * len(outs),
        out_shape=[struct(shape, BF) for shape in outs],
        scratch=[pltpu.VMEM(shape, BF) for shape in outs] + [pltpu.SemaphoreType.DMA((17,))],
        estimate=EST["heads_own"],
        name="heads_own",
        mib=56,
    )(bits, length, x, vec, wq, wk, wv, cos, sin, wu, wd)


def heads_other_kernel(
    at, bits_ref, len_ref, n_ref, wm_ref, wf_ref, b_ref, cos_ref, sin_ref, q_h, k_h, v_h, ctx_h, aug_h,
    q_s, k_s, v_s, ctx_s, aug_s, sem,
):
    rows = n_ref.shape[0]
    width = q_s.shape[1]
    half = wm_ref.shape[0]
    c = bits_ref[0]
    blk = 256
    for i in range(rows // blk):
        sl = slice(i * blk, (i + 1) * blk)
        pre = dot(n_ref[sl, block(c, half)], wm_ref[...]) + dot(n_ref[sl, block(1 - c, half)], wf_ref[...])
        pre = pre + b_ref[:, at.qkv]
        put_qkv(
            [pre[:, j * width : (j + 1) * width] for j in range(3)], cos_ref[sl, :], sin_ref[sl, :],
            *(ref.at[sl, :] for ref in (q_s, k_s, v_s)),
        )
    stores = [pull(src, dst, sem.at[i]) for i, (src, dst) in enumerate(((q_s, q_h), (k_s, k_h), (v_s, v_h)))]
    attend_all(len_ref[0], q_s, k_s, v_s, ctx_s, aug_s)
    stores += [pull(ctx_s, ctx_h, sem.at[3]), pull(aug_s, aug_h, sem.at[4])]
    for store in stores:
        store.wait()


def heads_other(at, bits, length, n, w_mine, w_far, bias, cos, sin, after=()):
    rows = n.shape[0]
    width = w_mine.shape[1] // 3
    outs = [(rows, width)] * 5
    return call(
        lambda *refs: heads_other_kernel(at, *refs),
        after,
        prefetch=2,
        in_specs=[whole(a.shape) for a in (n, w_mine, w_far, bias, cos, sin)],
        out_specs=[ANY] * 5,
        out_shape=[struct(shape, BF) for shape in outs],
        scratch=[pltpu.VMEM(shape, BF) for shape in outs] + [pltpu.SemaphoreType.DMA((5,))],
        estimate=EST["heads_other"],
        name="heads_other",
        mib=56,
    )(bits, length, n, w_mine, w_far, bias, cos, sin)


def attend_back_kernel(
    bq, bits_ref, len_ref, q_ref, k_ref, v_ref, g_ref, ctx_ref, aug_ref, cos_ref, sin_ref, nt_ref, wo_ref,
    d_ref, sum_ref, send_ref, keep_ref, dqt, dall, gaug,
):
    rows = q_ref.shape[0]
    length = len_ref[0]
    lane1 = lax.broadcasted_iota(jnp.int32, (1, 128), 1)
    krow = lax.broadcasted_iota(jnp.int32, (rows, 128), 0)
    klane = lax.broadcasted_iota(jnp.int32, (rows, 128), 1)
    lane = lax.broadcasted_iota(jnp.int32, (bq, 128), 1)
    k = k_ref[...]
    v = v_ref[...]
    kt = k.T
    dks, dvs = [], []
    for h in range(2):
        keep = ((lane1 < 64) if h == 0 else (lane1 >= 64)).astype(BF)
        first = 1 + 3 * h
        mine = jnp.where((klane >= first) & (klane < first + 3), -1.0, 0.0)
        kaug = jnp.where((klane == 0) & (krow >= length), BIG, mine).astype(BF)
        kh = jnp.concatenate([k * keep, kaug], 1)
        vh = jnp.concatenate([v * keep, mine.astype(BF)], 1)
        dk = jnp.zeros((rows, 128), F32)
        dv = jnp.zeros((rows, 128), F32)
        for i in range(rows // bq):
            sl = slice(i * bq, (i + 1) * bq)
            q = q_ref[sl, :]
            g = g_ref[sl, :]
            if h == 0:
                prod = g.astype(F32) * ctx_ref[sl, :].astype(F32)
                d0 = jnp.sum(jnp.where(lane < 64, prod, 0.0), 1, keepdims=True)
                d1 = jnp.sum(jnp.where(lane < 64, 0.0, prod), 1, keepdims=True)
                gaug[sl, :] = spread(lane, 0.0, d0, d1)
            st = dot(kh, jnp.concatenate([q, aug_ref[sl, :]], 1), 1, 1)
            pt = jnp.exp2(st)
            dpt = dot(vh, jnp.concatenate([g, gaug[sl, :]], 1), 1, 1)
            ds = (pt * dpt).astype(BF)
            dv = dv + dot(pt.astype(BF), g)
            dk = dk + dot(ds, q)
            dqt[h * 64 : (h + 1) * 64, sl] = dot(kt[h * 64 : (h + 1) * 64, :], ds)
        dks.append(dk)
        dvs.append(dv)
    cos = cos_ref[...]
    sin = sin_ref[...]
    dq = rotate_back(dqt[...].T * (1.0 / 8.0), cos, sin).astype(BF)
    dk = rotate_back(jnp.where(klane < 64, dks[0], dks[1]) * LN2, cos, sin).astype(BF)
    dv = jnp.where(klane < 64, dvs[0], dvs[1]).astype(BF)
    for at, val in enumerate((dq, dk, dv)):
        sl = slice(at * 128, (at + 1) * 128)
        d_ref[:, sl] = val
        sum_ref[:, sl] = jnp.sum(val.astype(F32), axis=0, keepdims=True)
    j = pl.program_id(0)
    dall[:, block(j, 384)] = jnp.concatenate([dq, dk, dv], 1)

    @pl.when(j == pl.num_programs(0) - 1)
    def _():
        half = send_ref.shape[0]
        c = bits_ref[0]
        for ref, part in ((send_ref, 1 - c), (keep_ref, c)):
            width = dall.shape[1]
            ref[:, 0:width] = dot(nt_ref[block(part, half), :], dall[...]).astype(BF)
            ref[:, width:] = wo_ref[block(part, half), :]


def attend_back(bits, length, q, k, v, g, ctx, aug, cos, sin, nt, wo, after=(), est=100):
    rows, width = q.shape
    d = 2 * width
    bs = pl.BlockSpec((rows, 128), lambda j, *_: (0, j))
    return call(
        lambda *refs: attend_back_kernel(256, *refs),
        after,
        prefetch=2,
        grid=(width // 128,),
        in_specs=[bs] * 6 + [whole((rows, 128))] * 2 + [whole(nt.shape), whole(wo.shape)],
        out_specs=[pl.BlockSpec((rows, 384), lambda j, *_: (0, j)), pl.BlockSpec((1, 384), lambda j, *_: (0, j))]
        + [whole_out((d // 2, 4 * width))] * 2,
        out_shape=[struct((rows, 3 * width), BF), struct((1, 3 * width), F32)] + [struct((d // 2, 4 * width), BF)] * 2,
        scratch=[pltpu.VMEM((128, rows), F32), pltpu.VMEM((rows, 3 * width), BF), pltpu.VMEM((rows, 128), BF)],
        estimate=busy(est),
        name="attend_back",
        mib=56,
    )(bits, length, q, k, v, g, ctx, aug, cos, sin, nt, wo)


def gelu_pair(h):
    z = jnp.abs(h) * (0.3275911 / math.sqrt(2.0)) + 1.0
    t = pl.reciprocal(z, approx=True)
    t = t * (2.0 - z * t)
    e = jnp.exp2(h * h * (-0.5 * LOG2E))
    poly = 0.5 * 1.061405429 * t - 0.5 * 1.453152027
    poly = poly * t + 0.5 * 1.421413741
    poly = poly * t - 0.5 * 0.284496736
    poly = poly * t + 0.5 * 0.254829592
    w = poly * t * e
    cdf = jnp.where(h >= 0.0, 1.0 - w, w)
    return h * cdf, cdf + h * e * (1.0 / math.sqrt(2.0 * math.pi))


def ffn_quarter(n2, n2t, og, wu, wd, bias, out_acc, dn_acc, act_s, dh_s, gd, gu, first, before=None, done=None):
    rows, d = og.shape
    part = wd.shape[0]
    blk = 256
    dbias = jnp.zeros((1, part), F32)
    if before is not None:
        before(0, blk)
    for i in range(rows // blk):
        sl = slice(i * blk, (i + 1) * blk)
        if before is not None and i + 1 < rows // blk:
            before(i + 1, blk)
        h = dot(n2[sl, :], wu[...]) + bias
        act, slope = gelu_pair(h)
        act = act.astype(BF)
        dh = (slope * dot(og[sl, :], wd[...], 1, 1)).astype(BF)
        act_s[sl, :] = act
        dh_s[sl, :] = dh
        dbias = dbias + jnp.sum(dh.astype(F32), axis=0, keepdims=True)
        o = dot(act, wd[...])
        e = dot(dh, wu[...], 1, 1)
        out_acc[sl, :] = o if first else out_acc[sl, :] + o
        dn_acc[sl, :] = e if first else dn_acc[sl, :] + e
        if done is not None and i > 0:
            done(i - 1, blk)
    if done is not None:
        done(rows // blk - 1, blk)
    gd[...] = dot(act_s[...], og[...], 0, 0).astype(BF)
    gu[...] = dot(n2t[...], dh_s[...]).astype(BF)
    return dbias


def ffn_own_kernel(
    at, bits_ref, x_ref, co_ref, cx_ref, woo_ref, wox, vec_ref, og_h, wu_h, wd_h,
    mid_h, n2_h, n2t_h, out_h, dn_h, send_h, keep_h, db_ref,
    og, wu, wd, mid, n2, n2t, out, dn, outb, dnb, act_s, dh_s, gd, gu, sem,
):
    rows, d = x_ref.shape
    part = wu_h.shape[1] // 2
    c = bits_ref[0]
    cols = [block(p, part) for p in (1 - c, c)]
    biases = [pl.ds(pl.multiple_of(at.up.start + p * part, 128), part) for p in (1 - c, c)]
    loads = [pull(og_h, og, sem.at[0])]
    for q in range(2):
        loads.append(pull(wu_h.at[:, cols[q]], wu.at[q], sem.at[1 + 2 * q]))
        loads.append(pull(wd_h.at[cols[q], :], wd.at[q], sem.at[2 + 2 * q]))
    stores = []

    def enter(i, blk):
        sl = slice(i * blk, (i + 1) * blk)
        att = dot(co_ref[sl, :], woo_ref[...]) + dot(cx_ref[sl, :], wox[...])
        v = x_ref[sl, :].astype(F32) + att + vec_ref[:, at.out_bias]
        mid[sl, :] = v
        n, _ = norm_rows(v)
        low = (n * vec_ref[:, at.gain2] + vec_ref[:, at.shift2]).astype(BF)
        n2[sl, :] = low
        n2t[:, sl] = low.T
        if i == 0:
            for load in loads:
                load.wait()
        if (i + 1) * blk == rows:
            stores.extend([pull(mid, mid_h, sem.at[5]), pull(n2, n2_h, sem.at[6]), pull(n2t, n2t_h, sem.at[7])])

    def flush(i, blk):
        sl = pl.ds(i * blk, blk)
        outb[sl, :] = out[sl, :].astype(BF)
        dnb[sl, :] = dn[sl, :].astype(BF)
        stores.append(pull(outb.at[sl, :], out_h.at[sl, :], sem.at[8 + i]))
        stores.append(pull(dnb.at[sl, :], dn_h.at[sl, :], sem.at[12 + i]))

    for q in range(2):
        db_ref[:, cols[q]] = ffn_quarter(
            n2, n2t, og, wu.at[q], wd.at[q], vec_ref[:, biases[q]], out, dn, act_s, dh_s, gd.at[q], gu.at[q], q == 0,
            enter if q == 0 else None, flush if q == 1 else None,
        )
        stores.append(pull(gd.at[q], (send_h, keep_h)[q].at[0:part, :], sem.at[16 + q]))
        stores.append(pull(gu.at[q], (send_h, keep_h)[q].at[part:, :], sem.at[20 + q]))
    for store in stores:
        store.wait()


def ffn_own(at, bits, x, ctx_own, ctx_other, wo_own, wo_other, vec, og, wu, wd, after=()):
    rows, d = x.shape
    ff = wu.shape[1]
    part = ff // 2
    half = ctx_own.shape[1]
    return call(
        lambda *refs: ffn_own_kernel(at, *refs),
        after,
        prefetch=1,
        in_specs=[
            whole((rows, d)), whole((rows, half)), whole((rows, half)), whole((half, d)), whole((half, d)), whole(vec.shape),
        ] + [ANY] * 3,
        out_specs=[ANY] * 7 + [whole_out((1, ff))],
        scratch=[
            pltpu.VMEM((rows, d), BF), pltpu.VMEM((2, d, part), BF), pltpu.VMEM((2, part, d), BF),
            pltpu.VMEM((rows, d), F32), pltpu.VMEM((rows, d), BF), pltpu.VMEM((d, rows), BF),
            pltpu.VMEM((rows, d), F32), pltpu.VMEM((rows, d), F32), pltpu.VMEM((rows, d), BF), pltpu.VMEM((rows, d), BF),
            pltpu.VMEM((rows, part), BF), pltpu.VMEM((rows, part), BF),
            pltpu.VMEM((2, part, d), BF), pltpu.VMEM((2, d, part), BF),
            pltpu.SemaphoreType.DMA((22,)),
        ],
        out_shape=[
            struct((rows, d), F32), struct((rows, d), BF), struct((d, rows), BF), struct((rows, d), BF),
            struct((rows, d), BF), struct((part + d, d), BF), struct((part + d, d), BF),
            struct((1, ff), F32),
        ],
        estimate=EST["ffn_own"],
        name="ffn_own",
        mib=56,
    )(bits, x, ctx_own, ctx_other, wo_own, wo_other, vec, og, wu, wd)


BLOCK_BITS = 4


def sub_block(s, q, x, n):
    out = q + 2 * x
    for k in range(2, n):
        out = out + (((s >> (n - 1 - k)) & 1) << k)
    return out


def put_blocks(grads, stack, q, n, sem, at):
    count = 1 << (n - 2)
    size = grads[0].shape[0] // count
    return [
        pull(
            grads[x].at[s * size : (s + 1) * size, :],
            stack.at[pl.ds(pl.multiple_of(sub_block(s, q, x, n) * size, size), size), :],
            sem.at[at + x * count + s],
        )
        for x in range(2)
        for s in range(count)
    ]


def gather_weights(bits_ref, near, near_x, rest, w, sem, at):
    rows = near.shape[0]
    b = bits_ref[1]
    return [
        pull(near, w.at[block(b, rows), :], sem.at[at]),
        pull(near_x, w.at[block(1 - b, rows), :], sem.at[at + 1]),
        pull(rest, w.at[2 * rows :, :], sem.at[at + 2]),
    ]


def ffn_mine_kernel(
    n, bits_ref, n2_ref, b_ref, near_h, near_x_h, rest_h, og_h, n2t_h, out_h, dn_h, stack_h, db_ref,
    w_ref, og, n2t, out, dn, outb, dnb, act_s, dh_s, gd, gu, sem,
):
    d = og.shape[1]
    part = w_ref.shape[0] - d
    c = bits_ref[0]
    bias_at = b_ref.shape[1] - 2 * part
    at = 10 + (1 << (n - 1))
    loads = gather_weights(bits_ref, near_h, near_x_h, rest_h, w_ref, sem, at)
    loads += [pull(og_h, og, sem.at[0]), pull(n2t_h, n2t, sem.at[1])]
    for load in loads:
        load.wait()
    stores = []

    def flush(i, blk):
        sl = pl.ds(i * blk, blk)
        outb[sl, :] = out[sl, :].astype(BF)
        dnb[sl, :] = dn[sl, :].astype(BF)
        stores.append(pull(outb.at[sl, :], out_h.at[sl, :], sem.at[2 + i]))
        stores.append(pull(dnb.at[sl, :], dn_h.at[sl, :], sem.at[6 + i]))

    bias = b_ref[:, pl.ds(pl.multiple_of(bias_at + c * part, 128), part)]
    db_ref[...] = ffn_quarter(
        n2_ref, n2t, og, w_ref.at[0:d, :], w_ref.at[d:, :], bias, out, dn, act_s, dh_s, gd, gu, True, None, flush
    )
    stores += put_blocks((gd, gu), stack_h, c, n, sem, 10)
    for store in stores:
        store.wait()


def ffn_mine(bits, n2, near, near_x, rest, bias, og, n2t, after=()):
    rows, d = og.shape
    part = 2 * near.shape[0] + rest.shape[0] - d
    n = min(bits.shape[0], BLOCK_BITS)
    return call(
        lambda *refs: ffn_mine_kernel(n, *refs),
        after,
        prefetch=1,
        in_specs=[whole((rows, d)), whole(bias.shape)] + [ANY] * 5,
        out_specs=[ANY] * 3 + [whole_out((1, part))],
        scratch=[
            pltpu.VMEM((d + part, d), BF),
            pltpu.VMEM((rows, d), BF), pltpu.VMEM((d, rows), BF), pltpu.VMEM((rows, d), F32), pltpu.VMEM((rows, d), F32),
            pltpu.VMEM((rows, d), BF), pltpu.VMEM((rows, d), BF),
            pltpu.VMEM((rows, part), BF), pltpu.VMEM((rows, part), BF), pltpu.VMEM((part, d), BF), pltpu.VMEM((d, part), BF),
            pltpu.SemaphoreType.DMA((13 + (1 << (n - 1)),)),
        ],
        out_shape=[
            struct((rows, d), BF), struct((rows, d), BF), struct((4 * part, d), BF), struct((1, part), F32),
        ],
        estimate=EST["ffn_mine"],
        name="ffn_mine",
        mib=56,
    )(bits, n2, bias, near, near_x, rest, og, n2t)


def ffn_far_kernel(
    at, n, bits_ref, len_ref, n2_ref, b_ref, vec_ref, near_h, near_x_h, rest_h, og_h, n2t_h, mid_h, out1_h, dn1_h, out2_h, dn2_h,
    co_h, cx_h, woo_h, wox_h, stack_in,
    lay_h, gm_h, dco_h, dcx_h, stack_h, dwoo_h, dwox_h, sums_ref, db_ref,
    w_ref, og, n2t, mid, out1, dn1, out2, dn2, co, cx, woo, wox, out, dn, act_s, dh_s, gd, gu, lay, gmb, dco, dcx, dwoo, dwox, sem,
):
    rows, d = og.shape
    part = w_ref.shape[0] - d
    half = co.shape[1]
    c = bits_ref[0]
    length = len_ref[0]
    bias_at = b_ref.shape[1] - 2 * part
    first = gather_weights(bits_ref, near_h, near_x_h, rest_h, w_ref, sem, 18 + (1 << (n - 1)))
    loads = [
        pull(src, dst, sem.at[i])
        for i, (src, dst) in enumerate((
            (og_h, og), (n2t_h, n2t), (mid_h, mid), (dn1_h, dn1), (dn2_h, dn2), (out1_h, out1), (out2_h, out2),
            (woo_h, woo), (wox_h, wox), (co_h, co), (cx_h, cx),
        ))
    ]
    for load in first + loads[:1]:
        load.wait()
    sums_ref[...] = jnp.zeros_like(sums_ref)
    stores = []

    def finish(i, blk):
        if i == 0:
            for load in loads[1:]:
                load.wait()
        sl = slice(i * blk, (i + 1) * blk)
        v = mid[sl, :]
        out_sum = out1[sl, :].astype(F32) + out2[sl, :].astype(F32) + out[sl, :]
        lay[sl, :] = (v + out_sum + vec_ref[:, at.down_bias]).astype(BF)
        unit, r = norm_rows(v)
        gn = dn1[sl, :].astype(F32) + dn2[sl, :].astype(F32) + dn[sl, :]
        o = og[sl, :].astype(F32)
        g = o + norm_back(gn * vec_ref[:, at.gain2], unit, r)
        mid[sl, :] = g
        low = g.astype(BF)
        gmb[sl, :] = low
        for k, val in enumerate((g, gn * unit, gn, o)):
            sums_ref[k : k + 1, :] += jnp.sum(val, axis=0, keepdims=True)
        valid = lax.broadcasted_iota(jnp.int32, (blk, 1), 0) + i * blk < length
        dco[sl, :] = jnp.where(valid, dot(low, woo[...], 1, 1), 0.0).astype(BF)
        dcx[sl, :] = jnp.where(valid, dot(low, wox[...], 1, 1), 0.0).astype(BF)

    bias = b_ref[:, pl.ds(pl.multiple_of(bias_at + (1 - c) * part, 128), part)]
    db_ref[...] = ffn_quarter(
        n2_ref, n2t, og, w_ref.at[0:d, :], w_ref.at[d:, :], bias, out, dn, act_s, dh_s, gd, gu, True, None, finish
    )
    stores = put_blocks((gd, gu), stack_h, 1 - c, n, sem, 18)
    stores += [
        pull(src, dst, sem.at[12 + k])
        for k, (src, dst) in enumerate(((lay, lay_h), (mid, gm_h), (dco, dco_h), (dcx, dcx_h)))
    ]
    dwoo[...] = dot(gmb[...], co[...], 0, 0).astype(BF)
    dwox[...] = dot(gmb[...], cx[...], 0, 0).astype(BF)
    stores += [pull(dwoo, dwoo_h, sem.at[16]), pull(dwox, dwox_h, sem.at[17])]
    for store in stores:
        store.wait()


def ffn_far(
    at, bits, length, n2, near, near_x, rest, bias, vec, og, n2t, mid, out1, dn1, out2, dn2, ctx_own, ctx_other, wo_own,
    wo_other, stack, after=(),
):
    rows, d = og.shape
    part = 2 * near.shape[0] + rest.shape[0] - d
    n = min(bits.shape[0], BLOCK_BITS)
    half = ctx_own.shape[1]
    bf = lambda *shape: pltpu.VMEM(shape, BF)
    f32 = lambda *shape: pltpu.VMEM(shape, F32)
    return call(
        lambda *refs: ffn_far_kernel(at, n, *refs),
        after,
        prefetch=2,
        in_specs=[whole((rows, d)), whole(bias.shape), whole(vec.shape)] + [ANY] * 15,
        out_specs=[ANY] * 7 + [whole_out((8, d)), whole_out((1, part))],
        scratch=[
            bf(d + part, d), bf(rows, d), bf(d, rows), f32(rows, d), bf(rows, d), bf(rows, d), bf(rows, d), bf(rows, d),
            bf(rows, half), bf(rows, half), bf(half, d), bf(half, d), f32(rows, d), f32(rows, d),
            bf(rows, part), bf(rows, part), bf(part, d), bf(d, part), bf(rows, d), bf(rows, d), bf(rows, half),
            bf(rows, half), bf(d, half), bf(d, half), pltpu.SemaphoreType.DMA((21 + (1 << (n - 1)),)),
        ],
        out_shape=[
            struct((rows, d), BF), struct((rows, d), F32), struct((rows, half), BF), struct((rows, half), BF),
            struct(stack.shape, BF), struct((d, half), BF), struct((d, half), BF), struct((8, d), F32), struct((1, part), F32),
        ],
        alias={19: 4},
        estimate=EST["ffn_far"],
        name="ffn_far",
        mib=56,
    )(
        bits, length, n2, bias, vec, near, near_x, rest, og, n2t, mid, out1, dn1, out2, dn2, ctx_own, ctx_other, wo_own,
        wo_other, stack,
    )


def by_pairs(wcat, matrices, rows, width):
    for p in range(width // 128):
        for i in range(3):
            to = slice((3 * p + i) * 128, (3 * p + i + 1) * 128)
            ref, base = matrices[i]
            wcat[rows, to] = ref[:, base + p * 128 : base + (p + 1) * 128]


def share_kernel(bits_ref, g_ref, wm, wf, out_ref, wcat):
    width = g_ref.shape[1] // 3
    c = bits_ref[0]
    half = wm.shape[0]

    @pl.when(pl.program_id(0) == 0)
    def _():
        for ref, part in ((wm, c), (wf, 1 - c)):
            by_pairs(wcat, [(ref, i * width) for i in range(3)], block(part, half), width)

    out_ref[...] = dot(g_ref[...], wcat[...], 1, 1).astype(BF)


def input_share(bits, g, w_mine, w_far, after=()):
    rows, cols = g.shape
    d = 2 * w_mine.shape[0]
    blk = 512
    row = lambda w: pl.BlockSpec((blk, w), lambda i, *_: (i, 0))
    return call(
        share_kernel, after, prefetch=1, grid=(rows // blk,),
        in_specs=[row(cols), whole(w_mine.shape), whole(w_far.shape)], out_specs=row(d),
        out_shape=struct((rows, d), BF), scratch=[pltpu.VMEM((d, cols), BF)],
        estimate=EST["share"], name="input_share", mib=56,
    )(bits, g, w_mine, w_far)


def input_grad_kernel(
    at, bits_ref, x_ref, gm_ref, vec_ref, g_ref, share_ref, wq, wk, wv, sums2, sums_o, sums_x, db_own, db_mine, db_far,
    out_ref, small_ref, wcat,
):
    width = wq.shape[1]
    d = x_ref.shape[1]

    @pl.when(pl.program_id(0) == 0)
    def _():
        by_pairs(wcat, [(ref, 0) for ref in (wq, wk, wv)], slice(None), width)
        small_ref[...] = jnp.zeros_like(small_ref)
        for k in range(4):
            small_ref[1 + k // 2 : 2 + k // 2, (k % 2) * d : (k % 2 + 1) * d] = sums2[k : k + 1, :]
        low_core = bits_ref[0] == 0
        db_other = jnp.concatenate(
            [jnp.where(low_core, db_mine[...], db_far[...]), jnp.where(low_core, db_far[...], db_mine[...])], 1
        )
        first = bits_ref[bits_ref.shape[0] - 1] == 0
        for row, own, other in ((3, sums_o[...], sums_x[...]), (4, db_own[...], db_other)):
            small_ref[row : row + 1, 0 : own.shape[1]] = jnp.where(first, own, other)
            small_ref[row + 2 : row + 3, 0 : own.shape[1]] = jnp.where(first, other, own)

    gn = dot(g_ref[...], wcat[...], 1, 1) + share_ref[...].astype(F32)
    n, r = norm_rows(x_ref[...].astype(F32))
    out_ref[...] = (gm_ref[...] + norm_back(gn * vec_ref[:, at.gain1], n, r)).astype(BF)
    small_ref[0:1, 0:d] += jnp.sum(gn * n, axis=0, keepdims=True)
    small_ref[0:1, d:] += jnp.sum(gn, axis=0, keepdims=True)


def input_grad(at, bits, x, gm, vec, g, share, wq, wk, wv, sums, after=()):
    rows, d = x.shape
    width = wq.shape[1]
    blk = 256
    row = lambda w: pl.BlockSpec((blk, w), lambda i, *_: (i, 0))
    return call(
        lambda *refs: input_grad_kernel(at, *refs),
        after,
        prefetch=1,
        grid=(rows // blk,),
        in_specs=[row(d), row(d), whole(vec.shape), row(3 * width), row(d)]
        + [whole((d, width))] * 3
        + [whole(v.shape) for v in sums],
        out_specs=[row(d), whole_out((8, 2 * d))],
        out_shape=[struct((rows, d), BF), struct((8, 2 * d), F32)],
        scratch=[pltpu.VMEM((d, 3 * width), BF)],
        estimate=EST["input_grad"],
        name="input_grad",
        mib=56,
    )(bits, x, gm, vec, g, share, wq, wk, wv, *sums)


def wide_qkv(bits, near, far, after=()):
    size, width = near[0].shape
    width //= 4

    def kernel(bits_ref, *refs):
        ins, outs, turn = refs[:4], refs[4:8], refs[8]
        base = (pl.program_id(0) != bits_ref[0]).astype(jnp.int32) * 2
        for half in range(2):
            want = base + (half != bits_ref[1]).astype(jnp.int32)
            rows = slice(half * size, (half + 1) * size)
            for k in range(4):

                @pl.when(want == k)
                def _():
                    ref = ins[k]
                    for i, out in enumerate(outs[:3]):
                        for p in range(width // 128):
                            src = slice((3 * p + i) * 128, (3 * p + i + 1) * 128)
                            out[rows, p * 128 : (p + 1) * 128] = ref[:, src].astype(F32)
                    turn[rows, :] = ref[:, 3 * width :].astype(F32)

        outs[3][...] = turn[...].T

    return call(
        kernel, after, prefetch=1, grid=(2,),
        in_specs=[whole((size, 4 * width))] * 4,
        out_specs=[pl.BlockSpec((2 * size, width), lambda i, *_: (i, 0))] * 3
        + [pl.BlockSpec((width, 2 * size), lambda i, *_: (0, i))],
        out_shape=[struct((4 * size, width), F32)] * 3 + [struct((width, 4 * size), F32)],
        scratch=[pltpu.VMEM((2 * size, width), F32)], estimate=EST["move"], name="wide_qkv", mib=56,
    )(bits, *near, *far)


def wide_ffn(bits, stack, after=()):
    rows, d = stack.shape
    n = min(bits.shape[0], BLOCK_BITS)
    part = rows // 4
    count = 1 << (n - 2)
    size = part // count

    def kernel(bits_ref, *refs):
        for x in range(2):
            for k in range(2):
                refs[4 + x][k * size : (k + 1) * size, :] = refs[2 * x + k][...].astype(F32)

    def place(x, k):
        return lambda q, t, *_: (sub_block(2 * t + k, q, x, n), 0)

    return call(
        kernel, after, prefetch=1, grid=(2, count // 2),
        in_specs=[pl.BlockSpec((size, d), place(x, k)) for x in range(2) for k in range(2)],
        out_specs=[
            pl.BlockSpec((2 * size, d), lambda q, t, *_: (q * (count // 2) + t, 0)),
            pl.BlockSpec((2 * size, d), lambda q, t, *_: (t, q)),
        ],
        out_shape=[struct((2 * part, d), F32), struct((part, 2 * d), F32)],
        estimate=EST["move"], name="wide_ffn", mib=56,
    )(bits, stack, stack, stack, stack)


def wide_both(bits, stack, pieces, after=()):
    rows, d = stack.shape
    n = min(bits.shape[0], BLOCK_BITS)
    part = rows // 2
    count = 1 << (n - 2)
    size = part // count // 2

    def kernel(bits_ref, *refs):
        blocks, ins, outs = refs[:4], refs[4:8], refs[8:]
        base = (pl.program_id(0) != bits_ref[0]).astype(jnp.int32) * 2
        t = pl.program_id(1)
        for x in range(2):
            for k in range(2):
                outs[x][2 * k * size : (2 * k + 1) * size, :] = blocks[2 * x + k][...].astype(F32)
            want = base + (x != bits_ref[1]).astype(jnp.int32)
            for p in range(4):

                @pl.when(want == p)
                def _():
                    for k in range(2):
                        src = pl.ds(pl.multiple_of((2 * t + k) * size, size), size)
                        outs[x][(2 * k + 1) * size : (2 * k + 2) * size, :] = ins[p][src, :].astype(F32)

    def place(x, k):
        return lambda q, t, *_: (sub_block(2 * t + k, q, x, n), 0)

    return call(
        kernel, after, prefetch=1, grid=(2, count // 2),
        in_specs=[pl.BlockSpec((size, d), place(x, k)) for x in range(2) for k in range(2)]
        + [whole(p.shape) for p in pieces],
        out_specs=[
            pl.BlockSpec((4 * size, d), lambda q, t, *_: (q * (count // 2) + t, 0)),
            pl.BlockSpec((4 * size, d), lambda q, t, *_: (t, q)),
        ],
        out_shape=[struct((2 * part, d), F32), struct((part, 2 * d), F32)],
        estimate=EST["move"], name="wide_both", mib=56,
    )(bits, stack, stack, stack, stack, *pieces)


class Links:
    def __init__(self, dp_size):
        self.size = dp_size
        self.bits = dp_size.bit_length() - 1
        index = lax.axis_index("dp")
        digits = [(index >> i) & 1 for i in range(self.bits)] + [lax.axis_index("tensor")]
        self.value = jnp.stack(digits).astype(jnp.int32)

    def swap(self, value, at):
        return lax.ppermute(value, "dp", [(i, i ^ (1 << at)) for i in range(self.size)])

    def across(self, value):
        return lax.ppermute(value, "tensor", [(0, 1), (1, 0)])

    def join(self, mine, other, at, after=()):
        half, width = mine.shape
        if half % 16:
            low = self.value[at] == 0
            return jnp.concatenate([jnp.where(low, mine, other), jnp.where(low, other, mine)], 0)

        def moves(bits, ins, outs):
            return [
                (ins[0], outs[0].at[block(bits[at], half), :]), (ins[1], outs[0].at[block(1 - bits[at], half), :])
            ]

        return arrange(self.value, [mine, other], [(2 * half, width)], moves, "join", after)[0]


def halve(bits, parts, bit, after=()):
    count = len(parts)
    parts = lax.optimization_barrier((*parts, *after))[:count]
    size = parts[0].shape[0] // 2

    def half(at):
        return sum(lax.dynamic_slice_in_dim(v, at * size, size, 0).astype(F32) for v in parts).astype(BF)

    return half(1 - bits[bit]), half(bits[bit])


class Halve:
    def __init__(self, links, keep, recv):
        self.links, self.keep, self.recv, self.at = links, keep, recv, 0
        low = min(links.bits, BLOCK_BITS)
        self.order = [*range(low), *reversed(range(low, links.bits))]
        self.done = False

    def advance(self, after):
        links = self.links
        self.at += 1
        self.done = self.at == links.bits
        if self.done:
            return
        bit = self.order[self.at]
        send, self.keep = halve(links.value, (self.keep, self.recv), bit, after)
        self.recv = links.swap(send, bit)


RIDE = 16


def ride_kernel(rows, cut, bits_ref, *refs):
    *ins, small_ref, send_ref, keep_ref, next_ref, acc = refs
    width = small_ref.shape[1]
    small = small_ref[...]
    total = None
    for ref in ins:
        value = ref[0:rows, :].astype(F32)
        total = value if total is None else total + value
        if ref.shape[0] > rows:
            riding = ref[rows : rows + RIDE, :].astype(F32)
            small = small + riding[0:8] + riding[8:16]
    next_ref[...] = small
    if send_ref is None:
        keep_ref[...] = total.astype(BF)
        return
    acc[...] = total
    if cut is None:
        size = rows
        send_ref[0:size, :] = total.astype(BF)
        keep_ref[...] = total.astype(BF)
    else:
        size = rows // 2
        bit = bits_ref[cut]
        low, high = acc[0:size, :], acc[size : 2 * size, :]
        send_ref[0:size, :] = jnp.where(bit == 0, high, low).astype(BF)
        keep_ref[...] = jnp.where(bit == 0, low, high).astype(BF)
    high = small.astype(BF)
    send_ref[size:, :] = jnp.concatenate([high, (small - high.astype(F32)).astype(BF)], 0)


def ride(bits, parts, small, cut, last, after=()):
    rows = parts[0].shape[0]
    width = small.shape[1]
    size = rows // 2 if cut is not None else rows
    shapes = [struct((size, width), BF), struct(small.shape, F32)]
    if not last:
        shapes.insert(0, struct((size + RIDE, width), BF))

    def kernel(bits_ref, *refs):
        refs = list(refs)
        if last:
            refs.insert(len(parts) + 1, None)
        ride_kernel(rows, cut, bits_ref, *refs)

    out = call(
        kernel, after, prefetch=1, in_specs=[whole(a.shape) for a in (*parts, small)],
        out_specs=[whole_out(t.shape) for t in shapes], out_shape=shapes,
        scratch=[pltpu.VMEM((rows, width), F32)], estimate=EST["move"], name="ride",
    )(bits, *parts, small)
    return (None, *out) if last else out


def layer(
    dp_size, inputs, lengths, norm1_gain, norm1_shift, query_weight, query_bias, key_weight, key_bias, value_weight,
    value_bias, out_weight, out_bias, norm2_gain, norm2_shift, up_weight, up_bias, down_weight, down_bias, out_grad,
):
    rows, d = inputs.shape
    width = query_weight.shape[1]
    ff = up_weight.shape[1]
    part = ff // 2
    links = Links(dp_size)
    bits = links.value
    tensor = lax.axis_index("tensor")
    length = jnp.where(tensor == 0, lengths[:1], lengths[1:])
    cos, sin = (jnp.asarray(t) for t in rotary_tables(rows))
    at = Row(d, width, ff)
    vec = [norm1_gain, norm1_shift, out_bias, norm2_gain, norm2_shift, down_bias, query_bias, key_bias, value_bias, up_bias]
    vec = jnp.concatenate([v.reshape(1, -1) for v in vec], 1)

    def qkv_moves(bits_ref, ins, outs):
        return [
            (w.at[block(bits_ref[0], d // 2), :], outs[0].at[:, i * width : (i + 1) * width]) for i, w in enumerate(ins)
        ]

    near_rows = 5 * d // 12
    half = width // 2
    def cut_moves(bits_ref, ins, outs):
        c, b = bits_ref[0], bits_ref[1]
        wu, wd = ins
        near, rest = outs
        cols = block(c, part)
        return [
            (wu.at[block(b, near_rows), cols], near),
            (wu.at[2 * near_rows :, cols], rest.at[0 : d - 2 * near_rows, :]),
            (wd.at[block(c, part), :], rest.at[d - 2 * near_rows :, :]),
        ]

    qkv_mine, = arrange(bits, [query_weight, key_weight, value_weight], [(d // 2, 3 * width)], qkv_moves, "cut_qkv", mib=56)
    qkv_mine = links.across(qkv_mine)
    normed, normed_t, *own, ctx_own, aug_own, near, rest = heads_own(
        at, cut_moves, [(near_rows, d), (d + part - 2 * near_rows, d)], bits, length, inputs, vec, query_weight,
        key_weight, value_weight, cos, sin, up_weight, down_weight,
    )
    bias_x = links.across(vec)
    near, out_x = links.across(near), links.across(out_weight)
    qkv_mine, _ = lax.optimization_barrier((qkv_mine, ctx_own))
    qkv_far = links.swap(qkv_mine, 0)
    *other, ctx_x, aug_x = heads_other(at, bits, length, normed, qkv_mine, qkv_far, bias_x, cos, sin, after=(ctx_own,))
    near, out_x, rest, ctx_x = lax.optimization_barrier((near, out_x, rest, ctx_x))
    rest = links.across(rest)
    near_x = links.swap(near, 1)
    near_far = links.swap(near, 0)
    mid, n2, n2t, out1, dn1, w_send, w_keep, dbu = ffn_own(
        at, bits, inputs, ctx_own, ctx_x, out_weight, out_x, vec, out_grad, up_weight, down_weight
    )

    w_recv = links.swap(w_send, 0)
    near_x_far, rest_far = links.swap(near_x, 0), links.swap(rest, 0)
    out2, dn2, stack, dbu_mine = ffn_mine(bits, n2, near, near_x, rest, bias_x, out_grad, n2t, after=(mid,))
    own_sum = Halve(links, w_keep, w_recv)
    own_sum.advance((out2,))
    layer_out, gm, g_own, g_x, stack, dwo, dwo_x, sums2, dbu_far = ffn_far(
        at, bits, length, n2, near_far, near_x_far, rest_far, bias_x, vec, out_grad, n2t, mid, out1, dn1, out2, dn2,
        ctx_own, ctx_x, out_weight, out_x, stack, after=(own_sum.keep,),
    )
    blocks = min(dp_size, 1 << BLOCK_BITS)

    def turned(rows_, first, second):
        return rows_.reshape(first, second, -1, d).swapaxes(0, 1).reshape(-1, d)

    if dp_size > blocks:
        stack = turned(stack, blocks, dp_size // blocks)
    stack = lax.psum_scatter(stack, "dp", scatter_dimension=0, tiled=True)
    n = d // 2
    gx, sums_x, qx_s, qx_k = attend_back(
        bits, length, *other, g_x, ctx_x, aug_x, cos, sin, normed_t, dwo_x
    )
    qx_r = links.swap(qx_s, 0)
    own_sum.advance((qx_k,))
    share = input_share(bits, gx, qkv_mine, qkv_far, after=(own_sum.keep,))
    qx_k, qx_r, _ = lax.optimization_barrier((qx_k, qx_r, share))
    qx = (qx_k.astype(F32) + qx_r.astype(F32)).astype(BF)
    qx_y = links.across(qx)
    go, sums_o, qo_s, qo_k = attend_back(
        bits, length, *own, g_own, ctx_own, aug_own, cos, sin, normed_t, dwo, after=(qx,), est=12
    )
    own_sum.advance((qo_k,))
    qo_r = links.swap(qo_s, 0)
    q, = fold(bits, [(qo_k, 0, 0, n), (qx_y, 0, 0, n)], n, [(0, n)], "fold_qkv_y", after=(own_sum.keep,), est=busy(8))
    q_s, q_k = halve(bits, (q, qo_r), 1)
    q_r = links.swap(q_s, 1)
    input_grad_out, small = input_grad(
        at, bits, inputs, gm, vec, go, share, query_weight, key_weight, value_weight,
        (sums2, sums_o, sums_x, dbu, dbu_mine, dbu_far), after=(q_k,),
    )
    last = links.bits - 1
    small, = fold(bits, [(small, 0, 0, 8), (links.swap(small, 1), 0, 0, 8)], 8, [(0, 8)], "fold_small")
    send, keep1, small = ride(bits, [q_k, q_r], small, 2 if last > 2 else None, False, (q_k,))
    q_parts = [keep1, links.swap(send, 2)]
    stack, keep1 = lax.optimization_barrier((stack, keep1))
    stack_r = links.across(stack)
    while not own_sum.done:
        own_sum.advance((keep1,))
    size = stack.shape[0]
    parts = [(v, 0, 0, size) for v in (stack, stack_r, own_sum.keep, own_sum.recv)][1:]
    split = dp_size == blocks
    cuts = [(0, size // 2), (size // 2, size // 2)] if split else [(0, size)]
    stack, *piece = fold(bits, parts, size, cuts, "fold_stack", after=(keep1,))
    gathered = lax.all_gather(stack, "dp", axis=0, tiled=True)
    if dp_size > blocks:
        gathered = turned(gathered, dp_size // blocks, blocks)
    piece_r = links.swap(piece[0], last) if split else None

    after = (stack,)
    parts = q_parts
    for bit in range(3, links.bits):
        send, keep, small = ride(bits, parts, small, bit if bit < last else None, False, after)
        after = ()
        parts = [keep, links.swap(send, bit)]
    if split:
        piece = piece[0]
        for bit in reversed(range(2, links.bits)):
            piece = links.join(piece, piece_r, bit, after=(keep,))
            piece_r = links.swap(piece, bit - 1)
        after = (piece,)
    _, q, small = ride(bits, parts, small, None, True, after)
    for bit in reversed(range(2, last)):
        q_r = links.swap(q, bit)
        if bit == last - 1:
            size = small.shape[0]
            for swap in (links.across, lambda v: links.swap(v, 0)):
                parts = [(small, 0, 0, size), (swap(small), 0, 0, size)]
                small, = fold(bits, parts, size, [(0, size)], "fold_small", after=(q,))
        q = links.join(q, q_r, bit, after=(small,))
    q_r = links.swap(q, 1)
    q_far = links.swap(q, 0)
    if split:
        pieces = [piece, piece_r, links.swap(piece, 0), links.swap(piece_r, 0)]
        grad_down, grad_up = wide_both(bits, gathered, pieces, after=(q,))
    else:
        grad_down, grad_up = wide_ffn(bits, gathered, after=(q,))
    q_r, grad_up = lax.optimization_barrier((q_r, grad_up))
    q_r_far = links.swap(q_r, 0)
    grad_q, grad_k, grad_v, grad_out = wide_qkv(bits, (q, q_r), (q_far, q_r_far), after=(grad_up,))

    gain1, shift1, out_b, gain2, shift2, down_b = (small[i // 2, (i % 2) * d : (i % 2 + 1) * d] for i in range(6))
    mine = lax.dynamic_slice_in_dim(small, 3 + 2 * tensor, 2, 0)
    qkv_bias = mine[0, : 3 * width].reshape(-1, 3, 128)
    return (
        layer_out, input_grad_out, gain1, shift1,
        grad_q, qkv_bias[:, 0].reshape(-1), grad_k, qkv_bias[:, 1].reshape(-1), grad_v, qkv_bias[:, 2].reshape(-1),
        grad_out, out_b, gain2, shift2, grad_up, mine[1, :ff], grad_down, down_b,
    )


def solution(mesh):
    rows = P(("dp", "tensor"), None)
    cols = P(None, "tensor")
    tens = P("tensor")
    return jax.shard_map(
        lambda *args: layer(mesh.shape["dp"], *args),
        mesh=mesh,
        in_specs=(
            rows, P("dp"), P(), P(), cols, tens, cols, tens, cols, tens, P("tensor", None), P(), P(), P(), cols, tens,
            P("tensor", None), P(), rows,
        ),
        out_specs=(
            rows, rows, P(), P(), cols, tens, cols, tens, cols, tens, P("tensor", None), P(), P(), P(), cols, tens,
            P("tensor", None), P(),
        ),
        check_vma=False,
    )
```

```python
import math

import jax
import jax.numpy as jnp
import numpy as np
from jax import lax
from jax.experimental import pallas as pl
from jax.experimental.pallas import tpu as pltpu
from jax.sharding import PartitionSpec as P

HEAD_DIM = 64
EPS = 1e-05
LOG2E = math.log2(math.e)
LN2 = math.log(2.0)
F32 = jnp.float32
BF = jnp.bfloat16
BIG = -1e30


def dot(a, b, ca=1, cb=0):
    return lax.dot_general(a, b, (((ca,), (cb,)), ((), ())), preferred_element_type=F32)


def cost(macs, nbytes, exps=0):
    return pl.CostEstimate(flops=int(2 * macs), bytes_accessed=int(nbytes), transcendentals=int(exps))


def busy(micros):
    return pl.CostEstimate(flops=int(micros * 1.1e9), bytes_accessed=1000, transcendentals=0)


EST = {
    "move": busy(0.01),
    "heads_own": busy(16),
    "heads_other": busy(100),
    "ffn_own": busy(0.01),
    "ffn_mine": busy(100),
    "ffn_far": busy(100),
    "share": busy(8),
    "input_grad": busy(8),
    "halve": busy(20),
}


def struct(shape, dtype):
    return jax.ShapeDtypeStruct(shape, dtype)


def whole(shape):
    return pl.BlockSpec(shape, lambda *_: (0,) * len(shape), pipeline_mode=pl.Buffered(1))


def whole_out(shape):
    return pl.BlockSpec(shape, lambda *_: (0,) * len(shape))


ANY = pl.BlockSpec(memory_space=pl.ANY)


def call(kernel, after, *, in_specs, out_specs, out_shape, estimate, name, grid=(1,), prefetch=0, scratch=(), alias=None, mib=28):
    after = tuple(after)
    n_in = prefetch + len(in_specs)

    def body(*refs):
        kernel(*refs[:n_in], *refs[n_in + len(after) :])

    run = pl.pallas_call(
        body,
        grid_spec=pltpu.PrefetchScalarGridSpec(
            num_scalar_prefetch=prefetch,
            grid=grid,
            in_specs=list(in_specs) + [ANY] * len(after),
            out_specs=out_specs,
            scratch_shapes=list(scratch),
        ),
        out_shape=out_shape,
        compiler_params=pltpu.CompilerParams(vmem_limit_bytes=mib << 20),
        input_output_aliases=alias or {},
        cost_estimate=estimate,
        name=name,
    )
    return lambda *args: run(*args, *after)


def norm_rows(v):
    mean = jnp.mean(v, axis=1, keepdims=True)
    cent = v - mean
    var = jnp.mean(cent * cent, axis=1, keepdims=True)
    r = lax.rsqrt(var + EPS)
    return cent * r, r


def norm_back(e, n, r):
    return r * (e - jnp.mean(e, axis=1, keepdims=True) - n * jnp.mean(e * n, axis=1, keepdims=True))


def rotary_tables(rows):
    half = HEAD_DIM // 2
    freq = (10000.0 ** (-2.0 * np.arange(half, dtype=np.float32) / HEAD_DIM)).astype(np.float32)
    ang = (np.arange(rows, dtype=np.float32)[:, None] * freq[None, :]).astype(np.float64)
    cos = np.cos(ang).astype(np.float32)
    sin = np.sin(ang).astype(np.float32)
    return np.concatenate([cos] * 4, 1), np.concatenate([-sin, sin] * 2, 1)


def swap_halves(v):
    lane = lax.broadcasted_iota(jnp.int32, v.shape, 1)
    return jnp.where((lane & 32) == 0, pltpu.roll(v, 96, 1), pltpu.roll(v, 32, 1))


def rotate(v, cos, sin):
    return v * cos + swap_halves(v) * sin


def rotate_back(v, cos, sin):
    return v * cos - swap_halves(v) * sin


class Row:
    def __init__(self, d, width, ff):
        at = 0
        for name, size in (
            ("gain1", d), ("shift1", d), ("out_bias", d), ("gain2", d), ("shift2", d), ("down_bias", d),
            ("qkv", 3 * width), ("up", ff),
        ):
            setattr(self, name, slice(at, at + size))
            at += size


def pull(src, dst, sem):
    copy = pltpu.make_async_copy(src, dst, sem)
    copy.start()
    return copy


def arrange(bits, arrays, shapes, moves, name, after=(), mib=28):
    def kernel(bits_ref, *refs):
        ins, outs, sem = refs[: len(arrays)], refs[len(arrays) : -1], refs[-1]
        copies = [pull(src, dst, sem.at[i]) for i, (src, dst) in enumerate(moves(bits_ref, ins, outs))]
        for copy in copies:
            copy.wait()

    return call(
        kernel,
        after,
        prefetch=1,
        in_specs=[ANY] * len(arrays),
        out_specs=[whole_out(shape) for shape in shapes],
        out_shape=[struct(shape, BF) for shape in shapes],
        scratch=[pltpu.SemaphoreType.DMA((8,))],
        estimate=EST["move"],
        name=name,
        mib=mib,
    )(bits, *arrays)


def block(bit, size):
    return pl.ds(pl.multiple_of(bit * size, size), size)


def fold(bits, parts, rows, outs, name, after=(), width=None, est=EST["move"]):
    arrays = [p[0] for p in parts]
    width = width or arrays[0].shape[1]
    dtype = arrays[0].dtype
    half = rows // 2
    shapes = [(half, width)] * 2 if isinstance(outs, int) else [(n, width) for _, n in outs]

    def kernel(bits_ref, *refs):
        ins, outs_r, acc = refs[: len(parts)], refs[len(parts) : -1], refs[-1]
        seen = []
        for ref, (_, src, dst, n) in zip(ins, parts):
            value = ref[src : src + n, 0:width].astype(F32)
            fresh = not any(dst < b and a < dst + n for a, b in seen)
            acc[dst : dst + n, :] = value if fresh else acc[dst : dst + n, :] + value
            seen.append((dst, dst + n))
        if isinstance(outs, int):
            bit = bits_ref[outs]
            for ref, at in zip(outs_r, (1 - bit, bit)):
                ref[...] = acc[pl.ds(pl.multiple_of(at * half, 8 if half % 8 == 0 else 1), half), :].astype(dtype)
        else:
            for ref, (start, n) in zip(outs_r, outs):
                ref[...] = acc[start : start + n, :].astype(dtype)

    return call(
        kernel,
        after,
        prefetch=1,
        in_specs=[whole(a.shape) for a in arrays],
        out_specs=[whole_out(shape) for shape in shapes],
        out_shape=[struct(shape, dtype) for shape in shapes],
        scratch=[pltpu.VMEM((rows, width), F32)],
        estimate=est,
        name=name,
    )(bits, *arrays)


def put_qkv(pre, cos, sin, q_ref, k_ref, v_ref):
    width = q_ref.shape[1]
    for i in range(width // 128):
        sl = slice(i * 128, (i + 1) * 128)
        q_ref[:, sl] = (rotate(pre[0][:, sl], cos, sin) * (LOG2E / 8.0)).astype(BF)
        k_ref[:, sl] = rotate(pre[1][:, sl], cos, sin).astype(BF)
        v_ref[:, sl] = pre[2][:, sl].astype(BF)


def split3(v):
    hi = v.astype(BF)
    rest = v - hi.astype(F32)
    mid = rest.astype(BF)
    lo = rest - mid.astype(F32)
    return hi.astype(F32), mid.astype(F32), lo


def spread(lane, first, one, two):
    out = jnp.where(lane == 0, first, 0.0)
    for at, part in enumerate((*split3(one), *split3(two))):
        out = jnp.where(lane == at + 1, part, out)
    return out.astype(BF)


def attend_pair(length, q_ref, k_ref, v_ref, ctx_ref, aug_ref):
    bq = 256
    rows = q_ref.shape[0]
    lane1 = lax.broadcasted_iota(jnp.int32, (1, 128), 1)
    krow = lax.broadcasted_iota(jnp.int32, (rows, 128), 0)
    klane = lax.broadcasted_iota(jnp.int32, (rows, 128), 1)
    lane = lax.broadcasted_iota(jnp.int32, (bq, 128), 1)
    qrow = lax.broadcasted_iota(jnp.int32, (bq, 128), 0)
    kaug = jnp.where((klane == 0) & (krow >= length), BIG, 0.0).astype(BF)
    k = jnp.concatenate([k_ref[...], kaug], 1)
    v = jnp.concatenate([v_ref[...], jnp.ones((rows, 128), BF)], 1)
    qaug = jnp.where(lane == 0, 1.0, 0.0).astype(BF)
    for i in range(rows // bq):
        sl = slice(i * bq, (i + 1) * bq)
        q = q_ref[sl, :]
        outs, totals = [], []
        for h in range(2):
            keep = ((lane1 < 64) if h == 0 else (lane1 >= 64)).astype(BF)
            s = dot(jnp.concatenate([q * keep, qaug], 1), k, 1, 1)
            top = jnp.max(s, axis=1, keepdims=True)
            p = jnp.exp2(s - top).astype(BF)
            o = dot(p, v)
            total = o[:, 128:]
            outs.append(o[:, :128] / total)
            totals.append(top + jnp.log2(total))
        ctx = jnp.where(lane < 64, outs[0], outs[1])
        ctx_ref[sl, :] = jnp.where(qrow + i * bq < length, ctx, 0.0).astype(BF)
        aug_ref[sl, :] = spread(lane, 1.0, totals[0], totals[1])


def attend_all(length, q, k, v, ctx, aug):
    for p in range(q.shape[1] // 128):
        sl = slice(p * 128, (p + 1) * 128)
        attend_pair(length, *(ref.at[:, sl] for ref in (q, k, v, ctx, aug)))


def heads_own_kernel(
    at, cut, bits_ref, len_ref, x_ref, vec_ref, wq_ref, wk_ref, wv_ref, cos_ref, sin_ref, wu_h, wd_h, wo_h,
    n_h, nt_h, q_h, k_h, v_h, ctx_h, aug_h, near_h, rest_h, half_h,
    n_s, nt_s, q_s, k_s, v_s, ctx_s, aug_s, near_s, rest_s, half_s, sem,
):
    rows = x_ref.shape[0]
    width = q_s.shape[1]
    loads = [
        pull(src, dst, sem.at[i]) for i, (src, dst) in enumerate(cut(bits_ref, (wu_h, wd_h, wo_h), (near_s, rest_s, half_s)))
    ]
    blk = 256
    bias = vec_ref[:, at.qkv]
    for i in range(rows // blk):
        sl = slice(i * blk, (i + 1) * blk)
        n, _ = norm_rows(x_ref[sl, :].astype(F32))
        low = (n * vec_ref[:, at.gain1] + vec_ref[:, at.shift1]).astype(BF)
        n_s[sl, :] = low
        nt_s[:, sl] = low.T
        pre = [
            dot(low, w[...]) + bias[:, j * width : (j + 1) * width] for j, w in enumerate((wq_ref, wk_ref, wv_ref))
        ]
        put_qkv(pre, cos_ref[sl, :], sin_ref[sl, :], *(ref.at[sl, :] for ref in (q_s, k_s, v_s)))
    for load in loads:
        load.wait()
    pairs = [
        (near_s, near_h), (rest_s, rest_h), (n_s, n_h), (nt_s, nt_h), (q_s, q_h), (k_s, k_h), (v_s, v_h), (half_s, half_h)
    ]
    stores = [pull(src, dst, sem.at[8 + i]) for i, (src, dst) in enumerate(pairs)]
    attend_all(len_ref[0], q_s, k_s, v_s, ctx_s, aug_s)
    stores += [pull(ctx_s, ctx_h, sem.at[16]), pull(aug_s, aug_h, sem.at[17])]
    for store in stores:
        store.wait()


def heads_own(at, cut, shapes, bits, length, x, vec, wq, wk, wv, cos, sin, wu, wd, wo, after=()):
    rows, d = x.shape
    width = wq.shape[1]
    outs = [(rows, d), (d, rows)] + [(rows, width)] * 5 + list(shapes)
    return call(
        lambda *refs: heads_own_kernel(at, cut, *refs),
        after,
        prefetch=2,
        in_specs=[whole(a.shape) for a in (x, vec, wq, wk, wv, cos, sin)] + [ANY] * 3,
        out_specs=[ANY] * len(outs),
        out_shape=[struct(shape, BF) for shape in outs],
        scratch=[pltpu.VMEM(shape, BF) for shape in outs] + [pltpu.SemaphoreType.DMA((18,))],
        estimate=EST["heads_own"],
        name="heads_own",
        mib=56,
    )(bits, length, x, vec, wq, wk, wv, cos, sin, wu, wd, wo)


def heads_other_kernel(
    at, bits_ref, len_ref, n_ref, wm_ref, wf_ref, b_ref, cos_ref, sin_ref, q_h, k_h, v_h, ctx_h, aug_h,
    q_s, k_s, v_s, ctx_s, aug_s, sem,
):
    rows = n_ref.shape[0]
    width = q_s.shape[1]
    half = wm_ref.shape[0]
    c = bits_ref[0]
    blk = 256
    for i in range(rows // blk):
        sl = slice(i * blk, (i + 1) * blk)
        pre = dot(n_ref[sl, block(c, half)], wm_ref[...]) + dot(n_ref[sl, block(1 - c, half)], wf_ref[...])
        pre = pre + b_ref[:, at.qkv]
        put_qkv(
            [pre[:, j * width : (j + 1) * width] for j in range(3)], cos_ref[sl, :], sin_ref[sl, :],
            *(ref.at[sl, :] for ref in (q_s, k_s, v_s)),
        )
    stores = [pull(src, dst, sem.at[i]) for i, (src, dst) in enumerate(((q_s, q_h), (k_s, k_h), (v_s, v_h)))]
    attend_all(len_ref[0], q_s, k_s, v_s, ctx_s, aug_s)
    stores += [pull(ctx_s, ctx_h, sem.at[3]), pull(aug_s, aug_h, sem.at[4])]
    for store in stores:
        store.wait()


def heads_other(at, bits, length, n, w_mine, w_far, bias, cos, sin, after=()):
    rows = n.shape[0]
    width = w_mine.shape[1] // 3
    outs = [(rows, width)] * 5
    return call(
        lambda *refs: heads_other_kernel(at, *refs),
        after,
        prefetch=2,
        in_specs=[whole(a.shape) for a in (n, w_mine, w_far, bias, cos, sin)],
        out_specs=[ANY] * 5,
        out_shape=[struct(shape, BF) for shape in outs],
        scratch=[pltpu.VMEM(shape, BF) for shape in outs] + [pltpu.SemaphoreType.DMA((5,))],
        estimate=EST["heads_other"],
        name="heads_other",
        mib=56,
    )(bits, length, n, w_mine, w_far, bias, cos, sin)


def attend_back_kernel(
    bq, bits_ref, len_ref, q_ref, k_ref, v_ref, g_ref, ctx_ref, aug_ref, cos_ref, sin_ref, nt_ref, wo_ref,
    d_ref, sum_ref, send_ref, keep_ref, dqt, dall, gaug,
):
    rows = q_ref.shape[0]
    length = len_ref[0]
    lane1 = lax.broadcasted_iota(jnp.int32, (1, 128), 1)
    krow = lax.broadcasted_iota(jnp.int32, (rows, 128), 0)
    klane = lax.broadcasted_iota(jnp.int32, (rows, 128), 1)
    lane = lax.broadcasted_iota(jnp.int32, (bq, 128), 1)
    k = k_ref[...]
    v = v_ref[...]
    kt = k.T
    dks, dvs = [], []
    for h in range(2):
        keep = ((lane1 < 64) if h == 0 else (lane1 >= 64)).astype(BF)
        first = 1 + 3 * h
        mine = jnp.where((klane >= first) & (klane < first + 3), -1.0, 0.0)
        kaug = jnp.where((klane == 0) & (krow >= length), BIG, mine).astype(BF)
        kh = jnp.concatenate([k * keep, kaug], 1)
        vh = jnp.concatenate([v * keep, mine.astype(BF)], 1)
        dk = jnp.zeros((rows, 128), F32)
        dv = jnp.zeros((rows, 128), F32)
        for i in range(rows // bq):
            sl = slice(i * bq, (i + 1) * bq)
            q = q_ref[sl, :]
            g = g_ref[sl, :]
            if h == 0:
                prod = g.astype(F32) * ctx_ref[sl, :].astype(F32)
                d0 = jnp.sum(jnp.where(lane < 64, prod, 0.0), 1, keepdims=True)
                d1 = jnp.sum(jnp.where(lane < 64, 0.0, prod), 1, keepdims=True)
                gaug[sl, :] = spread(lane, 0.0, d0, d1)
            st = dot(kh, jnp.concatenate([q, aug_ref[sl, :]], 1), 1, 1)
            pt = jnp.exp2(st)
            dpt = dot(vh, jnp.concatenate([g, gaug[sl, :]], 1), 1, 1)
            ds = (pt * dpt).astype(BF)
            dv = dv + dot(pt.astype(BF), g)
            dk = dk + dot(ds, q)
            dqt[h * 64 : (h + 1) * 64, sl] = dot(kt[h * 64 : (h + 1) * 64, :], ds)
        dks.append(dk)
        dvs.append(dv)
    cos = cos_ref[...]
    sin = sin_ref[...]
    dq = rotate_back(dqt[...].T * (1.0 / 8.0), cos, sin).astype(BF)
    dk = rotate_back(jnp.where(klane < 64, dks[0], dks[1]) * LN2, cos, sin).astype(BF)
    dv = jnp.where(klane < 64, dvs[0], dvs[1]).astype(BF)
    for at, val in enumerate((dq, dk, dv)):
        sl = slice(at * 128, (at + 1) * 128)
        d_ref[:, sl] = val
        sum_ref[:, sl] = jnp.sum(val.astype(F32), axis=0, keepdims=True)
    j = pl.program_id(0)
    dall[:, block(j, 384)] = jnp.concatenate([dq, dk, dv], 1)

    @pl.when(j == pl.num_programs(0) - 1)
    def _():
        half = send_ref.shape[0]
        c = bits_ref[0]
        for ref, part in ((send_ref, 1 - c), (keep_ref, c)):
            width = dall.shape[1]
            ref[:, 0:width] = dot(nt_ref[block(part, half), :], dall[...]).astype(BF)
            ref[:, width:] = wo_ref[block(part, half), :]


def attend_back(bits, length, q, k, v, g, ctx, aug, cos, sin, nt, wo, after=(), est=100):
    rows, width = q.shape
    d = 2 * width
    bs = pl.BlockSpec((rows, 128), lambda j, *_: (0, j))
    return call(
        lambda *refs: attend_back_kernel(256, *refs),
        after,
        prefetch=2,
        grid=(width // 128,),
        in_specs=[bs] * 6 + [whole((rows, 128))] * 2 + [whole(nt.shape), whole(wo.shape)],
        out_specs=[pl.BlockSpec((rows, 384), lambda j, *_: (0, j)), pl.BlockSpec((1, 384), lambda j, *_: (0, j))]
        + [whole_out((d // 2, 4 * width))] * 2,
        out_shape=[struct((rows, 3 * width), BF), struct((1, 3 * width), F32)] + [struct((d // 2, 4 * width), BF)] * 2,
        scratch=[pltpu.VMEM((128, rows), F32), pltpu.VMEM((rows, 3 * width), BF), pltpu.VMEM((rows, 128), BF)],
        estimate=busy(est),
        name="attend_back",
        mib=56,
    )(bits, length, q, k, v, g, ctx, aug, cos, sin, nt, wo)


def gelu_pair(h):
    z = jnp.abs(h) * (0.3275911 / math.sqrt(2.0)) + 1.0
    t = pl.reciprocal(z, approx=True)
    t = t * (2.0 - z * t)
    e = jnp.exp2(h * h * (-0.5 * LOG2E))
    poly = 0.5 * 1.061405429 * t - 0.5 * 1.453152027
    poly = poly * t + 0.5 * 1.421413741
    poly = poly * t - 0.5 * 0.284496736
    poly = poly * t + 0.5 * 0.254829592
    w = poly * t * e
    cdf = jnp.where(h >= 0.0, 1.0 - w, w)
    return h * cdf, cdf + h * e * (1.0 / math.sqrt(2.0 * math.pi))


def ffn_quarter(n2, n2t, og, wu, wd, bias, out_acc, dn_acc, act_s, dh_s, gd, gu, first, before=None, done=None):
    rows, d = og.shape
    part = wd.shape[0]
    blk = 256
    dbias = jnp.zeros((1, part), F32)
    if before is not None:
        before(0, blk)
    for i in range(rows // blk):
        sl = slice(i * blk, (i + 1) * blk)
        if before is not None and i + 1 < rows // blk:
            before(i + 1, blk)
        h = dot(n2[sl, :], wu[...]) + bias
        act, slope = gelu_pair(h)
        act = act.astype(BF)
        dh = (slope * dot(og[sl, :], wd[...], 1, 1)).astype(BF)
        act_s[sl, :] = act
        dh_s[sl, :] = dh
        dbias = dbias + jnp.sum(dh.astype(F32), axis=0, keepdims=True)
        o = dot(act, wd[...])
        e = dot(dh, wu[...], 1, 1)
        out_acc[sl, :] = o if first else out_acc[sl, :] + o
        dn_acc[sl, :] = e if first else dn_acc[sl, :] + e
        if done is not None and i > 0:
            done(i - 1, blk)
    if done is not None:
        done(rows // blk - 1, blk)
    gd[...] = dot(act_s[...], og[...], 0, 0).astype(BF)
    gu[...] = dot(n2t[...], dh_s[...]).astype(BF)
    return dbias


def ffn_own_kernel(
    at, bits_ref, x_ref, co_ref, cx_ref, woo_ref, vec_ref, wom_h, wof_h, og_h, wu_h, wd_h,
    mid_h, n2_h, n2t_h, out_h, dn_h, send_h, keep_h, db_ref,
    wox, og, wu, wd, mid, n2, n2t, out, dn, outb, dnb, act_s, dh_s, gd, gu, sem,
):
    rows, d = x_ref.shape
    part = wu_h.shape[1] // 2
    c = bits_ref[0]
    cols = [block(p, part) for p in (1 - c, c)]
    biases = [pl.ds(pl.multiple_of(at.up.start + p * part, 128), part) for p in (1 - c, c)]
    quarter = wom_h.shape[0]
    first = [
        pull(wom_h, wox.at[block(c, quarter), :], sem.at[18]), pull(wof_h, wox.at[block(1 - c, quarter), :], sem.at[19])
    ]
    loads = [pull(og_h, og, sem.at[0])]
    for q in range(2):
        loads.append(pull(wu_h.at[:, cols[q]], wu.at[q], sem.at[1 + 2 * q]))
        loads.append(pull(wd_h.at[cols[q], :], wd.at[q], sem.at[2 + 2 * q]))
    for load in first:
        load.wait()
    stores = []

    def enter(i, blk):
        sl = slice(i * blk, (i + 1) * blk)
        att = dot(co_ref[sl, :], woo_ref[...]) + dot(cx_ref[sl, :], wox[...])
        v = x_ref[sl, :].astype(F32) + att + vec_ref[:, at.out_bias]
        mid[sl, :] = v
        n, _ = norm_rows(v)
        low = (n * vec_ref[:, at.gain2] + vec_ref[:, at.shift2]).astype(BF)
        n2[sl, :] = low
        n2t[:, sl] = low.T
        if i == 0:
            for load in loads:
                load.wait()
        if (i + 1) * blk == rows:
            stores.extend([pull(mid, mid_h, sem.at[5]), pull(n2, n2_h, sem.at[6]), pull(n2t, n2t_h, sem.at[7])])

    def flush(i, blk):
        sl = pl.ds(i * blk, blk)
        outb[sl, :] = out[sl, :].astype(BF)
        dnb[sl, :] = dn[sl, :].astype(BF)
        stores.append(pull(outb.at[sl, :], out_h.at[sl, :], sem.at[8 + i]))
        stores.append(pull(dnb.at[sl, :], dn_h.at[sl, :], sem.at[12 + i]))

    for q in range(2):
        db_ref[:, cols[q]] = ffn_quarter(
            n2, n2t, og, wu.at[q], wd.at[q], vec_ref[:, biases[q]], out, dn, act_s, dh_s, gd.at[q], gu.at[q], q == 0,
            enter if q == 0 else None, flush if q == 1 else None,
        )
        stores.append(pull(gd.at[q], (send_h, keep_h)[q].at[0:part, :], sem.at[16 + q]))
        stores.append(pull(gu.at[q], (send_h, keep_h)[q].at[part:, :], sem.at[20 + q]))
    for store in stores:
        store.wait()


def ffn_own(at, bits, x, ctx_own, ctx_other, wo_own, vec, wo_mine, wo_far, og, wu, wd, after=()):
    rows, d = x.shape
    ff = wu.shape[1]
    part = ff // 2
    half = ctx_own.shape[1]
    return call(
        lambda *refs: ffn_own_kernel(at, *refs),
        after,
        prefetch=1,
        in_specs=[
            whole((rows, d)), whole((rows, half)), whole((rows, half)), whole((half, d)), whole(vec.shape),
        ] + [ANY] * 5,
        out_specs=[ANY] * 7 + [whole_out((1, ff))],
        scratch=[
            pltpu.VMEM((half, d), BF),
            pltpu.VMEM((rows, d), BF), pltpu.VMEM((2, d, part), BF), pltpu.VMEM((2, part, d), BF),
            pltpu.VMEM((rows, d), F32), pltpu.VMEM((rows, d), BF), pltpu.VMEM((d, rows), BF),
            pltpu.VMEM((rows, d), F32), pltpu.VMEM((rows, d), F32), pltpu.VMEM((rows, d), BF), pltpu.VMEM((rows, d), BF),
            pltpu.VMEM((rows, part), BF), pltpu.VMEM((rows, part), BF),
            pltpu.VMEM((2, part, d), BF), pltpu.VMEM((2, d, part), BF),
            pltpu.SemaphoreType.DMA((22,)),
        ],
        out_shape=[
            struct((rows, d), F32), struct((rows, d), BF), struct((d, rows), BF), struct((rows, d), BF),
            struct((rows, d), BF), struct((part + d, d), BF), struct((part + d, d), BF),
            struct((1, ff), F32),
        ],
        estimate=EST["ffn_own"],
        name="ffn_own",
        mib=56,
    )(bits, x, ctx_own, ctx_other, wo_own, vec, wo_mine, wo_far, og, wu, wd)


BLOCK_BITS = 4


def sub_block(s, q, x, n):
    out = q + 2 * x
    for k in range(2, n):
        out = out + (((s >> (n - 1 - k)) & 1) << k)
    return out


def put_blocks(grads, stack, q, n, sem, at):
    count = 1 << (n - 2)
    size = grads[0].shape[0] // count
    return [
        pull(
            grads[x].at[s * size : (s + 1) * size, :],
            stack.at[pl.ds(pl.multiple_of(sub_block(s, q, x, n) * size, size), size), :],
            sem.at[at + x * count + s],
        )
        for x in range(2)
        for s in range(count)
    ]


def gather_weights(bits_ref, near, near_x, rest, w, sem, at):
    rows = near.shape[0]
    b = bits_ref[1]
    return [
        pull(near, w.at[block(b, rows), :], sem.at[at]),
        pull(near_x, w.at[block(1 - b, rows), :], sem.at[at + 1]),
        pull(rest, w.at[2 * rows :, :], sem.at[at + 2]),
    ]


def ffn_mine_kernel(
    n, bits_ref, n2_ref, b_ref, near_h, near_x_h, rest_h, og_h, n2t_h, out_h, dn_h, stack_h, db_ref,
    w_ref, og, n2t, out, dn, outb, dnb, act_s, dh_s, gd, gu, sem,
):
    d = og.shape[1]
    part = w_ref.shape[0] - d
    c = bits_ref[0]
    bias_at = b_ref.shape[1] - 2 * part
    at = 10 + (1 << (n - 1))
    loads = gather_weights(bits_ref, near_h, near_x_h, rest_h, w_ref, sem, at)
    loads += [pull(og_h, og, sem.at[0]), pull(n2t_h, n2t, sem.at[1])]
    for load in loads:
        load.wait()
    stores = []

    def flush(i, blk):
        sl = pl.ds(i * blk, blk)
        outb[sl, :] = out[sl, :].astype(BF)
        dnb[sl, :] = dn[sl, :].astype(BF)
        stores.append(pull(outb.at[sl, :], out_h.at[sl, :], sem.at[2 + i]))
        stores.append(pull(dnb.at[sl, :], dn_h.at[sl, :], sem.at[6 + i]))

    bias = b_ref[:, pl.ds(pl.multiple_of(bias_at + c * part, 128), part)]
    db_ref[...] = ffn_quarter(
        n2_ref, n2t, og, w_ref.at[0:d, :], w_ref.at[d:, :], bias, out, dn, act_s, dh_s, gd, gu, True, None, flush
    )
    stores += put_blocks((gd, gu), stack_h, c, n, sem, 10)
    for store in stores:
        store.wait()


def ffn_mine(bits, n2, near, near_x, rest, bias, og, n2t, after=()):
    rows, d = og.shape
    part = 2 * near.shape[0] + rest.shape[0] - d
    n = min(bits.shape[0], BLOCK_BITS)
    return call(
        lambda *refs: ffn_mine_kernel(n, *refs),
        after,
        prefetch=1,
        in_specs=[whole((rows, d)), whole(bias.shape)] + [ANY] * 5,
        out_specs=[ANY] * 3 + [whole_out((1, part))],
        scratch=[
            pltpu.VMEM((d + part, d), BF),
            pltpu.VMEM((rows, d), BF), pltpu.VMEM((d, rows), BF), pltpu.VMEM((rows, d), F32), pltpu.VMEM((rows, d), F32),
            pltpu.VMEM((rows, d), BF), pltpu.VMEM((rows, d), BF),
            pltpu.VMEM((rows, part), BF), pltpu.VMEM((rows, part), BF), pltpu.VMEM((part, d), BF), pltpu.VMEM((d, part), BF),
            pltpu.SemaphoreType.DMA((13 + (1 << (n - 1)),)),
        ],
        out_shape=[
            struct((rows, d), BF), struct((rows, d), BF), struct((4 * part, d), BF), struct((1, part), F32),
        ],
        estimate=EST["ffn_mine"],
        name="ffn_mine",
        mib=56,
    )(bits, n2, bias, near, near_x, rest, og, n2t)


def ffn_far_kernel(
    at, n, bits_ref, len_ref, n2_ref, b_ref, vec_ref, near_h, near_x_h, rest_h, og_h, n2t_h, mid_h, out1_h, dn1_h, out2_h, dn2_h,
    co_h, cx_h, woo_h, wom_h, wof_h, stack_in,
    lay_h, gm_h, dco_h, dcx_h, stack_h, dwoo_h, dwox_h, sums_ref, db_ref,
    w_ref, og, n2t, mid, out1, dn1, out2, dn2, co, cx, woo, wox, out, dn, act_s, dh_s, gd, gu, lay, gmb, dco, dcx, dwoo, dwox, sem,
):
    rows, d = og.shape
    part = w_ref.shape[0] - d
    half = co.shape[1]
    c = bits_ref[0]
    length = len_ref[0]
    bias_at = b_ref.shape[1] - 2 * part
    first = gather_weights(bits_ref, near_h, near_x_h, rest_h, w_ref, sem, 18 + (1 << (n - 1)))
    loads = [
        pull(src, dst, sem.at[i])
        for i, (src, dst) in enumerate((
            (og_h, og), (n2t_h, n2t), (mid_h, mid), (dn1_h, dn1), (dn2_h, dn2), (out1_h, out1), (out2_h, out2),
            (woo_h, woo), (wom_h, wox.at[block(c, half // 2), :]), (wof_h, wox.at[block(1 - c, half // 2), :]),
            (co_h, co), (cx_h, cx),
        ))
    ]
    for load in first + loads[:1]:
        load.wait()
    sums_ref[...] = jnp.zeros_like(sums_ref)
    stores = []

    def finish(i, blk):
        if i == 0:
            for load in loads[1:]:
                load.wait()
        sl = slice(i * blk, (i + 1) * blk)
        v = mid[sl, :]
        out_sum = out1[sl, :].astype(F32) + out2[sl, :].astype(F32) + out[sl, :]
        lay[sl, :] = (v + out_sum + vec_ref[:, at.down_bias]).astype(BF)
        unit, r = norm_rows(v)
        gn = dn1[sl, :].astype(F32) + dn2[sl, :].astype(F32) + dn[sl, :]
        o = og[sl, :].astype(F32)
        g = o + norm_back(gn * vec_ref[:, at.gain2], unit, r)
        mid[sl, :] = g
        low = g.astype(BF)
        gmb[sl, :] = low
        for k, val in enumerate((g, gn * unit, gn, o)):
            sums_ref[k : k + 1, :] += jnp.sum(val, axis=0, keepdims=True)
        valid = lax.broadcasted_iota(jnp.int32, (blk, 1), 0) + i * blk < length
        dco[sl, :] = jnp.where(valid, dot(low, woo[...], 1, 1), 0.0).astype(BF)
        dcx[sl, :] = jnp.where(valid, dot(low, wox[...], 1, 1), 0.0).astype(BF)

    bias = b_ref[:, pl.ds(pl.multiple_of(bias_at + (1 - c) * part, 128), part)]
    db_ref[...] = ffn_quarter(
        n2_ref, n2t, og, w_ref.at[0:d, :], w_ref.at[d:, :], bias, out, dn, act_s, dh_s, gd, gu, True, None, finish
    )
    stores = put_blocks((gd, gu), stack_h, 1 - c, n, sem, 18)
    stores += [
        pull(src, dst, sem.at[12 + k])
        for k, (src, dst) in enumerate(((lay, lay_h), (mid, gm_h), (dco, dco_h), (dcx, dcx_h)))
    ]
    dwoo[...] = dot(gmb[...], co[...], 0, 0).astype(BF)
    dwox[...] = dot(gmb[...], cx[...], 0, 0).astype(BF)
    stores += [pull(dwoo, dwoo_h, sem.at[16]), pull(dwox, dwox_h, sem.at[17])]
    for store in stores:
        store.wait()


def ffn_far(
    at, bits, length, n2, near, near_x, rest, bias, vec, og, n2t, mid, out1, dn1, out2, dn2, ctx_own, ctx_other, wo_own,
    wo_mine, wo_far, stack, after=(),
):
    rows, d = og.shape
    part = 2 * near.shape[0] + rest.shape[0] - d
    n = min(bits.shape[0], BLOCK_BITS)
    half = ctx_own.shape[1]
    bf = lambda *shape: pltpu.VMEM(shape, BF)
    f32 = lambda *shape: pltpu.VMEM(shape, F32)
    return call(
        lambda *refs: ffn_far_kernel(at, n, *refs),
        after,
        prefetch=2,
        in_specs=[whole((rows, d)), whole(bias.shape), whole(vec.shape)] + [ANY] * 16,
        out_specs=[ANY] * 7 + [whole_out((8, d)), whole_out((1, part))],
        scratch=[
            bf(d + part, d), bf(rows, d), bf(d, rows), f32(rows, d), bf(rows, d), bf(rows, d), bf(rows, d), bf(rows, d),
            bf(rows, half), bf(rows, half), bf(half, d), bf(half, d), f32(rows, d), f32(rows, d),
            bf(rows, part), bf(rows, part), bf(part, d), bf(d, part), bf(rows, d), bf(rows, d), bf(rows, half),
            bf(rows, half), bf(d, half), bf(d, half), pltpu.SemaphoreType.DMA((21 + (1 << (n - 1)),)),
        ],
        out_shape=[
            struct((rows, d), BF), struct((rows, d), F32), struct((rows, half), BF), struct((rows, half), BF),
            struct(stack.shape, BF), struct((d, half), BF), struct((d, half), BF), struct((8, d), F32), struct((1, part), F32),
        ],
        alias={20: 4},
        estimate=EST["ffn_far"],
        name="ffn_far",
        mib=56,
    )(
        bits, length, n2, bias, vec, near, near_x, rest, og, n2t, mid, out1, dn1, out2, dn2, ctx_own, ctx_other, wo_own,
        wo_mine, wo_far, stack,
    )


def by_pairs(wcat, matrices, rows, width):
    for p in range(width // 128):
        for i in range(3):
            to = slice((3 * p + i) * 128, (3 * p + i + 1) * 128)
            ref, base = matrices[i]
            wcat[rows, to] = ref[:, base + p * 128 : base + (p + 1) * 128]


def share_kernel(bits_ref, g_ref, wm, wf, out_ref, wcat):
    width = g_ref.shape[1] // 3
    c = bits_ref[0]
    half = wm.shape[0]

    @pl.when(pl.program_id(0) == 0)
    def _():
        for ref, part in ((wm, c), (wf, 1 - c)):
            by_pairs(wcat, [(ref, i * width) for i in range(3)], block(part, half), width)

    out_ref[...] = dot(g_ref[...], wcat[...], 1, 1).astype(BF)


def input_share(bits, g, w_mine, w_far, after=()):
    rows, cols = g.shape
    d = 2 * w_mine.shape[0]
    blk = 512
    row = lambda w: pl.BlockSpec((blk, w), lambda i, *_: (i, 0))
    return call(
        share_kernel, after, prefetch=1, grid=(rows // blk,),
        in_specs=[row(cols), whole(w_mine.shape), whole(w_far.shape)], out_specs=row(d),
        out_shape=struct((rows, d), BF), scratch=[pltpu.VMEM((d, cols), BF)],
        estimate=EST["share"], name="input_share", mib=56,
    )(bits, g, w_mine, w_far)


def input_grad_kernel(
    at, bits_ref, x_ref, gm_ref, vec_ref, g_ref, share_ref, wq, wk, wv, sums2, sums_o, sums_x, db_own, db_mine, db_far,
    out_ref, small_ref, wcat,
):
    width = wq.shape[1]
    d = x_ref.shape[1]

    @pl.when(pl.program_id(0) == 0)
    def _():
        by_pairs(wcat, [(ref, 0) for ref in (wq, wk, wv)], slice(None), width)
        small_ref[...] = jnp.zeros_like(small_ref)
        for k in range(4):
            small_ref[1 + k // 2 : 2 + k // 2, (k % 2) * d : (k % 2 + 1) * d] = sums2[k : k + 1, :]
        low_core = bits_ref[0] == 0
        db_other = jnp.concatenate(
            [jnp.where(low_core, db_mine[...], db_far[...]), jnp.where(low_core, db_far[...], db_mine[...])], 1
        )
        first = bits_ref[bits_ref.shape[0] - 1] == 0
        for row, own, other in ((3, sums_o[...], sums_x[...]), (4, db_own[...], db_other)):
            small_ref[row : row + 1, 0 : own.shape[1]] = jnp.where(first, own, other)
            small_ref[row + 2 : row + 3, 0 : own.shape[1]] = jnp.where(first, other, own)

    gn = dot(g_ref[...], wcat[...], 1, 1) + share_ref[...].astype(F32)
    n, r = norm_rows(x_ref[...].astype(F32))
    out_ref[...] = (gm_ref[...] + norm_back(gn * vec_ref[:, at.gain1], n, r)).astype(BF)
    small_ref[0:1, 0:d] += jnp.sum(gn * n, axis=0, keepdims=True)
    small_ref[0:1, d:] += jnp.sum(gn, axis=0, keepdims=True)


def input_grad(at, bits, x, gm, vec, g, share, wq, wk, wv, sums, after=()):
    rows, d = x.shape
    width = wq.shape[1]
    blk = 256
    row = lambda w: pl.BlockSpec((blk, w), lambda i, *_: (i, 0))
    return call(
        lambda *refs: input_grad_kernel(at, *refs),
        after,
        prefetch=1,
        grid=(rows // blk,),
        in_specs=[row(d), row(d), whole(vec.shape), row(3 * width), row(d)]
        + [whole((d, width))] * 3
        + [whole(v.shape) for v in sums],
        out_specs=[row(d), whole_out((8, 2 * d))],
        out_shape=[struct((rows, d), BF), struct((8, 2 * d), F32)],
        scratch=[pltpu.VMEM((d, 3 * width), BF)],
        estimate=EST["input_grad"],
        name="input_grad",
        mib=56,
    )(bits, x, gm, vec, g, share, wq, wk, wv, *sums)


def wide_qkv(bits, near, far, after=()):
    size, width = near[0].shape
    width //= 4

    def kernel(bits_ref, *refs):
        ins, outs, turn = refs[:4], refs[4:8], refs[8]
        base = (pl.program_id(0) != bits_ref[0]).astype(jnp.int32) * 2
        for half in range(2):
            want = base + (half != bits_ref[1]).astype(jnp.int32)
            rows = slice(half * size, (half + 1) * size)
            for k in range(4):

                @pl.when(want == k)
                def _():
                    ref = ins[k]
                    for i, out in enumerate(outs[:3]):
                        for p in range(width // 128):
                            src = slice((3 * p + i) * 128, (3 * p + i + 1) * 128)
                            out[rows, p * 128 : (p + 1) * 128] = ref[:, src].astype(F32)
                    turn[rows, :] = ref[:, 3 * width :].astype(F32)

        outs[3][...] = turn[...].T

    return call(
        kernel, after, prefetch=1, grid=(2,),
        in_specs=[whole((size, 4 * width))] * 4,
        out_specs=[pl.BlockSpec((2 * size, width), lambda i, *_: (i, 0))] * 3
        + [pl.BlockSpec((width, 2 * size), lambda i, *_: (0, i))],
        out_shape=[struct((4 * size, width), F32)] * 3 + [struct((width, 4 * size), F32)],
        scratch=[pltpu.VMEM((2 * size, width), F32)], estimate=EST["move"], name="wide_qkv", mib=56,
    )(bits, *near, *far)


def wide_ffn(bits, stack, after=()):
    rows, d = stack.shape
    n = min(bits.shape[0], BLOCK_BITS)
    part = rows // 4
    count = 1 << (n - 2)
    size = part // count

    def kernel(bits_ref, *refs):
        for x in range(2):
            for k in range(2):
                refs[4 + x][k * size : (k + 1) * size, :] = refs[2 * x + k][...].astype(F32)

    def place(x, k):
        return lambda q, t, *_: (sub_block(2 * t + k, q, x, n), 0)

    return call(
        kernel, after, prefetch=1, grid=(2, count // 2),
        in_specs=[pl.BlockSpec((size, d), place(x, k)) for x in range(2) for k in range(2)],
        out_specs=[
            pl.BlockSpec((2 * size, d), lambda q, t, *_: (q * (count // 2) + t, 0)),
            pl.BlockSpec((2 * size, d), lambda q, t, *_: (t, q)),
        ],
        out_shape=[struct((2 * part, d), F32), struct((part, 2 * d), F32)],
        estimate=EST["move"], name="wide_ffn", mib=56,
    )(bits, stack, stack, stack, stack)


def wide_both(bits, stack, pieces, after=()):
    rows, d = stack.shape
    n = min(bits.shape[0], BLOCK_BITS)
    part = rows // 2
    count = 1 << (n - 2)
    size = part // count // 2

    def kernel(bits_ref, *refs):
        blocks, ins, outs = refs[:4], refs[4:8], refs[8:]
        base = (pl.program_id(0) != bits_ref[0]).astype(jnp.int32) * 2
        t = pl.program_id(1)
        for x in range(2):
            for k in range(2):
                outs[x][2 * k * size : (2 * k + 1) * size, :] = blocks[2 * x + k][...].astype(F32)
            want = base + (x != bits_ref[1]).astype(jnp.int32)
            for p in range(4):

                @pl.when(want == p)
                def _():
                    for k in range(2):
                        src = pl.ds(pl.multiple_of((2 * t + k) * size, size), size)
                        outs[x][(2 * k + 1) * size : (2 * k + 2) * size, :] = ins[p][src, :].astype(F32)

    def place(x, k):
        return lambda q, t, *_: (sub_block(2 * t + k, q, x, n), 0)

    return call(
        kernel, after, prefetch=1, grid=(2, count // 2),
        in_specs=[pl.BlockSpec((size, d), place(x, k)) for x in range(2) for k in range(2)]
        + [whole(p.shape) for p in pieces],
        out_specs=[
            pl.BlockSpec((4 * size, d), lambda q, t, *_: (q * (count // 2) + t, 0)),
            pl.BlockSpec((4 * size, d), lambda q, t, *_: (t, q)),
        ],
        out_shape=[struct((2 * part, d), F32), struct((part, 2 * d), F32)],
        estimate=EST["move"], name="wide_both", mib=56,
    )(bits, stack, stack, stack, stack, *pieces)


class Links:
    def __init__(self, dp_size):
        self.size = dp_size
        self.bits = dp_size.bit_length() - 1
        index = lax.axis_index("dp")
        digits = [(index >> i) & 1 for i in range(self.bits)] + [lax.axis_index("tensor")]
        self.value = jnp.stack(digits).astype(jnp.int32)

    def swap(self, value, at):
        return lax.ppermute(value, "dp", [(i, i ^ (1 << at)) for i in range(self.size)])

    def across(self, value):
        return lax.ppermute(value, "tensor", [(0, 1), (1, 0)])

    def join(self, mine, other, at, after=()):
        half, width = mine.shape
        if half % 16:
            low = self.value[at] == 0
            return jnp.concatenate([jnp.where(low, mine, other), jnp.where(low, other, mine)], 0)

        def moves(bits, ins, outs):
            return [
                (ins[0], outs[0].at[block(bits[at], half), :]), (ins[1], outs[0].at[block(1 - bits[at], half), :])
            ]

        return arrange(self.value, [mine, other], [(2 * half, width)], moves, "join", after)[0]


def halve(bits, parts, bit, after=()):
    count = len(parts)
    parts = lax.optimization_barrier((*parts, *after))[:count]
    size = parts[0].shape[0] // 2

    def half(at):
        return sum(lax.dynamic_slice_in_dim(v, at * size, size, 0).astype(F32) for v in parts).astype(BF)

    return half(1 - bits[bit]), half(bits[bit])


class Halve:
    def __init__(self, links, keep, recv):
        self.links, self.keep, self.recv, self.at = links, keep, recv, 0
        low = min(links.bits, BLOCK_BITS)
        self.order = [*range(low), *reversed(range(low, links.bits))]
        self.done = False

    def advance(self, after):
        links = self.links
        self.at += 1
        self.done = self.at == links.bits
        if self.done:
            return
        bit = self.order[self.at]
        send, self.keep = halve(links.value, (self.keep, self.recv), bit, after)
        self.recv = links.swap(send, bit)


RIDE = 16


def ride_kernel(rows, cut, bits_ref, *refs):
    *ins, small_ref, send_ref, keep_ref, next_ref, acc = refs
    width = small_ref.shape[1]
    small = small_ref[...]
    total = None
    for ref in ins:
        value = ref[0:rows, :].astype(F32)
        total = value if total is None else total + value
        if ref.shape[0] > rows:
            riding = ref[rows : rows + RIDE, :].astype(F32)
            small = small + riding[0:8] + riding[8:16]
    next_ref[...] = small
    if send_ref is None:
        keep_ref[...] = total.astype(BF)
        return
    acc[...] = total
    if cut is None:
        size = rows
        send_ref[0:size, :] = total.astype(BF)
        keep_ref[...] = total.astype(BF)
    else:
        size = rows // 2
        bit = bits_ref[cut]
        low, high = acc[0:size, :], acc[size : 2 * size, :]
        send_ref[0:size, :] = jnp.where(bit == 0, high, low).astype(BF)
        keep_ref[...] = jnp.where(bit == 0, low, high).astype(BF)
    high = small.astype(BF)
    send_ref[size:, :] = jnp.concatenate([high, (small - high.astype(F32)).astype(BF)], 0)


def ride(bits, parts, small, cut, last, after=()):
    rows = parts[0].shape[0]
    width = small.shape[1]
    size = rows // 2 if cut is not None else rows
    shapes = [struct((size, width), BF), struct(small.shape, F32)]
    if not last:
        shapes.insert(0, struct((size + RIDE, width), BF))

    def kernel(bits_ref, *refs):
        refs = list(refs)
        if last:
            refs.insert(len(parts) + 1, None)
        ride_kernel(rows, cut, bits_ref, *refs)

    out = call(
        kernel, after, prefetch=1, in_specs=[whole(a.shape) for a in (*parts, small)],
        out_specs=[whole_out(t.shape) for t in shapes], out_shape=shapes,
        scratch=[pltpu.VMEM((rows, width), F32)], estimate=EST["move"], name="ride",
    )(bits, *parts, small)
    return (None, *out) if last else out


def layer(
    dp_size, inputs, lengths, norm1_gain, norm1_shift, query_weight, query_bias, key_weight, key_bias, value_weight,
    value_bias, out_weight, out_bias, norm2_gain, norm2_shift, up_weight, up_bias, down_weight, down_bias, out_grad,
):
    rows, d = inputs.shape
    width = query_weight.shape[1]
    ff = up_weight.shape[1]
    part = ff // 2
    links = Links(dp_size)
    bits = links.value
    tensor = lax.axis_index("tensor")
    length = jnp.where(tensor == 0, lengths[:1], lengths[1:])
    cos, sin = (jnp.asarray(t) for t in rotary_tables(rows))
    at = Row(d, width, ff)
    vec = [norm1_gain, norm1_shift, out_bias, norm2_gain, norm2_shift, down_bias, query_bias, key_bias, value_bias, up_bias]
    vec = jnp.concatenate([v.reshape(1, -1) for v in vec], 1)

    def qkv_moves(bits_ref, ins, outs):
        return [
            (w.at[block(bits_ref[0], d // 2), :], outs[0].at[:, i * width : (i + 1) * width]) for i, w in enumerate(ins)
        ]

    near_rows = 5 * d // 12
    half = width // 2
    def cut_moves(bits_ref, ins, outs):
        c, b = bits_ref[0], bits_ref[1]
        wu, wd, wo = ins
        near, rest, out_half = outs
        cols = block(c, part)
        return [
            (wo.at[block(c, half), :], out_half),
            (wu.at[block(b, near_rows), cols], near),
            (wu.at[2 * near_rows :, cols], rest.at[0 : d - 2 * near_rows, :]),
            (wd.at[block(c, part), :], rest.at[d - 2 * near_rows :, :]),
        ]

    qkv_mine, = arrange(bits, [query_weight, key_weight, value_weight], [(d // 2, 3 * width)], qkv_moves, "cut_qkv", mib=56)
    qkv_mine = links.across(qkv_mine)
    normed, normed_t, *own, ctx_own, aug_own, near, rest, out_half = heads_own(
        at, cut_moves, [(near_rows, d), (d + part - 2 * near_rows, d), (half, d)], bits, length, inputs, vec, query_weight,
        key_weight, value_weight, cos, sin, up_weight, down_weight, out_weight,
    )
    bias_x = links.across(vec)
    near, out_mine = links.across(near), links.across(out_half)
    qkv_mine, _ = lax.optimization_barrier((qkv_mine, ctx_own))
    qkv_far = links.swap(qkv_mine, 0)
    *other, ctx_x, aug_x = heads_other(at, bits, length, normed, qkv_mine, qkv_far, bias_x, cos, sin, after=(ctx_own,))
    near, out_mine, rest, ctx_x = lax.optimization_barrier((near, out_mine, rest, ctx_x))
    out_far = links.swap(out_mine, 0)
    rest = links.across(rest)
    near_x = links.swap(near, 1)
    near_far = links.swap(near, 0)
    mid, n2, n2t, out1, dn1, w_send, w_keep, dbu = ffn_own(
        at, bits, inputs, ctx_own, ctx_x, out_weight, vec, out_mine, out_far, out_grad, up_weight, down_weight
    )

    w_recv = links.swap(w_send, 0)
    near_x_far, rest_far = links.swap(near_x, 0), links.swap(rest, 0)
    out2, dn2, stack, dbu_mine = ffn_mine(bits, n2, near, near_x, rest, bias_x, out_grad, n2t, after=(mid,))
    own_sum = Halve(links, w_keep, w_recv)
    own_sum.advance((out2,))
    layer_out, gm, g_own, g_x, stack, dwo, dwo_x, sums2, dbu_far = ffn_far(
        at, bits, length, n2, near_far, near_x_far, rest_far, bias_x, vec, out_grad, n2t, mid, out1, dn1, out2, dn2,
        ctx_own, ctx_x, out_weight, out_mine, out_far, stack, after=(own_sum.keep,),
    )
    blocks = min(dp_size, 1 << BLOCK_BITS)

    def turned(rows_, first, second):
        return rows_.reshape(first, second, -1, d).swapaxes(0, 1).reshape(-1, d)

    if dp_size > blocks:
        stack = turned(stack, blocks, dp_size // blocks)
    stack = lax.psum_scatter(stack, "dp", scatter_dimension=0, tiled=True)
    n = d // 2
    gx, sums_x, qx_s, qx_k = attend_back(
        bits, length, *other, g_x, ctx_x, aug_x, cos, sin, normed_t, dwo_x
    )
    qx_r = links.swap(qx_s, 0)
    own_sum.advance((qx_k,))
    share = input_share(bits, gx, qkv_mine, qkv_far, after=(own_sum.keep,))
    qx_k, qx_r, _ = lax.optimization_barrier((qx_k, qx_r, share))
    qx = (qx_k.astype(F32) + qx_r.astype(F32)).astype(BF)
    qx_y = links.across(qx)
    go, sums_o, qo_s, qo_k = attend_back(
        bits, length, *own, g_own, ctx_own, aug_own, cos, sin, normed_t, dwo, after=(qx,), est=12
    )
    own_sum.advance((qo_k,))
    qo_r = links.swap(qo_s, 0)
    q, = fold(bits, [(qo_k, 0, 0, n), (qx_y, 0, 0, n)], n, [(0, n)], "fold_qkv_y", after=(own_sum.keep,), est=busy(8))
    q_s, q_k = halve(bits, (q, qo_r), 1)
    q_r = links.swap(q_s, 1)
    input_grad_out, small = input_grad(
        at, bits, inputs, gm, vec, go, share, query_weight, key_weight, value_weight,
        (sums2, sums_o, sums_x, dbu, dbu_mine, dbu_far), after=(q_k,),
    )
    last = links.bits - 1
    small, = fold(bits, [(small, 0, 0, 8), (links.swap(small, 1), 0, 0, 8)], 8, [(0, 8)], "fold_small")
    send, keep1, small = ride(bits, [q_k, q_r], small, 2 if last > 2 else None, False, (q_k, own_sum.recv))
    q_parts = [keep1, links.swap(send, 2)]
    stack, keep1 = lax.optimization_barrier((stack, keep1))
    stack_r = links.across(stack)
    while not own_sum.done:
        own_sum.advance((keep1,))
    size = stack.shape[0]
    parts = [(v, 0, 0, size) for v in (stack, stack_r, own_sum.keep, own_sum.recv)][1:]
    split = dp_size == blocks
    cuts = [(0, size // 2), (size // 2, size // 2)] if split else [(0, size)]
    stack, *piece = fold(bits, parts, size, cuts, "fold_stack", after=q_parts)
    gathered = lax.all_gather(stack, "dp", axis=0, tiled=True)
    if dp_size > blocks:
        gathered = turned(gathered, dp_size // blocks, blocks)
    piece_r = links.swap(piece[0], last) if split else None

    after = (stack,)
    parts = q_parts
    for bit in range(3, links.bits):
        send, keep, small = ride(bits, parts, small, bit if bit < last else None, False, after)
        after = ()
        parts = [keep, links.swap(send, bit)]
    if split:
        piece = piece[0]
        for bit in reversed(range(2, links.bits)):
            piece = links.join(piece, piece_r, bit, after=(keep,))
            piece_r = links.swap(piece, bit - 1)
        after = (piece,)
    _, q, small = ride(bits, parts, small, None, True, after)
    for bit in reversed(range(2, last)):
        q_r = links.swap(q, bit)
        if bit == last - 1:
            size = small.shape[0]
            for swap in (links.across, lambda v: links.swap(v, 0)):
                parts = [(small, 0, 0, size), (swap(small), 0, 0, size)]
                small, = fold(bits, parts, size, [(0, size)], "fold_small", after=(q,))
        q = links.join(q, q_r, bit, after=(small,))
    q_r = links.swap(q, 1)
    q_far = links.swap(q, 0)
    if split:
        piece_r, _ = lax.optimization_barrier((piece_r, q))
        pieces = [piece, piece_r, links.swap(piece, 0), links.swap(piece_r, 0)]
        grad_down, grad_up = wide_both(bits, gathered, pieces, after=(q,))
    else:
        grad_down, grad_up = wide_ffn(bits, gathered, after=(q,))
    q_r, grad_up = lax.optimization_barrier((q_r, grad_up))
    q_r_far = links.swap(q_r, 0)
    grad_q, grad_k, grad_v, grad_out = wide_qkv(bits, (q, q_r), (q_far, q_r_far), after=(grad_up,))

    gain1, shift1, out_b, gain2, shift2, down_b = (small[i // 2, (i % 2) * d : (i % 2 + 1) * d] for i in range(6))
    mine = lax.dynamic_slice_in_dim(small, 3 + 2 * tensor, 2, 0)
    qkv_bias = mine[0, : 3 * width].reshape(-1, 3, 128)
    return (
        layer_out, input_grad_out, gain1, shift1,
        grad_q, qkv_bias[:, 0].reshape(-1), grad_k, qkv_bias[:, 1].reshape(-1), grad_v, qkv_bias[:, 2].reshape(-1),
        grad_out, out_b, gain2, shift2, grad_up, mine[1, :ff], grad_down, down_b,
    )


def solution(mesh):
    rows = P(("dp", "tensor"), None)
    cols = P(None, "tensor")
    tens = P("tensor")
    return jax.shard_map(
        lambda *args: layer(mesh.shape["dp"], *args),
        mesh=mesh,
        in_specs=(
            rows, P("dp"), P(), P(), cols, tens, cols, tens, cols, tens, P("tensor", None), P(), P(), P(), cols, tens,
            P("tensor", None), P(), rows,
        ),
        out_specs=(
            rows, rows, P(), P(), cols, tens, cols, tens, cols, tens, P("tensor", None), P(), P(), P(), cols, tens,
            P("tensor", None), P(),
        ),
        check_vma=False,
    )
```

```python
import math

import jax
import jax.numpy as jnp
import numpy as np
from jax import lax
from jax.experimental import pallas as pl
from jax.experimental.pallas import tpu as pltpu
from jax.sharding import PartitionSpec as P

HEAD_DIM = 64
EPS = 1e-05
LOG2E = math.log2(math.e)
LN2 = math.log(2.0)
F32 = jnp.float32
BF = jnp.bfloat16
BIG = -1e30


def dot(a, b, ca=1, cb=0):
    return lax.dot_general(a, b, (((ca,), (cb,)), ((), ())), preferred_element_type=F32)


def cost(macs, nbytes, exps=0):
    return pl.CostEstimate(flops=int(2 * macs), bytes_accessed=int(nbytes), transcendentals=int(exps))


def busy(micros):
    return pl.CostEstimate(flops=int(micros * 1.1e9), bytes_accessed=1000, transcendentals=0)


EST = {
    "move": busy(0.01),
    "heads_own": busy(16),
    "heads_other": busy(100),
    "ffn_own": busy(0.01),
    "ffn_mine": busy(100),
    "ffn_far": busy(100),
    "share": busy(8),
    "input_grad": busy(8),
    "halve": busy(20),
}


def struct(shape, dtype):
    return jax.ShapeDtypeStruct(shape, dtype)


def whole(shape):
    return pl.BlockSpec(shape, lambda *_: (0,) * len(shape), pipeline_mode=pl.Buffered(1))


def whole_out(shape):
    return pl.BlockSpec(shape, lambda *_: (0,) * len(shape))


ANY = pl.BlockSpec(memory_space=pl.ANY)


def call(kernel, after, *, in_specs, out_specs, out_shape, estimate, name, grid=(1,), prefetch=0, scratch=(), alias=None, mib=28):
    after = tuple(after)
    n_in = prefetch + len(in_specs)

    def body(*refs):
        kernel(*refs[:n_in], *refs[n_in + len(after) :])

    run = pl.pallas_call(
        body,
        grid_spec=pltpu.PrefetchScalarGridSpec(
            num_scalar_prefetch=prefetch,
            grid=grid,
            in_specs=list(in_specs) + [ANY] * len(after),
            out_specs=out_specs,
            scratch_shapes=list(scratch),
        ),
        out_shape=out_shape,
        compiler_params=pltpu.CompilerParams(vmem_limit_bytes=mib << 20),
        input_output_aliases=alias or {},
        cost_estimate=estimate,
        name=name,
    )
    return lambda *args: run(*args, *after)


def norm_rows(v):
    mean = jnp.mean(v, axis=1, keepdims=True)
    cent = v - mean
    var = jnp.mean(cent * cent, axis=1, keepdims=True)
    r = lax.rsqrt(var + EPS)
    return cent * r, r


def norm_back(e, n, r):
    return r * (e - jnp.mean(e, axis=1, keepdims=True) - n * jnp.mean(e * n, axis=1, keepdims=True))


def rotary_tables(rows):
    half = HEAD_DIM // 2
    freq = (10000.0 ** (-2.0 * np.arange(half, dtype=np.float32) / HEAD_DIM)).astype(np.float32)
    ang = (np.arange(rows, dtype=np.float32)[:, None] * freq[None, :]).astype(np.float64)
    cos = np.cos(ang).astype(np.float32)
    sin = np.sin(ang).astype(np.float32)
    return np.concatenate([cos] * 4, 1), np.concatenate([-sin, sin] * 2, 1)


def swap_halves(v):
    lane = lax.broadcasted_iota(jnp.int32, v.shape, 1)
    return jnp.where((lane & 32) == 0, pltpu.roll(v, 96, 1), pltpu.roll(v, 32, 1))


def rotate(v, cos, sin):
    return v * cos + swap_halves(v) * sin


def rotate_back(v, cos, sin):
    return v * cos - swap_halves(v) * sin


class Row:
    def __init__(self, d, width, ff):
        at = 0
        for name, size in (
            ("gain1", d), ("shift1", d), ("out_bias", d), ("gain2", d), ("shift2", d), ("down_bias", d),
            ("qkv", 3 * width), ("up", ff),
        ):
            setattr(self, name, slice(at, at + size))
            at += size


def pull(src, dst, sem):
    copy = pltpu.make_async_copy(src, dst, sem)
    copy.start()
    return copy


def arrange(bits, arrays, shapes, moves, name, after=(), mib=28):
    def kernel(bits_ref, *refs):
        ins, outs, sem = refs[: len(arrays)], refs[len(arrays) : -1], refs[-1]
        copies = [pull(src, dst, sem.at[i]) for i, (src, dst) in enumerate(moves(bits_ref, ins, outs))]
        for copy in copies:
            copy.wait()

    return call(
        kernel,
        after,
        prefetch=1,
        in_specs=[ANY] * len(arrays),
        out_specs=[whole_out(shape) for shape in shapes],
        out_shape=[struct(shape, BF) for shape in shapes],
        scratch=[pltpu.SemaphoreType.DMA((8,))],
        estimate=EST["move"],
        name=name,
        mib=mib,
    )(bits, *arrays)


def block(bit, size):
    return pl.ds(pl.multiple_of(bit * size, size), size)


def fold(bits, parts, rows, outs, name, after=(), width=None, est=EST["move"]):
    arrays = [p[0] for p in parts]
    width = width or arrays[0].shape[1]
    dtype = arrays[0].dtype
    half = rows // 2
    shapes = [(half, width)] * 2 if isinstance(outs, int) else [(n, width) for _, n in outs]

    def kernel(bits_ref, *refs):
        ins, outs_r, acc = refs[: len(parts)], refs[len(parts) : -1], refs[-1]
        seen = []
        for ref, (_, src, dst, n) in zip(ins, parts):
            value = ref[src : src + n, 0:width].astype(F32)
            fresh = not any(dst < b and a < dst + n for a, b in seen)
            acc[dst : dst + n, :] = value if fresh else acc[dst : dst + n, :] + value
            seen.append((dst, dst + n))
        if isinstance(outs, int):
            bit = bits_ref[outs]
            for ref, at in zip(outs_r, (1 - bit, bit)):
                ref[...] = acc[pl.ds(pl.multiple_of(at * half, 8 if half % 8 == 0 else 1), half), :].astype(dtype)
        else:
            for ref, (start, n) in zip(outs_r, outs):
                ref[...] = acc[start : start + n, :].astype(dtype)

    return call(
        kernel,
        after,
        prefetch=1,
        in_specs=[whole(a.shape) for a in arrays],
        out_specs=[whole_out(shape) for shape in shapes],
        out_shape=[struct(shape, dtype) for shape in shapes],
        scratch=[pltpu.VMEM((rows, width), F32)],
        estimate=est,
        name=name,
    )(bits, *arrays)


def put_qkv(pre, cos, sin, q_ref, k_ref, v_ref):
    width = q_ref.shape[1]
    for i in range(width // 128):
        sl = slice(i * 128, (i + 1) * 128)
        q_ref[:, sl] = (rotate(pre[0][:, sl], cos, sin) * (LOG2E / 8.0)).astype(BF)
        k_ref[:, sl] = rotate(pre[1][:, sl], cos, sin).astype(BF)
        v_ref[:, sl] = pre[2][:, sl].astype(BF)


def split3(v):
    hi = v.astype(BF)
    rest = v - hi.astype(F32)
    mid = rest.astype(BF)
    lo = rest - mid.astype(F32)
    return hi.astype(F32), mid.astype(F32), lo


def spread(lane, first, one, two):
    out = jnp.where(lane == 0, first, 0.0)
    for at, part in enumerate((*split3(one), *split3(two))):
        out = jnp.where(lane == at + 1, part, out)
    return out.astype(BF)


def attend_pair(length, q_ref, k_ref, v_ref, ctx_ref, aug_ref):
    bq = 256
    rows = q_ref.shape[0]
    lane1 = lax.broadcasted_iota(jnp.int32, (1, 128), 1)
    krow = lax.broadcasted_iota(jnp.int32, (rows, 128), 0)
    klane = lax.broadcasted_iota(jnp.int32, (rows, 128), 1)
    lane = lax.broadcasted_iota(jnp.int32, (bq, 128), 1)
    qrow = lax.broadcasted_iota(jnp.int32, (bq, 128), 0)
    kaug = jnp.where((klane == 0) & (krow >= length), BIG, 0.0).astype(BF)
    k = jnp.concatenate([k_ref[...], kaug], 1)
    v = jnp.concatenate([v_ref[...], jnp.ones((rows, 128), BF)], 1)
    qaug = jnp.where(lane == 0, 1.0, 0.0).astype(BF)
    for i in range(rows // bq):
        sl = slice(i * bq, (i + 1) * bq)
        q = q_ref[sl, :]
        outs, totals = [], []
        for h in range(2):
            keep = ((lane1 < 64) if h == 0 else (lane1 >= 64)).astype(BF)
            s = dot(jnp.concatenate([q * keep, qaug], 1), k, 1, 1)
            top = jnp.max(s, axis=1, keepdims=True)
            p = jnp.exp2(s - top).astype(BF)
            o = dot(p, v)
            total = o[:, 128:]
            outs.append(o[:, :128] / total)
            totals.append(top + jnp.log2(total))
        ctx = jnp.where(lane < 64, outs[0], outs[1])
        ctx_ref[sl, :] = jnp.where(qrow + i * bq < length, ctx, 0.0).astype(BF)
        aug_ref[sl, :] = spread(lane, 1.0, totals[0], totals[1])


def attend_all(length, q, k, v, ctx, aug):
    for p in range(q.shape[1] // 128):
        sl = slice(p * 128, (p + 1) * 128)
        attend_pair(length, *(ref.at[:, sl] for ref in (q, k, v, ctx, aug)))


def heads_own_kernel(
    at, cut, bits_ref, len_ref, x_ref, vec_ref, wq_ref, wk_ref, wv_ref, cos_ref, sin_ref, wu_h, wd_h, wo_h,
    n_h, nt_h, q_h, k_h, v_h, ctx_h, aug_h, near_h, rest_h, half_h,
    n_s, nt_s, q_s, k_s, v_s, ctx_s, aug_s, near_s, rest_s, half_s, sem,
):
    rows = x_ref.shape[0]
    width = q_s.shape[1]
    loads = [
        pull(src, dst, sem.at[i]) for i, (src, dst) in enumerate(cut(bits_ref, (wu_h, wd_h, wo_h), (near_s, rest_s, half_s)))
    ]
    blk = 256
    bias = vec_ref[:, at.qkv]
    for i in range(rows // blk):
        sl = slice(i * blk, (i + 1) * blk)
        n, _ = norm_rows(x_ref[sl, :].astype(F32))
        low = (n * vec_ref[:, at.gain1] + vec_ref[:, at.shift1]).astype(BF)
        n_s[sl, :] = low
        nt_s[:, sl] = low.T
        pre = [
            dot(low, w[...]) + bias[:, j * width : (j + 1) * width] for j, w in enumerate((wq_ref, wk_ref, wv_ref))
        ]
        put_qkv(pre, cos_ref[sl, :], sin_ref[sl, :], *(ref.at[sl, :] for ref in (q_s, k_s, v_s)))
    for load in loads:
        load.wait()
    pairs = [
        (near_s, near_h), (rest_s, rest_h), (n_s, n_h), (nt_s, nt_h), (q_s, q_h), (k_s, k_h), (v_s, v_h), (half_s, half_h)
    ]
    stores = [pull(src, dst, sem.at[8 + i]) for i, (src, dst) in enumerate(pairs)]
    attend_all(len_ref[0], q_s, k_s, v_s, ctx_s, aug_s)
    stores += [pull(ctx_s, ctx_h, sem.at[16]), pull(aug_s, aug_h, sem.at[17])]
    for store in stores:
        store.wait()


def heads_own(at, cut, shapes, bits, length, x, vec, wq, wk, wv, cos, sin, wu, wd, wo, after=()):
    rows, d = x.shape
    width = wq.shape[1]
    outs = [(rows, d), (d, rows)] + [(rows, width)] * 5 + list(shapes)
    return call(
        lambda *refs: heads_own_kernel(at, cut, *refs),
        after,
        prefetch=2,
        in_specs=[whole(a.shape) for a in (x, vec, wq, wk, wv, cos, sin)] + [ANY] * 3,
        out_specs=[ANY] * len(outs),
        out_shape=[struct(shape, BF) for shape in outs],
        scratch=[pltpu.VMEM(shape, BF) for shape in outs] + [pltpu.SemaphoreType.DMA((18,))],
        estimate=EST["heads_own"],
        name="heads_own",
        mib=56,
    )(bits, length, x, vec, wq, wk, wv, cos, sin, wu, wd, wo)


def heads_other_kernel(
    at, bits_ref, len_ref, n_ref, wm_ref, wf_ref, b_ref, cos_ref, sin_ref, q_h, k_h, v_h, ctx_h, aug_h,
    q_s, k_s, v_s, ctx_s, aug_s, sem,
):
    rows = n_ref.shape[0]
    width = q_s.shape[1]
    half = wm_ref.shape[0]
    c = bits_ref[0]
    blk = 256
    for i in range(rows // blk):
        sl = slice(i * blk, (i + 1) * blk)
        pre = dot(n_ref[sl, block(c, half)], wm_ref[...]) + dot(n_ref[sl, block(1 - c, half)], wf_ref[...])
        pre = pre + b_ref[:, at.qkv]
        put_qkv(
            [pre[:, j * width : (j + 1) * width] for j in range(3)], cos_ref[sl, :], sin_ref[sl, :],
            *(ref.at[sl, :] for ref in (q_s, k_s, v_s)),
        )
    stores = [pull(src, dst, sem.at[i]) for i, (src, dst) in enumerate(((q_s, q_h), (k_s, k_h), (v_s, v_h)))]
    attend_all(len_ref[0], q_s, k_s, v_s, ctx_s, aug_s)
    stores += [pull(ctx_s, ctx_h, sem.at[3]), pull(aug_s, aug_h, sem.at[4])]
    for store in stores:
        store.wait()


def heads_other(at, bits, length, n, w_mine, w_far, bias, cos, sin, after=()):
    rows = n.shape[0]
    width = w_mine.shape[1] // 3
    outs = [(rows, width)] * 5
    return call(
        lambda *refs: heads_other_kernel(at, *refs),
        after,
        prefetch=2,
        in_specs=[whole(a.shape) for a in (n, w_mine, w_far, bias, cos, sin)],
        out_specs=[ANY] * 5,
        out_shape=[struct(shape, BF) for shape in outs],
        scratch=[pltpu.VMEM(shape, BF) for shape in outs] + [pltpu.SemaphoreType.DMA((5,))],
        estimate=EST["heads_other"],
        name="heads_other",
        mib=56,
    )(bits, length, n, w_mine, w_far, bias, cos, sin)


def attend_back_kernel(
    bq, bits_ref, len_ref, q_ref, k_ref, v_ref, g_ref, ctx_ref, aug_ref, cos_ref, sin_ref, nt_ref, wo_ref,
    d_ref, sum_ref, send_ref, keep_ref, dqt, dall, gaug,
):
    rows = q_ref.shape[0]
    length = len_ref[0]
    lane1 = lax.broadcasted_iota(jnp.int32, (1, 128), 1)
    krow = lax.broadcasted_iota(jnp.int32, (rows, 128), 0)
    klane = lax.broadcasted_iota(jnp.int32, (rows, 128), 1)
    lane = lax.broadcasted_iota(jnp.int32, (bq, 128), 1)
    k = k_ref[...]
    v = v_ref[...]
    kt = k.T
    dks, dvs = [], []
    for h in range(2):
        keep = ((lane1 < 64) if h == 0 else (lane1 >= 64)).astype(BF)
        first = 1 + 3 * h
        mine = jnp.where((klane >= first) & (klane < first + 3), -1.0, 0.0)
        kaug = jnp.where((klane == 0) & (krow >= length), BIG, mine).astype(BF)
        kh = jnp.concatenate([k * keep, kaug], 1)
        vh = jnp.concatenate([v * keep, mine.astype(BF)], 1)
        dk = jnp.zeros((rows, 128), F32)
        dv = jnp.zeros((rows, 128), F32)
        for i in range(rows // bq):
            sl = slice(i * bq, (i + 1) * bq)
            q = q_ref[sl, :]
            g = g_ref[sl, :]
            if h == 0:
                prod = g.astype(F32) * ctx_ref[sl, :].astype(F32)
                d0 = jnp.sum(jnp.where(lane < 64, prod, 0.0), 1, keepdims=True)
                d1 = jnp.sum(jnp.where(lane < 64, 0.0, prod), 1, keepdims=True)
                gaug[sl, :] = spread(lane, 0.0, d0, d1)
            st = dot(kh, jnp.concatenate([q, aug_ref[sl, :]], 1), 1, 1)
            pt = jnp.exp2(st)
            dpt = dot(vh, jnp.concatenate([g, gaug[sl, :]], 1), 1, 1)
            ds = (pt * dpt).astype(BF)
            dv = dv + dot(pt.astype(BF), g)
            dk = dk + dot(ds, q)
            dqt[h * 64 : (h + 1) * 64, sl] = dot(kt[h * 64 : (h + 1) * 64, :], ds)
        dks.append(dk)
        dvs.append(dv)
    cos = cos_ref[...]
    sin = sin_ref[...]
    dq = rotate_back(dqt[...].T * (1.0 / 8.0), cos, sin).astype(BF)
    dk = rotate_back(jnp.where(klane < 64, dks[0], dks[1]) * LN2, cos, sin).astype(BF)
    dv = jnp.where(klane < 64, dvs[0], dvs[1]).astype(BF)
    for at, val in enumerate((dq, dk, dv)):
        sl = slice(at * 128, (at + 1) * 128)
        d_ref[:, sl] = val
        sum_ref[:, sl] = jnp.sum(val.astype(F32), axis=0, keepdims=True)
    j = pl.program_id(0)
    dall[:, block(j, 384)] = jnp.concatenate([dq, dk, dv], 1)

    @pl.when(j == pl.num_programs(0) - 1)
    def _():
        half = send_ref.shape[0]
        c = bits_ref[0]
        for ref, part in ((send_ref, 1 - c), (keep_ref, c)):
            width = dall.shape[1]
            ref[:, 0:width] = dot(nt_ref[block(part, half), :], dall[...]).astype(BF)
            ref[:, width:] = wo_ref[block(part, half), :]


def attend_back(bits, length, q, k, v, g, ctx, aug, cos, sin, nt, wo, after=(), est=100):
    rows, width = q.shape
    d = 2 * width
    bs = pl.BlockSpec((rows, 128), lambda j, *_: (0, j))
    return call(
        lambda *refs: attend_back_kernel(256, *refs),
        after,
        prefetch=2,
        grid=(width // 128,),
        in_specs=[bs] * 6 + [whole((rows, 128))] * 2 + [whole(nt.shape), whole(wo.shape)],
        out_specs=[pl.BlockSpec((rows, 384), lambda j, *_: (0, j)), pl.BlockSpec((1, 384), lambda j, *_: (0, j))]
        + [whole_out((d // 2, 4 * width))] * 2,
        out_shape=[struct((rows, 3 * width), BF), struct((1, 3 * width), F32)] + [struct((d // 2, 4 * width), BF)] * 2,
        scratch=[pltpu.VMEM((128, rows), F32), pltpu.VMEM((rows, 3 * width), BF), pltpu.VMEM((rows, 128), BF)],
        estimate=busy(est),
        name="attend_back",
        mib=56,
    )(bits, length, q, k, v, g, ctx, aug, cos, sin, nt, wo)


def gelu_pair(h):
    z = jnp.abs(h) * (0.3275911 / math.sqrt(2.0)) + 1.0
    t = pl.reciprocal(z, approx=True)
    t = t * (2.0 - z * t)
    e = jnp.exp2(h * h * (-0.5 * LOG2E))
    poly = 0.5 * 1.061405429 * t - 0.5 * 1.453152027
    poly = poly * t + 0.5 * 1.421413741
    poly = poly * t - 0.5 * 0.284496736
    poly = poly * t + 0.5 * 0.254829592
    w = poly * t * e
    cdf = jnp.where(h >= 0.0, 1.0 - w, w)
    return h * cdf, cdf + h * e * (1.0 / math.sqrt(2.0 * math.pi))


def ffn_quarter(n2, n2t, og, wu, wd, bias, out_acc, dn_acc, act_s, dh_s, gd, gu, first, before=None, done=None, flush=None):
    rows, d = og.shape
    part = wd.shape[0]
    blk = 256
    dbias = jnp.zeros((1, part), F32)
    if before is not None:
        before(0, blk)
    for i in range(rows // blk):
        sl = slice(i * blk, (i + 1) * blk)
        if before is not None and i + 1 < rows // blk:
            before(i + 1, blk)
        h = dot(n2[sl, :], wu[...]) + bias
        act, slope = gelu_pair(h)
        act = act.astype(BF)
        dh = (slope * dot(og[sl, :], wd[...], 1, 1)).astype(BF)
        act_s[sl, :] = act
        dh_s[sl, :] = dh
        dbias = dbias + jnp.sum(dh.astype(F32), axis=0, keepdims=True)
        o = dot(act, wd[...])
        e = dot(dh, wu[...], 1, 1)
        out_acc[sl, :] = o if first else out_acc[sl, :] + o
        dn_acc[sl, :] = e if first else dn_acc[sl, :] + e
        if done is not None and i > 0:
            done(i - 1, blk)
    if done is not None:
        done(rows // blk - 1, blk)
    gd[...] = dot(act_s[...], og[...], 0, 0).astype(BF)
    if flush is not None:
        flush()
    gu[...] = dot(n2t[...], dh_s[...]).astype(BF)
    return dbias


def ffn_own_kernel(
    at, bits_ref, x_ref, co_ref, cx_ref, woo_ref, vec_ref, wom_h, wof_h, og_h, wu_h, wd_h,
    mid_h, n2_h, n2t_h, out_h, dn_h, send_h, keep_h, db_ref,
    wox, og, wu, wd, mid, n2, n2t, out, dn, outb, dnb, act_s, dh_s, gd, gu, sem,
):
    rows, d = x_ref.shape
    part = wu_h.shape[1] // 2
    c = bits_ref[0]
    cols = [block(p, part) for p in (1 - c, c)]
    biases = [pl.ds(pl.multiple_of(at.up.start + p * part, 128), part) for p in (1 - c, c)]
    quarter = wom_h.shape[0]
    first = [
        pull(wom_h, wox.at[block(c, quarter), :], sem.at[18]), pull(wof_h, wox.at[block(1 - c, quarter), :], sem.at[19])
    ]
    loads = [pull(og_h, og, sem.at[0])]
    for q in range(2):
        loads.append(pull(wu_h.at[:, cols[q]], wu.at[q], sem.at[1 + 2 * q]))
        loads.append(pull(wd_h.at[cols[q], :], wd.at[q], sem.at[2 + 2 * q]))
    for load in first:
        load.wait()
    stores = []

    def enter(i, blk):
        sl = slice(i * blk, (i + 1) * blk)
        att = dot(co_ref[sl, :], woo_ref[...]) + dot(cx_ref[sl, :], wox[...])
        v = x_ref[sl, :].astype(F32) + att + vec_ref[:, at.out_bias]
        mid[sl, :] = v
        n, _ = norm_rows(v)
        low = (n * vec_ref[:, at.gain2] + vec_ref[:, at.shift2]).astype(BF)
        n2[sl, :] = low
        n2t[:, sl] = low.T
        if i == 0:
            for load in loads:
                load.wait()
        if (i + 1) * blk == rows:
            stores.extend([pull(mid, mid_h, sem.at[5]), pull(n2, n2_h, sem.at[6]), pull(n2t, n2t_h, sem.at[7])])

    def flush(i, blk):
        sl = pl.ds(i * blk, blk)
        outb[sl, :] = out[sl, :].astype(BF)
        dnb[sl, :] = dn[sl, :].astype(BF)
        stores.append(pull(outb.at[sl, :], out_h.at[sl, :], sem.at[8 + i]))
        stores.append(pull(dnb.at[sl, :], dn_h.at[sl, :], sem.at[12 + i]))

    for q in range(2):
        db_ref[:, cols[q]] = ffn_quarter(
            n2, n2t, og, wu.at[q], wd.at[q], vec_ref[:, biases[q]], out, dn, act_s, dh_s, gd.at[q], gu.at[q], q == 0,
            enter if q == 0 else None, flush if q == 1 else None,
            lambda: stores.append(pull(gd.at[q], (send_h, keep_h)[q].at[0:part, :], sem.at[16 + q])),
        )
        stores.append(pull(gu.at[q], (send_h, keep_h)[q].at[part:, :], sem.at[20 + q]))
    for store in stores:
        store.wait()


def ffn_own(at, bits, x, ctx_own, ctx_other, wo_own, vec, wo_mine, wo_far, og, wu, wd, after=()):
    rows, d = x.shape
    ff = wu.shape[1]
    part = ff // 2
    half = ctx_own.shape[1]
    return call(
        lambda *refs: ffn_own_kernel(at, *refs),
        after,
        prefetch=1,
        in_specs=[
            whole((rows, d)), whole((rows, half)), whole((rows, half)), whole((half, d)), whole(vec.shape),
        ] + [ANY] * 5,
        out_specs=[ANY] * 7 + [whole_out((1, ff))],
        scratch=[
            pltpu.VMEM((half, d), BF),
            pltpu.VMEM((rows, d), BF), pltpu.VMEM((2, d, part), BF), pltpu.VMEM((2, part, d), BF),
            pltpu.VMEM((rows, d), F32), pltpu.VMEM((rows, d), BF), pltpu.VMEM((d, rows), BF),
            pltpu.VMEM((rows, d), F32), pltpu.VMEM((rows, d), F32), pltpu.VMEM((rows, d), BF), pltpu.VMEM((rows, d), BF),
            pltpu.VMEM((rows, part), BF), pltpu.VMEM((rows, part), BF),
            pltpu.VMEM((2, part, d), BF), pltpu.VMEM((2, d, part), BF),
            pltpu.SemaphoreType.DMA((22,)),
        ],
        out_shape=[
            struct((rows, d), F32), struct((rows, d), BF), struct((d, rows), BF), struct((rows, d), BF),
            struct((rows, d), BF), struct((part + d, d), BF), struct((part + d, d), BF),
            struct((1, ff), F32),
        ],
        estimate=EST["ffn_own"],
        name="ffn_own",
        mib=56,
    )(bits, x, ctx_own, ctx_other, wo_own, vec, wo_mine, wo_far, og, wu, wd)


BLOCK_BITS = 4


def sub_block(s, q, x, n):
    out = q + 2 * x
    for k in range(2, n):
        out = out + (((s >> (n - 1 - k)) & 1) << k)
    return out


def put_blocks(grads, stack, q, n, sem, at, only=(0, 1)):
    count = 1 << (n - 2)
    size = grads[0].shape[0] // count
    return [
        pull(
            grads[x].at[s * size : (s + 1) * size, :],
            stack.at[pl.ds(pl.multiple_of(sub_block(s, q, x, n) * size, size), size), :],
            sem.at[at + x * count + s],
        )
        for x in only
        for s in range(count)
    ]


def gather_weights(bits_ref, near, near_x, rest, w, sem, at):
    rows = near.shape[0]
    b = bits_ref[1]
    return [
        pull(near, w.at[block(b, rows), :], sem.at[at]),
        pull(near_x, w.at[block(1 - b, rows), :], sem.at[at + 1]),
        pull(rest, w.at[2 * rows :, :], sem.at[at + 2]),
    ]


def ffn_mine_kernel(
    n, bits_ref, n2_ref, b_ref, near_h, near_x_h, rest_h, og_h, n2t_h, out_h, dn_h, stack_h, db_ref,
    w_ref, og, n2t, out, dn, outb, dnb, act_s, dh_s, gd, gu, sem,
):
    d = og.shape[1]
    part = w_ref.shape[0] - d
    c = bits_ref[0]
    bias_at = b_ref.shape[1] - 2 * part
    at = 10 + (1 << (n - 1))
    loads = gather_weights(bits_ref, near_h, near_x_h, rest_h, w_ref, sem, at)
    loads += [pull(og_h, og, sem.at[0]), pull(n2t_h, n2t, sem.at[1])]
    for load in loads:
        load.wait()
    stores = []

    def flush(i, blk):
        sl = pl.ds(i * blk, blk)
        outb[sl, :] = out[sl, :].astype(BF)
        dnb[sl, :] = dn[sl, :].astype(BF)
        stores.append(pull(outb.at[sl, :], out_h.at[sl, :], sem.at[2 + i]))
        stores.append(pull(dnb.at[sl, :], dn_h.at[sl, :], sem.at[6 + i]))

    bias = b_ref[:, pl.ds(pl.multiple_of(bias_at + c * part, 128), part)]
    db_ref[...] = ffn_quarter(
        n2_ref, n2t, og, w_ref.at[0:d, :], w_ref.at[d:, :], bias, out, dn, act_s, dh_s, gd, gu, True, None, flush,
        lambda: stores.extend(put_blocks((gd, gu), stack_h, c, n, sem, 10, (0,))),
    )
    stores += put_blocks((gd, gu), stack_h, c, n, sem, 10, (1,))
    for store in stores:
        store.wait()


def ffn_mine(bits, n2, near, near_x, rest, bias, og, n2t, after=()):
    rows, d = og.shape
    part = 2 * near.shape[0] + rest.shape[0] - d
    n = min(bits.shape[0], BLOCK_BITS)
    return call(
        lambda *refs: ffn_mine_kernel(n, *refs),
        after,
        prefetch=1,
        in_specs=[whole((rows, d)), whole(bias.shape)] + [ANY] * 5,
        out_specs=[ANY] * 3 + [whole_out((1, part))],
        scratch=[
            pltpu.VMEM((d + part, d), BF),
            pltpu.VMEM((rows, d), BF), pltpu.VMEM((d, rows), BF), pltpu.VMEM((rows, d), F32), pltpu.VMEM((rows, d), F32),
            pltpu.VMEM((rows, d), BF), pltpu.VMEM((rows, d), BF),
            pltpu.VMEM((rows, part), BF), pltpu.VMEM((rows, part), BF), pltpu.VMEM((part, d), BF), pltpu.VMEM((d, part), BF),
            pltpu.SemaphoreType.DMA((13 + (1 << (n - 1)),)),
        ],
        out_shape=[
            struct((rows, d), BF), struct((rows, d), BF), struct((4 * part, d), BF), struct((1, part), F32),
        ],
        estimate=EST["ffn_mine"],
        name="ffn_mine",
        mib=56,
    )(bits, n2, bias, near, near_x, rest, og, n2t)


def ffn_far_kernel(
    at, n, bits_ref, len_ref, n2_ref, b_ref, vec_ref, near_h, near_x_h, rest_h, og_h, n2t_h, mid_h, out1_h, dn1_h, out2_h, dn2_h,
    co_h, cx_h, woo_h, wom_h, wof_h, stack_in,
    lay_h, gm_h, dco_h, dcx_h, stack_h, dwoo_h, dwox_h, sums_ref, db_ref,
    w_ref, og, n2t, mid, out1, dn1, out2, dn2, co, cx, woo, wox, out, dn, act_s, dh_s, gd, gu, lay, gmb, dco, dcx, dwoo, dwox, sem,
):
    rows, d = og.shape
    part = w_ref.shape[0] - d
    half = co.shape[1]
    c = bits_ref[0]
    length = len_ref[0]
    bias_at = b_ref.shape[1] - 2 * part
    first = gather_weights(bits_ref, near_h, near_x_h, rest_h, w_ref, sem, 18 + (1 << (n - 1)))
    loads = [
        pull(src, dst, sem.at[i])
        for i, (src, dst) in enumerate((
            (og_h, og), (n2t_h, n2t), (mid_h, mid), (dn1_h, dn1), (dn2_h, dn2), (out1_h, out1), (out2_h, out2),
            (woo_h, woo), (wom_h, wox.at[block(c, half // 2), :]), (wof_h, wox.at[block(1 - c, half // 2), :]),
            (co_h, co), (cx_h, cx),
        ))
    ]
    for load in first + loads[:1]:
        load.wait()
    sums_ref[...] = jnp.zeros_like(sums_ref)
    stores = []

    def finish(i, blk):
        if i == 0:
            for load in loads[1:]:
                load.wait()
        sl = slice(i * blk, (i + 1) * blk)
        v = mid[sl, :]
        out_sum = out1[sl, :].astype(F32) + out2[sl, :].astype(F32) + out[sl, :]
        lay[sl, :] = (v + out_sum + vec_ref[:, at.down_bias]).astype(BF)
        unit, r = norm_rows(v)
        gn = dn1[sl, :].astype(F32) + dn2[sl, :].astype(F32) + dn[sl, :]
        o = og[sl, :].astype(F32)
        g = o + norm_back(gn * vec_ref[:, at.gain2], unit, r)
        mid[sl, :] = g
        low = g.astype(BF)
        gmb[sl, :] = low
        for k, val in enumerate((g, gn * unit, gn, o)):
            sums_ref[k : k + 1, :] += jnp.sum(val, axis=0, keepdims=True)
        valid = lax.broadcasted_iota(jnp.int32, (blk, 1), 0) + i * blk < length
        dco[sl, :] = jnp.where(valid, dot(low, woo[...], 1, 1), 0.0).astype(BF)
        dcx[sl, :] = jnp.where(valid, dot(low, wox[...], 1, 1), 0.0).astype(BF)

    bias = b_ref[:, pl.ds(pl.multiple_of(bias_at + (1 - c) * part, 128), part)]
    db_ref[...] = ffn_quarter(
        n2_ref, n2t, og, w_ref.at[0:d, :], w_ref.at[d:, :], bias, out, dn, act_s, dh_s, gd, gu, True, None, finish,
        lambda: stores.extend(put_blocks((gd, gu), stack_h, 1 - c, n, sem, 18, (0,))),
    )
    stores += put_blocks((gd, gu), stack_h, 1 - c, n, sem, 18, (1,))
    stores += [
        pull(src, dst, sem.at[12 + k])
        for k, (src, dst) in enumerate(((lay, lay_h), (mid, gm_h), (dco, dco_h), (dcx, dcx_h)))
    ]
    dwoo[...] = dot(gmb[...], co[...], 0, 0).astype(BF)
    dwox[...] = dot(gmb[...], cx[...], 0, 0).astype(BF)
    stores += [pull(dwoo, dwoo_h, sem.at[16]), pull(dwox, dwox_h, sem.at[17])]
    for store in stores:
        store.wait()


def ffn_far(
    at, bits, length, n2, near, near_x, rest, bias, vec, og, n2t, mid, out1, dn1, out2, dn2, ctx_own, ctx_other, wo_own,
    wo_mine, wo_far, stack, after=(),
):
    rows, d = og.shape
    part = 2 * near.shape[0] + rest.shape[0] - d
    n = min(bits.shape[0], BLOCK_BITS)
    half = ctx_own.shape[1]
    bf = lambda *shape: pltpu.VMEM(shape, BF)
    f32 = lambda *shape: pltpu.VMEM(shape, F32)
    return call(
        lambda *refs: ffn_far_kernel(at, n, *refs),
        after,
        prefetch=2,
        in_specs=[whole((rows, d)), whole(bias.shape), whole(vec.shape)] + [ANY] * 16,
        out_specs=[ANY] * 7 + [whole_out((8, d)), whole_out((1, part))],
        scratch=[
            bf(d + part, d), bf(rows, d), bf(d, rows), f32(rows, d), bf(rows, d), bf(rows, d), bf(rows, d), bf(rows, d),
            bf(rows, half), bf(rows, half), bf(half, d), bf(half, d), f32(rows, d), f32(rows, d),
            bf(rows, part), bf(rows, part), bf(part, d), bf(d, part), bf(rows, d), bf(rows, d), bf(rows, half),
            bf(rows, half), bf(d, half), bf(d, half), pltpu.SemaphoreType.DMA((21 + (1 << (n - 1)),)),
        ],
        out_shape=[
            struct((rows, d), BF), struct((rows, d), F32), struct((rows, half), BF), struct((rows, half), BF),
            struct(stack.shape, BF), struct((d, half), BF), struct((d, half), BF), struct((8, d), F32), struct((1, part), F32),
        ],
        alias={20: 4},
        estimate=EST["ffn_far"],
        name="ffn_far",
        mib=56,
    )(
        bits, length, n2, bias, vec, near, near_x, rest, og, n2t, mid, out1, dn1, out2, dn2, ctx_own, ctx_other, wo_own,
        wo_mine, wo_far, stack,
    )


def by_pairs(wcat, matrices, rows, width):
    for p in range(width // 128):
        for i in range(3):
            to = slice((3 * p + i) * 128, (3 * p + i + 1) * 128)
            ref, base = matrices[i]
            wcat[rows, to] = ref[:, base + p * 128 : base + (p + 1) * 128]


def share_kernel(bits_ref, g_ref, wm, wf, out_ref, wcat):
    width = g_ref.shape[1] // 3
    c = bits_ref[0]
    half = wm.shape[0]

    @pl.when(pl.program_id(0) == 0)
    def _():
        for ref, part in ((wm, c), (wf, 1 - c)):
            by_pairs(wcat, [(ref, i * width) for i in range(3)], block(part, half), width)

    out_ref[...] = dot(g_ref[...], wcat[...], 1, 1).astype(BF)


def input_share(bits, g, w_mine, w_far, after=()):
    rows, cols = g.shape
    d = 2 * w_mine.shape[0]
    blk = 512
    row = lambda w: pl.BlockSpec((blk, w), lambda i, *_: (i, 0))
    return call(
        share_kernel, after, prefetch=1, grid=(rows // blk,),
        in_specs=[row(cols), whole(w_mine.shape), whole(w_far.shape)], out_specs=row(d),
        out_shape=struct((rows, d), BF), scratch=[pltpu.VMEM((d, cols), BF)],
        estimate=EST["share"], name="input_share", mib=56,
    )(bits, g, w_mine, w_far)


def input_grad_kernel(
    at, bits_ref, x_ref, gm_ref, vec_ref, g_ref, share_ref, wq, wk, wv, sums2, sums_o, sums_x, db_own, db_mine, db_far,
    out_ref, small_ref, wcat,
):
    width = wq.shape[1]
    d = x_ref.shape[1]

    @pl.when(pl.program_id(0) == 0)
    def _():
        by_pairs(wcat, [(ref, 0) for ref in (wq, wk, wv)], slice(None), width)
        small_ref[...] = jnp.zeros_like(small_ref)
        for k in range(4):
            small_ref[1 + k // 2 : 2 + k // 2, (k % 2) * d : (k % 2 + 1) * d] = sums2[k : k + 1, :]
        low_core = bits_ref[0] == 0
        db_other = jnp.concatenate(
            [jnp.where(low_core, db_mine[...], db_far[...]), jnp.where(low_core, db_far[...], db_mine[...])], 1
        )
        first = bits_ref[bits_ref.shape[0] - 1] == 0
        for row, own, other in ((3, sums_o[...], sums_x[...]), (4, db_own[...], db_other)):
            small_ref[row : row + 1, 0 : own.shape[1]] = jnp.where(first, own, other)
            small_ref[row + 2 : row + 3, 0 : own.shape[1]] = jnp.where(first, other, own)

    gn = dot(g_ref[...], wcat[...], 1, 1) + share_ref[...].astype(F32)
    n, r = norm_rows(x_ref[...].astype(F32))
    out_ref[...] = (gm_ref[...] + norm_back(gn * vec_ref[:, at.gain1], n, r)).astype(BF)
    small_ref[0:1, 0:d] += jnp.sum(gn * n, axis=0, keepdims=True)
    small_ref[0:1, d:] += jnp.sum(gn, axis=0, keepdims=True)


def input_grad(at, bits, x, gm, vec, g, share, wq, wk, wv, sums, after=()):
    rows, d = x.shape
    width = wq.shape[1]
    blk = 256
    row = lambda w: pl.BlockSpec((blk, w), lambda i, *_: (i, 0))
    return call(
        lambda *refs: input_grad_kernel(at, *refs),
        after,
        prefetch=1,
        grid=(rows // blk,),
        in_specs=[row(d), row(d), whole(vec.shape), row(3 * width), row(d)]
        + [whole((d, width))] * 3
        + [whole(v.shape) for v in sums],
        out_specs=[row(d), whole_out((8, 2 * d))],
        out_shape=[struct((rows, d), BF), struct((8, 2 * d), F32)],
        scratch=[pltpu.VMEM((d, 3 * width), BF)],
        estimate=EST["input_grad"],
        name="input_grad",
        mib=56,
    )(bits, x, gm, vec, g, share, wq, wk, wv, *sums)


def wide_qkv(bits, near, far, after=()):
    size, width = near[0].shape
    width //= 4

    def kernel(bits_ref, *refs):
        ins, outs, turn = refs[:4], refs[4:8], refs[8]
        base = (pl.program_id(0) != bits_ref[0]).astype(jnp.int32) * 2
        for half in range(2):
            want = base + (half != bits_ref[1]).astype(jnp.int32)
            rows = slice(half * size, (half + 1) * size)
            for k in range(4):

                @pl.when(want == k)
                def _():
                    ref = ins[k]
                    for i, out in enumerate(outs[:3]):
                        for p in range(width // 128):
                            src = slice((3 * p + i) * 128, (3 * p + i + 1) * 128)
                            out[rows, p * 128 : (p + 1) * 128] = ref[:, src].astype(F32)
                    turn[rows, :] = ref[:, 3 * width :].astype(F32)

        outs[3][...] = turn[...].T

    return call(
        kernel, after, prefetch=1, grid=(2,),
        in_specs=[whole((size, 4 * width))] * 4,
        out_specs=[pl.BlockSpec((2 * size, width), lambda i, *_: (i, 0))] * 3
        + [pl.BlockSpec((width, 2 * size), lambda i, *_: (0, i))],
        out_shape=[struct((4 * size, width), F32)] * 3 + [struct((width, 4 * size), F32)],
        scratch=[pltpu.VMEM((2 * size, width), F32)], estimate=EST["move"], name="wide_qkv", mib=56,
    )(bits, *near, *far)


def wide_ffn(bits, stack, after=()):
    rows, d = stack.shape
    n = min(bits.shape[0], BLOCK_BITS)
    part = rows // 4
    count = 1 << (n - 2)
    size = part // count

    def kernel(bits_ref, *refs):
        for x in range(2):
            for k in range(2):
                refs[4 + x][k * size : (k + 1) * size, :] = refs[2 * x + k][...].astype(F32)

    def place(x, k):
        return lambda q, t, *_: (sub_block(2 * t + k, q, x, n), 0)

    return call(
        kernel, after, prefetch=1, grid=(2, count // 2),
        in_specs=[pl.BlockSpec((size, d), place(x, k)) for x in range(2) for k in range(2)],
        out_specs=[
            pl.BlockSpec((2 * size, d), lambda q, t, *_: (q * (count // 2) + t, 0)),
            pl.BlockSpec((2 * size, d), lambda q, t, *_: (t, q)),
        ],
        out_shape=[struct((2 * part, d), F32), struct((part, 2 * d), F32)],
        estimate=EST["move"], name="wide_ffn", mib=56,
    )(bits, stack, stack, stack, stack)


def wide_both(bits, stack, pieces, after=()):
    rows, d = stack.shape
    n = min(bits.shape[0], BLOCK_BITS)
    part = rows // 2
    count = 1 << (n - 2)
    size = part // count // 2

    def kernel(bits_ref, *refs):
        blocks, ins, outs = refs[:4], refs[4:8], refs[8:]
        base = (pl.program_id(0) != bits_ref[0]).astype(jnp.int32) * 2
        t = pl.program_id(1)
        for x in range(2):
            for k in range(2):
                outs[x][2 * k * size : (2 * k + 1) * size, :] = blocks[2 * x + k][...].astype(F32)
            want = base + (x != bits_ref[1]).astype(jnp.int32)
            for p in range(4):

                @pl.when(want == p)
                def _():
                    for k in range(2):
                        src = pl.ds(pl.multiple_of((2 * t + k) * size, size), size)
                        outs[x][(2 * k + 1) * size : (2 * k + 2) * size, :] = ins[p][src, :].astype(F32)

    def place(x, k):
        return lambda q, t, *_: (sub_block(2 * t + k, q, x, n), 0)

    return call(
        kernel, after, prefetch=1, grid=(2, count // 2),
        in_specs=[pl.BlockSpec((size, d), place(x, k)) for x in range(2) for k in range(2)]
        + [whole(p.shape) for p in pieces],
        out_specs=[
            pl.BlockSpec((4 * size, d), lambda q, t, *_: (q * (count // 2) + t, 0)),
            pl.BlockSpec((4 * size, d), lambda q, t, *_: (t, q)),
        ],
        out_shape=[struct((2 * part, d), F32), struct((part, 2 * d), F32)],
        estimate=EST["move"], name="wide_both", mib=56,
    )(bits, stack, stack, stack, stack, *pieces)


class Links:
    def __init__(self, dp_size):
        self.size = dp_size
        self.bits = dp_size.bit_length() - 1
        index = lax.axis_index("dp")
        digits = [(index >> i) & 1 for i in range(self.bits)] + [lax.axis_index("tensor")]
        self.value = jnp.stack(digits).astype(jnp.int32)

    def swap(self, value, at):
        return lax.ppermute(value, "dp", [(i, i ^ (1 << at)) for i in range(self.size)])

    def across(self, value):
        return lax.ppermute(value, "tensor", [(0, 1), (1, 0)])

    def join(self, mine, other, at, after=()):
        half, width = mine.shape
        if half % 16:
            low = self.value[at] == 0
            return jnp.concatenate([jnp.where(low, mine, other), jnp.where(low, other, mine)], 0)

        def moves(bits, ins, outs):
            return [
                (ins[0], outs[0].at[block(bits[at], half), :]), (ins[1], outs[0].at[block(1 - bits[at], half), :])
            ]

        return arrange(self.value, [mine, other], [(2 * half, width)], moves, "join", after)[0]


def halve(bits, parts, bit, after=()):
    count = len(parts)
    parts = lax.optimization_barrier((*parts, *after))[:count]
    size = parts[0].shape[0] // 2

    def half(at):
        return sum(lax.dynamic_slice_in_dim(v, at * size, size, 0).astype(F32) for v in parts).astype(BF)

    return half(1 - bits[bit]), half(bits[bit])


class Halve:
    def __init__(self, links, keep, recv):
        self.links, self.keep, self.recv, self.at = links, keep, recv, 0
        low = min(links.bits, BLOCK_BITS)
        self.order = [*range(low), *reversed(range(low, links.bits))]
        self.done = False

    def advance(self, after):
        links = self.links
        self.at += 1
        self.done = self.at == links.bits
        if self.done:
            return
        bit = self.order[self.at]
        send, self.keep = halve(links.value, (self.keep, self.recv), bit, after)
        self.recv = links.swap(send, bit)


RIDE = 16


def ride_kernel(rows, cut, bits_ref, *refs):
    *ins, small_ref, send_ref, keep_ref, next_ref, acc = refs
    width = small_ref.shape[1]
    small = small_ref[...]
    total = None
    for ref in ins:
        value = ref[0:rows, :].astype(F32)
        total = value if total is None else total + value
        if ref.shape[0] > rows:
            riding = ref[rows : rows + RIDE, :].astype(F32)
            small = small + riding[0:8] + riding[8:16]
    next_ref[...] = small
    if send_ref is None:
        keep_ref[...] = total.astype(BF)
        return
    acc[...] = total
    if cut is None:
        size = rows
        send_ref[0:size, :] = total.astype(BF)
        keep_ref[...] = total.astype(BF)
    else:
        size = rows // 2
        bit = bits_ref[cut]
        low, high = acc[0:size, :], acc[size : 2 * size, :]
        send_ref[0:size, :] = jnp.where(bit == 0, high, low).astype(BF)
        keep_ref[...] = jnp.where(bit == 0, low, high).astype(BF)
    high = small.astype(BF)
    send_ref[size:, :] = jnp.concatenate([high, (small - high.astype(F32)).astype(BF)], 0)


def ride(bits, parts, small, cut, last, after=()):
    rows = parts[0].shape[0]
    width = small.shape[1]
    size = rows // 2 if cut is not None else rows
    shapes = [struct((size, width), BF), struct(small.shape, F32)]
    if not last:
        shapes.insert(0, struct((size + RIDE, width), BF))

    def kernel(bits_ref, *refs):
        refs = list(refs)
        if last:
            refs.insert(len(parts) + 1, None)
        ride_kernel(rows, cut, bits_ref, *refs)

    out = call(
        kernel, after, prefetch=1, in_specs=[whole(a.shape) for a in (*parts, small)],
        out_specs=[whole_out(t.shape) for t in shapes], out_shape=shapes,
        scratch=[pltpu.VMEM((rows, width), F32)], estimate=EST["move"], name="ride",
    )(bits, *parts, small)
    return (None, *out) if last else out


def layer(
    dp_size, inputs, lengths, norm1_gain, norm1_shift, query_weight, query_bias, key_weight, key_bias, value_weight,
    value_bias, out_weight, out_bias, norm2_gain, norm2_shift, up_weight, up_bias, down_weight, down_bias, out_grad,
):
    rows, d = inputs.shape
    width = query_weight.shape[1]
    ff = up_weight.shape[1]
    part = ff // 2
    links = Links(dp_size)
    bits = links.value
    tensor = lax.axis_index("tensor")
    length = jnp.where(tensor == 0, lengths[:1], lengths[1:])
    cos, sin = (jnp.asarray(t) for t in rotary_tables(rows))
    at = Row(d, width, ff)
    vec = [norm1_gain, norm1_shift, out_bias, norm2_gain, norm2_shift, down_bias, query_bias, key_bias, value_bias, up_bias]
    vec = jnp.concatenate([v.reshape(1, -1) for v in vec], 1)

    def qkv_moves(bits_ref, ins, outs):
        return [
            (w.at[block(bits_ref[0], d // 2), :], outs[0].at[:, i * width : (i + 1) * width]) for i, w in enumerate(ins)
        ]

    near_rows = 5 * d // 12
    half = width // 2
    def cut_moves(bits_ref, ins, outs):
        c, b = bits_ref[0], bits_ref[1]
        wu, wd, wo = ins
        near, rest, out_half = outs
        cols = block(c, part)
        return [
            (wo.at[block(c, half), :], out_half),
            (wu.at[block(b, near_rows), cols], near),
            (wu.at[2 * near_rows :, cols], rest.at[0 : d - 2 * near_rows, :]),
            (wd.at[block(c, part), :], rest.at[d - 2 * near_rows :, :]),
        ]

    qkv_mine, = arrange(bits, [query_weight, key_weight, value_weight], [(d // 2, 3 * width)], qkv_moves, "cut_qkv", mib=56)
    qkv_mine = links.across(qkv_mine)
    normed, normed_t, *own, ctx_own, aug_own, near, rest, out_half = heads_own(
        at, cut_moves, [(near_rows, d), (d + part - 2 * near_rows, d), (half, d)], bits, length, inputs, vec, query_weight,
        key_weight, value_weight, cos, sin, up_weight, down_weight, out_weight,
    )
    bias_x = links.across(vec)
    near, out_mine = links.across(near), links.across(out_half)
    qkv_mine, _ = lax.optimization_barrier((qkv_mine, ctx_own))
    qkv_far = links.swap(qkv_mine, 0)
    *other, ctx_x, aug_x = heads_other(at, bits, length, normed, qkv_mine, qkv_far, bias_x, cos, sin, after=(ctx_own,))
    near, out_mine, rest, ctx_x = lax.optimization_barrier((near, out_mine, rest, ctx_x))
    out_far = links.swap(out_mine, 0)
    rest = links.across(rest)
    near_x = links.swap(near, 1)
    near_far = links.swap(near, 0)
    mid, n2, n2t, out1, dn1, w_send, w_keep, dbu = ffn_own(
        at, bits, inputs, ctx_own, ctx_x, out_weight, vec, out_mine, out_far, out_grad, up_weight, down_weight
    )

    w_recv = links.swap(w_send, 0)
    near_x_far, rest_far = links.swap(near_x, 0), links.swap(rest, 0)
    out2, dn2, stack, dbu_mine = ffn_mine(bits, n2, near, near_x, rest, bias_x, out_grad, n2t, after=(mid,))
    own_sum = Halve(links, w_keep, w_recv)
    own_sum.advance((out2,))
    layer_out, gm, g_own, g_x, stack, dwo, dwo_x, sums2, dbu_far = ffn_far(
        at, bits, length, n2, near_far, near_x_far, rest_far, bias_x, vec, out_grad, n2t, mid, out1, dn1, out2, dn2,
        ctx_own, ctx_x, out_weight, out_mine, out_far, stack, after=(own_sum.keep,),
    )
    blocks = min(dp_size, 1 << BLOCK_BITS)

    def turned(rows_, first, second):
        return rows_.reshape(first, second, -1, d).swapaxes(0, 1).reshape(-1, d)

    if dp_size > blocks:
        stack = turned(stack, blocks, dp_size // blocks)
    stack = lax.psum_scatter(stack, "dp", scatter_dimension=0, tiled=True)
    n = d // 2
    gx, sums_x, qx_s, qx_k = attend_back(
        bits, length, *other, g_x, ctx_x, aug_x, cos, sin, normed_t, dwo_x
    )
    qx_r = links.swap(qx_s, 0)
    own_sum.advance((qx_k,))
    share = input_share(bits, gx, qkv_mine, qkv_far, after=(own_sum.keep,))
    qx_k, qx_r, _ = lax.optimization_barrier((qx_k, qx_r, share))
    qx = (qx_k.astype(F32) + qx_r.astype(F32)).astype(BF)
    qx_y = links.across(qx)
    go, sums_o, qo_s, qo_k = attend_back(
        bits, length, *own, g_own, ctx_own, aug_own, cos, sin, normed_t, dwo, after=(qx,), est=12
    )
    own_sum.advance((qo_k,))
    qo_r = links.swap(qo_s, 0)
    q, = fold(bits, [(qo_k, 0, 0, n), (qx_y, 0, 0, n)], n, [(0, n)], "fold_qkv_y", after=(own_sum.keep,), est=busy(8))
    q_s, q_k = halve(bits, (q, qo_r), 1)
    q_r = links.swap(q_s, 1)
    input_grad_out, small = input_grad(
        at, bits, inputs, gm, vec, go, share, query_weight, key_weight, value_weight,
        (sums2, sums_o, sums_x, dbu, dbu_mine, dbu_far), after=(q_k,),
    )
    last = links.bits - 1
    small, = fold(bits, [(small, 0, 0, 8), (links.swap(small, 1), 0, 0, 8)], 8, [(0, 8)], "fold_small")
    send, keep1, small = ride(bits, [q_k, q_r], small, 2 if last > 2 else None, False, (q_k, own_sum.recv))
    q_parts = [keep1, links.swap(send, 2)]
    stack, keep1 = lax.optimization_barrier((stack, keep1))
    stack_r = links.across(stack)
    while not own_sum.done:
        own_sum.advance((keep1,))
    size = stack.shape[0]
    parts = [(v, 0, 0, size) for v in (stack, stack_r, own_sum.keep, own_sum.recv)][1:]
    split = dp_size == blocks
    cuts = [(0, size // 2), (size // 2, size // 2)] if split else [(0, size)]
    stack, *piece = fold(bits, parts, size, cuts, "fold_stack", after=q_parts)
    gathered = lax.all_gather(stack, "dp", axis=0, tiled=True)
    if dp_size > blocks:
        gathered = turned(gathered, dp_size // blocks, blocks)
    piece_r = links.swap(piece[0], last) if split else None

    after = (stack,)
    parts = q_parts
    for bit in range(3, links.bits):
        send, keep, small = ride(bits, parts, small, bit if bit < last else None, False, after)
        after = ()
        parts = [keep, links.swap(send, bit)]
    if split:
        piece = piece[0]
        for bit in reversed(range(2, links.bits)):
            piece = links.join(piece, piece_r, bit, after=(keep,))
            piece_r = links.swap(piece, bit - 1)
        after = (piece,)
    _, q, small = ride(bits, parts, small, None, True, after)
    for bit in reversed(range(2, last)):
        q_r = links.swap(q, bit)
        if bit == last - 1:
            size = small.shape[0]
            for swap in (links.across, lambda v: links.swap(v, 0)):
                parts = [(small, 0, 0, size), (swap(small), 0, 0, size)]
                small, = fold(bits, parts, size, [(0, size)], "fold_small", after=(q,))
        q = links.join(q, q_r, bit, after=(small,))
    q_r = links.swap(q, 1)
    q_far = links.swap(q, 0)
    if split:
        piece_r, _ = lax.optimization_barrier((piece_r, q))
        pieces = [piece, piece_r, links.swap(piece, 0), links.swap(piece_r, 0)]
        grad_down, grad_up = wide_both(bits, gathered, pieces, after=(q,))
    else:
        grad_down, grad_up = wide_ffn(bits, gathered, after=(q,))
    q_r, grad_up = lax.optimization_barrier((q_r, grad_up))
    q_r_far = links.swap(q_r, 0)
    grad_q, grad_k, grad_v, grad_out = wide_qkv(bits, (q, q_r), (q_far, q_r_far), after=(grad_up,))

    gain1, shift1, out_b, gain2, shift2, down_b = (small[i // 2, (i % 2) * d : (i % 2 + 1) * d] for i in range(6))
    mine = lax.dynamic_slice_in_dim(small, 3 + 2 * tensor, 2, 0)
    qkv_bias = mine[0, : 3 * width].reshape(-1, 3, 128)
    return (
        layer_out, input_grad_out, gain1, shift1,
        grad_q, qkv_bias[:, 0].reshape(-1), grad_k, qkv_bias[:, 1].reshape(-1), grad_v, qkv_bias[:, 2].reshape(-1),
        grad_out, out_b, gain2, shift2, grad_up, mine[1, :ff], grad_down, down_b,
    )


def solution(mesh):
    rows = P(("dp", "tensor"), None)
    cols = P(None, "tensor")
    tens = P("tensor")
    return jax.shard_map(
        lambda *args: layer(mesh.shape["dp"], *args),
        mesh=mesh,
        in_specs=(
            rows, P("dp"), P(), P(), cols, tens, cols, tens, cols, tens, P("tensor", None), P(), P(), P(), cols, tens,
            P("tensor", None), P(), rows,
        ),
        out_specs=(
            rows, rows, P(), P(), cols, tens, cols, tens, cols, tens, P("tensor", None), P(), P(), P(), cols, tens,
            P("tensor", None), P(),
        ),
        check_vma=False,
    )
```
